32 devices in a mesh: dp: 16 (over z, y, core), rep: 2 (over x).
Axes of the slice: x: 2, y: 2, z: 4, core: 2. Of those that a mesh axis runs over, the one named last changes fastest.
Arguments:
- images: bfloat16 [512, 7, 7, 2048], P(('dp', 'rep')), may hold values from -6 to 6
- labels: int32 [512], P(('dp', 'rep')), may hold values from 0 to 999
- conv1: float32 [2048, 512], P('rep'), may hold values from -0.125 to 0.125
- conv2: float32 [4608, 512], P('rep'), may hold values from -0.09375 to 0.09375
- classifier: float32 [512, 1000], P('rep'), may hold values from -0.9 to 0.9
- class_bias: float32 [1000], replicated, may hold values from -3 to 3
- batchnorm_parameters: float32 [2, 2, 512], replicated, may hold values from 0.25 to 1.75
- conv1_mom: float32 [2048, 512], P('rep'), may hold values from -0.0024414062 to 0.0024414062
- conv2_mom: float32 [4608, 512], P('rep'), may hold values from -0.0024414062 to 0.0024414062
- class_m: float32 [512, 1000], P('rep'), may hold values from -0.00061035156 to 0.00061035156
- class_v: float32 [512, 1000], P('rep'), may hold values from 7.8125e-10 to 3.125e-09
- bias_m: float32 [1000], replicated, may hold values from -0.0008544922 to 0.0008544922
- bias_v: float32 [1000], replicated, may hold values from 1.7578125e-09 to 7.03125e-09
- norm_m: float32 [2, 2, 512], replicated, may hold values from -0.00030517578 to 0.00030517578
- norm_v: float32 [2, 2, 512], replicated, may hold values from 1.953125e-10 to 7.8125e-10
- conv1_live: int32 [2048, 512], P('rep'), may hold values 0 or 1
- conv2_live: int32 [4608, 512], P('rep'), may hold values 0 or 1
- conv1_next: int32 [2048, 512], P('rep'), may hold values 0 or 1
- conv2_next: int32 [4608, 512], P('rep'), may hold values 0 or 1
Outputs:
- loss_sum: float32 [], replicated
- conv1_new: float32 [2048, 512], P('rep')
- conv2_new: float32 [4608, 512], P('rep')
- classifier_new: float32 [512, 1000], P('rep')
- class_bias_new: float32 [1000], replicated
- norm_new: float32 [2, 2, 512], replicated
- conv1_mom_new: float32 [2048, 512], P('rep')
- conv2_mom_new: float32 [4608, 512], P('rep')
- class_m_new: float32 [512, 1000], P('rep')
- class_v_new: float32 [512, 1000], P('rep')
- bias_m_new: float32 [1000], replicated
- bias_v_new: float32 [1000], replicated
- norm_m_new: float32 [2, 2, 512], replicated
- norm_v_first: float32 [2, 512], replicated
- norm_v_second: float32 [2, 512], replicated
The draws below stay inside these ranges and needn't reach their ends.
All inputs are finite; a program needn't handle non-finite values. No bound on the sum of `conv1_live` or of `conv2_live` or of `conv1_next` or of `conv2_next` on one device may be relied on, other than what follows from the above.
Results may differ from the reference program's by a relative error of at most 0.0055.
The reference program's roundings to bfloat16 on the way count: a program that leaves them out, or rounds other values in their place, can miss the bound.
Values may be sent and summed in bfloat16 or wider, within the bound.
A program may use at most 256 MiB of HBM per device.

```python
import math
import jax
import jax.numpy as jnp
from jax import lax

C_IN = 2048
C_MID = 512
CLASSES = 1000
SIDE = 7
TURNS = 5
STEP = 5
IMG_DEV = 16
IMAGES = 512
DEVICES = 32


def touch_ends(values, rng, low, largest):
    index_at = [jax.random.randint(jax.random.fold_in(rng, axis), (), 0, length) for axis, length in enumerate(values.shape)]
    main_axis = values.shape.index(max(values.shape))
    neighbour = index_at[:main_axis] + [(index_at[main_axis] + 1) % values.shape[main_axis]] + index_at[main_axis + 1:]
    return values.at[tuple(index_at)].set(low).at[tuple(neighbour)].set(largest)


def levels(stream_key, shape, shards, least, top_value):
    def one(axis_at, parts):
        draws = jax.random.uniform(jax.random.fold_in(jax.random.fold_in(stream_key, 6), axis_at), (parts,), jnp.float32, least / len(shards), top_value / len(shards))
        return jnp.repeat(jnp.exp(draws), shape[axis_at] // parts).reshape((-1,) + (1,) * (len(shape) - axis_at - 1))

    level = one(*shards[0])
    for cut in shards[1:]:
        level = level * one(*cut)
    return level


def scatter_about(stream_key, extent, scale, reach, cuts=(), dtype=jnp.bfloat16):
    entries = jax.random.normal(stream_key, extent, jnp.float32) * scale
    if len(cuts) > 0:
        entries = levels(stream_key, extent, cuts, -0.22, 0.18) * entries
    return jnp.clip(entries, min=-reach, max=reach).astype(dtype)


def setup_inputs(seed: int = 0) -> dict:
    arg_keys = jax.random.split(jax.random.key(seed), 20)
    return {
        "images": scatter_about(arg_keys[0], (IMAGES, SIDE, SIDE, C_IN), 1.0, 6.0, ((0, 32),)),
        "labels": touch_ends(jax.random.randint(arg_keys[1], (IMAGES,), 0, CLASSES), jax.random.fold_in(arg_keys[1], 1), 0, CLASSES - 1).astype(jnp.int32),
        "conv1": scatter_about(arg_keys[2], (C_IN, C_MID), C_IN ** -0.5, 0.125, ((0, 2),), jnp.float32),
        "conv2": scatter_about(arg_keys[3], (9 * C_MID, C_MID), (9 * C_MID) ** -0.5, 0.09375, ((0, 2),), jnp.float32),
        "classifier": scatter_about(arg_keys[4], (C_MID, CLASSES), 0.15, 0.9, ((0, 2),), jnp.float32),
        "class_bias": scatter_about(arg_keys[5], (CLASSES,), 0.5, 3.0, (), jnp.float32),
        "batchnorm_parameters": jnp.clip(1.0 + 0.15 * jax.random.normal(arg_keys[6], (2, 2, C_MID), jnp.float32), 0.25, 1.75),
        "conv1_mom": scatter_about(arg_keys[7], (C_IN, C_MID), (0.01 / (IMG_DEV * DEVICES) ** 0.5), 0.0024414062, ((0, 2),), jnp.float32),
        "conv2_mom": scatter_about(arg_keys[8], (9 * C_MID, C_MID), (0.01 / (IMG_DEV * DEVICES) ** 0.5), 0.0024414062, ((0, 2),), jnp.float32),
        "class_m": scatter_about(arg_keys[9], (C_MID, CLASSES), (0.0022 / (IMG_DEV * DEVICES) ** 0.5), 0.00061035156, ((0, 2),), jnp.float32),
        "class_v": jnp.clip(jnp.exp(math.log(3.1250000365190544e-09) - 1.3862944 * jax.random.uniform(arg_keys[10], (C_MID, CLASSES), jnp.float32) ** levels(arg_keys[10], (C_MID, CLASSES), ((0, 2),), -0.2, 0.2)), 7.812500091297636e-10, 3.1250000365190544e-09),
        "bias_m": scatter_about(arg_keys[11], (CLASSES,), (0.0033 / (IMG_DEV * DEVICES) ** 0.5), 0.0008544922, (), jnp.float32),
        "bias_v": jnp.clip(jnp.exp(jax.random.uniform(arg_keys[12], (CLASSES,), jnp.float32, math.log(1.757812451153029e-09), math.log(7.031249804612116e-09))), 1.757812451153029e-09, 7.031249804612116e-09),
        "norm_m": scatter_about(arg_keys[13], (2, 2, C_MID), (0.0011 / (IMG_DEV * DEVICES) ** 0.5), 0.00030517578, (), jnp.float32),
        "norm_v": jnp.clip(jnp.exp(jax.random.uniform(arg_keys[14], (2, 2, C_MID), jnp.float32, math.log(1.953125022824409e-10), math.log(7.812500091297636e-10))), 1.953125022824409e-10, 7.812500091297636e-10),
        "conv1_live": touch_ends((jax.random.randint(arg_keys[15], (C_IN, C_MID), 0, 4) < 3).astype(jnp.int32), jax.random.fold_in(arg_keys[15], 1), 0, 1),
        "conv2_live": touch_ends((jax.random.randint(arg_keys[16], (9 * C_MID, C_MID), 0, 4) < 3).astype(jnp.int32), jax.random.fold_in(arg_keys[16], 1), 0, 1),
        "conv1_next": touch_ends((jax.random.randint(arg_keys[17], (C_IN, C_MID), 0, 4) < 3).astype(jnp.int32), jax.random.fold_in(arg_keys[17], 1), 0, 1),
        "conv2_next": touch_ends((jax.random.randint(arg_keys[18], (9 * C_MID, C_MID), 0, 4) < 3).astype(jnp.int32), jax.random.fold_in(arg_keys[18], 1), 0, 1),
    }


@jax.custom_vjp
def low(v):
    return lax.optimization_barrier(v.astype(jnp.bfloat16)).astype(jnp.float32)

@jax.custom_vjp
def low_back(v):
    return v

def low_keep(v):
    return (low(v), None)

def low_pass(kept, grad):
    return (grad,)

def back_keep(v):
    return (v, None)

def back_low(kept, grad):
    return (low(grad),)
low.defvjp(low_keep, low_pass)
low_back.defvjp(back_keep, back_low)
HIGH = lax.Precision.HIGHEST
NORM_EPS = 1e-05
COEF_A = 3.4445
COEF_B = -4.775
COEF_C = 2.0315

def patches_of(act):
    count = act.shape[0]
    chans = act.shape[3]
    padded = jnp.pad(act, ((0, 0), (1, 1), (1, 1), (0, 0)))
    pieces = [padded[:, dy:dy + SIDE, dx:dx + SIDE, :] for dy in range(3) for dx in range(3)]
    return jnp.concatenate(pieces, axis=3).reshape(count * SIDE * SIDE, 9 * chans)

def batch_norm(hidden, norm_gain, norm_shift):
    element_count = hidden.shape[0]
    channel_mean = lax.optimization_barrier(jnp.sum(hidden, axis=0)) / element_count
    var = lax.optimization_barrier(jnp.sum(hidden * hidden, axis=0)) / element_count - channel_mean * channel_mean
    return norm_gain * (hidden - channel_mean) * lax.rsqrt(var + NORM_EPS) + norm_shift

def forward(w1e, w2e, wc, bias, norm, images, labels):
    w1b = low(w1e)
    w2b = low(w2e)
    wcb = low(wc)
    block = math.gcd(IMAGES, 64)
    blocks = IMAGES // block
    xblocks = images.reshape(blocks, block, SIDE, SIDE, C_IN)

    def first_block(xpart):
        return jnp.dot(xpart.reshape(-1, C_IN).astype(jnp.float32), w1b, precision=HIGH)
    hidden_first = lax.map(jax.checkpoint(first_block), xblocks).reshape(-1, C_MID)
    hidden_first = low_back(hidden_first)
    a1 = low(jax.nn.silu(batch_norm(hidden_first, norm[0, 0], norm[0, 1])))
    ablocks = a1.reshape(blocks, block, SIDE, SIDE, C_MID)

    def second_block(apart):
        return jnp.dot(patches_of(apart), w2b, precision=HIGH)
    hidden_second = lax.map(jax.checkpoint(second_block), ablocks).reshape(-1, C_MID)
    hidden_second = low_back(hidden_second)
    a2 = jax.nn.silu(batch_norm(hidden_second, norm[1, 0], norm[1, 1]))
    pooled = low(lax.optimization_barrier(jnp.mean(a2.reshape(IMAGES, SIDE * SIDE, C_MID), axis=1)))
    logits = low_back(jnp.dot(pooled, wcb, precision=HIGH)) + bias
    lse = jax.nn.logsumexp(logits, axis=1)
    target = jnp.take_along_axis(logits, labels[:, None], axis=1)[:, 0]
    loss_sum = jnp.sum(lse - target)
    return (loss_sum / IMAGES, loss_sum)

def gram_of(x):
    return lax.dot_general(x, x, (((0,), (0,)), ((), ())), precision=HIGH)

def orthogonal(x):
    for turn in range(TURNS):
        gram = gram_of(x)
        if turn == 0:
            scale = jnp.sqrt(jnp.trace(gram)) + 1e-07
            x = x / scale
            gram = gram / (scale * scale)
        inner = COEF_B * gram + COEF_C * jnp.dot(gram, gram, precision=HIGH)
        x = COEF_A * x + jnp.dot(x, inner, precision=HIGH)
    return x

def adam_update(weight, first, second, grad, rate):
    first = 0.9 * first + 0.1 * grad
    second = 0.999 * second + 0.001 * grad * grad
    mhat = first / (1.0 - 0.9 ** STEP)
    vhat = second / (1.0 - 0.999 ** STEP)
    return (weight - rate * (mhat / (jnp.sqrt(vhat) + 1e-08) + 0.01 * weight), first, second)

def reference(images, labels, conv1, conv2, classifier, class_bias, batchnorm_parameters, conv1_mom, conv2_mom, class_m, class_v, bias_m, bias_v, norm_m, norm_v, conv1_live, conv2_live, conv1_next, conv2_next):
    w1e = conv1 * conv1_live.astype(jnp.float32)
    w2e = conv2 * conv2_live.astype(jnp.float32)

    def loss_of(a, b, c, d, e):
        return forward(a, b, c, d, e, images, labels)
    loss, pull, loss_sum = jax.vjp(loss_of, w1e, w2e, classifier, class_bias, batchnorm_parameters, has_aux=True)
    g1, g2, gc, gb, gn = pull(jnp.ones((), jnp.float32))
    mom1 = 0.5 * conv1_mom + g1
    mom2 = 0.5 * conv2_mom + g2
    new1 = (conv1 - 1.0 * orthogonal(mom1)) * conv1_next.astype(jnp.float32)
    new2 = (conv2 - 1.0 * orthogonal(mom2)) * conv2_next.astype(jnp.float32)
    wc_new, cm, cv = adam_update(classifier, class_m, class_v, gc, 0.03)
    b_new, bm, bv = adam_update(class_bias, bias_m, bias_v, gb, 0.2)
    n_new, nm, nv = adam_update(batchnorm_parameters, norm_m, norm_v, gn, 0.2)
    return (loss_sum, new1, new2, wc_new, b_new, n_new, mom1, mom2, cm, cv, bm, bv, nm, nv[0], nv[1])
```

```python
import functools

import jax
import jax.numpy as jnp
from jax import lax
from jax.experimental import pallas as pl
from jax.experimental.pallas import tpu as pltpu
from jax.sharding import PartitionSpec as P

SIDE = 7
TURNS = 5
STEP = 5
NORM_EPS = 1e-05
COEF_A = 3.4445
COEF_B = -4.775
COEF_C = 2.0315
MESH = pl.DeviceIdType.MESH
BF = jnp.bfloat16
F32 = jnp.float32
DMA = pltpu.SemaphoreType.DMA


def nn(a, b):
    return jnp.dot(a, b, preferred_element_type=F32)


def nt(a, b):
    return lax.dot_general(a, b, (((1,), (1,)), ((), ())), preferred_element_type=F32)


def tn(a, b):
    return lax.dot_general(a, b, (((0,), (0,)), ((), ())), preferred_element_type=F32)


def sigmoid(v):
    return 1.0 / (1.0 + jnp.exp(-v))


class Place:
    def __init__(self, n_dp, n_rep):
        self.n_dp, self.n_rep = n_dp, n_rep
        self.chips = n_dp // 2 * n_rep
        self.dp, self.rep = lax.axis_index("dp"), lax.axis_index("rep")
        self.core = lax.rem(self.dp, 2)
        self.chip = self.dp // 2 * n_rep + self.rep

    def flip(self, bit):
        half = 1 << bit
        set_now = lax.rem(self.dp // half, 2)
        return {"dp": self.dp + half - 2 * half * set_now, "rep": self.rep}

    def other_chip(self, step):
        to = lax.rem(self.chip + step, self.chips)
        return {"dp": to // self.n_rep * 2 + self.core, "rep": lax.rem(to, self.n_rep)}

    def other_rep(self, step):
        return {"dp": self.dp, "rep": lax.rem(self.rep + step, self.n_rep)}


def send(src, dst, send_sem, recv_sem, to):
    copy = pltpu.make_async_remote_copy(src, dst, send_sem, recv_sem, to, MESH)
    copy.start()


def wait_bytes(ref, sem):
    pltpu.make_async_copy(ref, ref, sem).wait()


def enter(place):
    barrier = pltpu.get_barrier_semaphore()

    def greet(step, carry):
        pl.semaphore_signal(barrier, 1, device_id=place.other_chip(step), device_id_type=MESH)
        return carry

    lax.fori_loop(1, place.chips, greet, 0)
    pl.semaphore_signal(barrier, 1, device_id=place.flip(0), device_id_type=MESH)
    pl.semaphore_wait(barrier, place.chips)


def sum_over_all(place, value, pair_buf, chip_buf, sems, meanwhile=None):
    pair_buf[place.core] = value
    mine = pair_buf.at[place.core]
    send(mine, mine, sems.at[0], sems.at[1], place.flip(0))
    wait_bytes(mine, sems.at[1])
    chip_buf[place.chip] = pair_buf[0] + pair_buf[1]
    block = chip_buf.at[place.chip]

    def one(step, carry):
        send(block, block, sems.at[2], sems.at[3], place.other_chip(step))
        return carry

    lax.fori_loop(1, place.chips, one, 0)
    if meanwhile is not None:
        meanwhile()
    wait_bytes(chip_buf.at[pl.ds(0, place.chips - 1)], sems.at[3])
    total = jnp.sum(chip_buf[...], axis=0)
    wait_bytes(mine, sems.at[0])
    wait_bytes(chip_buf.at[pl.ds(0, place.chips - 1)], sems.at[2])
    return total


class Gather:
    def __init__(self, place, buf, pieces, sems):
        self.place, self.buf, self.pieces, self.sems = place, buf, pieces, sems
        self.quarter = buf.shape[1] // 4
        self.rows = self.quarter // pieces
        self.y = lax.rem(place.dp // 2, 2)

    def at(self, block, y, piece):
        first = self.place.core * (2 * self.quarter) + y * self.quarter + piece * self.rows
        return self.buf.at[block, pl.ds(pl.multiple_of(first, 16), self.rows)]

    def blocks(self):
        return [lax.rem(self.place.rep + step, self.place.n_rep) for step in range(1, self.place.n_rep)]

    def size(self):
        return self.buf.at[pl.ds(0, self.place.n_rep - 1), pl.ds(0, self.rows)]

    def start(self, piece):
        mine = self.at(self.place.rep, self.y, piece)
        for step in range(1, self.place.n_rep):
            send(mine, mine, self.sems.at[0, piece, 0], self.sems.at[0, piece, 1], self.place.other_rep(step))

    def hop_y(self, piece):
        wait_bytes(self.size(), self.sems.at[0, piece, 1])
        for block in self.blocks():
            here = self.at(block, self.y, piece)
            send(here, here, self.sems.at[1, piece, 0], self.sems.at[1, piece, 1], self.place.flip(1))
            send(here, here, self.sems.at[2, piece, 0], self.sems.at[2, piece, 1], self.place.flip(0))

    def hop_core(self, piece):
        wait_bytes(self.size(), self.sems.at[1, piece, 1])
        for block in self.blocks():
            here = self.at(block, 1 - self.y, piece)
            send(here, here, self.sems.at[3, piece, 0], self.sems.at[3, piece, 1], self.place.flip(0))

    def finish(self, piece):
        wait_bytes(self.size(), self.sems.at[2, piece, 1])
        wait_bytes(self.size(), self.sems.at[3, piece, 1])

    def drain(self):
        for piece in range(self.pieces):
            for hop in range(4):
                wait_bytes(self.size(), self.sems.at[hop, piece, 0])


def norm_of(total, count):
    mean = total[0:1] / count
    return mean, lax.rsqrt(total[1:2] / count - mean * mean + NORM_EPS)


def over_pixels(step, init, images):
    def body(pixel, carry):
        return step(pixel, pl.multiple_of(pixel * images, 16), carry)

    return lax.fori_loop(0, SIDE * SIDE, body, init, unroll=7)


def fold(acc):
    return jnp.sum(acc, axis=0, keepdims=True)


def sums_of(h_ref, images):
    chans = h_ref.shape[1]

    def step(pixel, row, carry):
        v = h_ref[pl.ds(row, images), :]
        return carry[0] + v, carry[1] + v * v

    zero = jnp.zeros((images, chans), F32)
    one, two = over_pixels(step, (zero, zero), images)
    return jnp.concatenate([fold(one), fold(two)], axis=0)


def put_padded(pad_ref, pixel, value, images):
    y, x = pixel // SIDE, lax.rem(pixel, SIDE)
    pad_ref[1 + y, pl.ds(pl.multiple_of((1 + x) * images, 16), images), :] = value


def clear_border(pad_ref, images):
    line = SIDE * images
    pad_ref[0] = jnp.zeros(pad_ref.shape[1:], pad_ref.dtype)
    pad_ref[SIDE + 1] = jnp.zeros(pad_ref.shape[1:], pad_ref.dtype)
    edge = jnp.zeros((SIDE, images, pad_ref.shape[2]), pad_ref.dtype)
    pad_ref[1 : SIDE + 1, 0:images, :] = edge
    pad_ref[1 : SIDE + 1, images + line : 2 * images + line, :] = edge


def build_patches(pad_ref, to_ref):
    rows, chans = to_ref.shape[0], pad_ref.shape[2]
    line = rows // SIDE
    images = line // SIDE
    for k in range(9):
        dy, dx = divmod(k, 3)
        piece = pad_ref[dy : dy + SIDE, dx * images : dx * images + line, :]
        to_ref[:, k * chans : (k + 1) * chans] = piece.reshape(rows, chans)


def kernel_a(n_dp, n_rep, *refs):
    (x_hbm, w1_hbm, w2_hbm, head_hbm, live1_hbm, live2_hbm, bias_ref, norm_ref, label_ref,
     h1_ref, h2_ref, pad_ref, w2b, stat_ref, dz_ref, pooled_ref, loss_ref, gbias_ref, dpool_ref,
     x_ref, f1, i1, f2, i2, fh, w1b, head_b, patches, bias_pad, pair_buf, chip_buf,
     load_sem, w1_sem, w2_sem, head_sem, sum_sem) = refs
    place = Place(n_dp, n_rep)
    core, rep = place.core, place.rep
    half1, half2, mid = w1b.shape[1], w2b.shape[1], w1b.shape[2]
    classes, head_cols = fh.shape
    wide = head_b.shape[1]
    rows = x_ref.shape[0]
    images = rows // (SIDE * SIDE)
    all_images = images * n_dp * n_rep
    count = all_images * SIDE * SIDE

    pairs = [(w1_hbm, f1), (live1_hbm, i1), (w2_hbm, f2), (live2_hbm, i2), (x_hbm, x_ref), (head_hbm, fh)]
    loads = [pltpu.make_async_copy(a, b, load_sem.at[k]) for k, (a, b) in enumerate(pairs)]
    for load in loads:
        load.start()
    g1, g2, gh = Gather(place, w1b, 2, w1_sem), Gather(place, w2b, 3, w2_sem), Gather(place, head_b, 1, head_sem)

    def mask(value, live, to, first, size):
        at = pl.ds(pl.multiple_of(first, 16), size)
        to[rep, at, :] = (value[at, :] * live[at, :].astype(F32)).astype(BF)

    def spread(gather, value, live, to):
        quarter = gather.quarter
        mine = core * 2 + gather.y
        for piece in range(gather.pieces):
            mask(value, live, to, mine * quarter + piece * gather.rows, gather.rows)
            gather.start(piece)
        for other in range(1, 4):
            mask(value, live, to, lax.rem(mine + other, 4) * quarter, quarter)

    loads[0].wait()
    loads[1].wait()
    enter(place)
    spread(g1, f1, i1, w1b)
    loads[2].wait()
    loads[3].wait()
    spread(g2, f2, i2, w2b)
    loads[5].wait()
    head_b[rep, 0:classes, :] = fh[...].astype(BF)
    head_b[rep, classes:, :] = jnp.zeros((wide - classes, head_cols), BF)
    gh.start(0)
    clear_border(pad_ref, images)
    bias_pad[:, 0:classes] = bias_ref[...]
    bias_pad[:, classes:] = jnp.zeros((1, wide - classes), F32)
    loads[4].wait()

    def cols(block, half):
        return pl.ds(pl.multiple_of(block * half, 128), half)

    h1_ref[...] = nn(x_ref[:, cols(rep, half1)], w1b[rep])
    for piece in range(2):
        g1.hop_y(piece)
    for piece in range(2):
        g1.hop_core(piece)
    g2.hop_y(0)
    for piece in range(2):
        g1.finish(piece)
    for block in g1.blocks():
        h1_ref[...] += nn(x_ref[:, cols(block, half1)], w1b[block])

    total = sum_over_all(place, sums_of(h1_ref, images), pair_buf.at[0], chip_buf.at[0], sum_sem.at[0], lambda: g2.hop_y(1))
    mean1, inv1 = norm_of(total, count)
    scale1 = norm_ref[0:1] * inv1
    move1 = norm_ref[1:2] - mean1 * scale1
    g2.hop_core(0)
    g2.hop_core(1)

    def act1(pixel, row, carry):
        v = h1_ref[pl.ds(row, images), :] * scale1 + move1
        put_padded(pad_ref, pixel, (v * sigmoid(v)).astype(BF), images)
        return carry

    over_pixels(act1, 0, images)
    g2.hop_y(2)
    build_patches(pad_ref, patches)
    if half2 % 128:
        g2.hop_core(2)
        gh.hop_y(0)
        gh.hop_core(0)
        for piece in range(3):
            g2.finish(piece)
        for block in range(n_rep):
            part = nn(patches[:, block * half2 : (block + 1) * half2], w2b[block])
            h2_ref[...] = part if block == 0 else h2_ref[...] + part
    else:
        h2_ref[...] = nn(patches[:, cols(rep, half2)], w2b[rep])
        g2.hop_core(2)
        gh.hop_y(0)
        gh.hop_core(0)
        for piece in range(3):
            g2.finish(piece)
        for block in g2.blocks():
            h2_ref[...] += nn(patches[:, cols(block, half2)], w2b[block])

    total = sum_over_all(place, sums_of(h2_ref, images), pair_buf.at[1], chip_buf.at[1], sum_sem.at[1])
    mean2, inv2 = norm_of(total, count)
    scale2 = norm_ref[2:3] * inv2
    move2 = norm_ref[3:4] - mean2 * scale2

    def pool(pixel, row, carry):
        v = h2_ref[pl.ds(row, images), :] * scale2 + move2
        return carry + v * sigmoid(v)

    pooled = (over_pixels(pool, jnp.zeros((images, mid), F32), images) / (SIDE * SIDE)).astype(BF)
    pooled_ref[...] = pooled
    gh.finish(0)
    logits = bias_pad[...]
    for block in range(n_rep):
        logits = logits + nt(pooled_ref[:, block * head_cols : (block + 1) * head_cols], head_b[block])
    column = lax.broadcasted_iota(jnp.int32, (images, wide), 1)
    shown = jnp.where(column < classes, logits, -jnp.inf)
    top = jnp.max(shown, axis=1, keepdims=True)
    lse = top + jnp.log(jnp.sum(jnp.exp(shown - top), axis=1, keepdims=True))
    hit = (column == label_ref[...]).astype(F32)
    target = jnp.sum(logits * hit, axis=1, keepdims=True)
    loss_ref[...] = jnp.sum(lse - target, axis=0, keepdims=True)
    grad = (jnp.exp(shown - lse) - hit) / all_images
    gbias_ref[...] = jnp.sum(grad, axis=0, keepdims=True)
    dz = grad.astype(BF)
    dz_ref[...] = dz
    for block in range(n_rep):
        dpool_ref[:, block * head_cols : (block + 1) * head_cols] = nn(dz, head_b[block]) / (SIDE * SIDE)
    dpool = dpool_ref[...]

    def back2(pixel, row, carry):
        h = h2_ref[pl.ds(row, images), :]
        v = h * scale2 + move2
        sig = sigmoid(v)
        dy = dpool * sig * (1.0 + v * (1.0 - sig))
        return carry[0] + dy, carry[1] + dy * ((h - mean2) * inv2)

    zero = jnp.zeros((images, mid), F32)
    one, two = over_pixels(back2, (zero, zero), images)
    sums = jnp.concatenate([fold(one), fold(two)], axis=0)
    total = sum_over_all(place, sums, pair_buf.at[2], chip_buf.at[2], sum_sem.at[2])
    stat_ref[...] = jnp.concatenate([mean1, inv1, mean2, inv2, total, total], axis=0)
    for gather in (g1, g2, gh):
        gather.drain()


def run_a(n_dp, n_rep, x, conv1, conv2, head, live1, live2, bias, norm, labels):
    rows, mid = x.shape[0], conv1.shape[1]
    images = rows // (SIDE * SIDE)
    half1, half2 = conv1.shape[0], conv2.shape[0]
    classes, head_cols = head.shape
    wide = (classes + 127) // 128 * 128
    chips = n_dp // 2 * n_rep
    shape = jax.ShapeDtypeStruct
    vmem, hbm = pl.BlockSpec(memory_space=pltpu.VMEM), pl.BlockSpec(memory_space=pl.ANY)
    return pl.pallas_call(
        functools.partial(kernel_a, n_dp, n_rep),
        out_shape=(
            shape((rows, mid), F32), shape((rows, mid), F32),
            shape((SIDE + 2, (SIDE + 2) * images, mid), BF), shape((n_rep, half2, mid), BF),
            shape((8, mid), F32), shape((images, wide), BF), shape((images, mid), BF),
            shape((1, 1), F32), shape((1, wide), F32), shape((images, mid), F32),
        ),
        in_specs=[hbm] * 6 + [vmem] * 3,
        out_specs=[vmem] * 10,
        scratch_shapes=[
            pltpu.VMEM(x.shape, BF),
            pltpu.VMEM((half1, mid), F32), pltpu.VMEM((half1, mid), jnp.int32),
            pltpu.VMEM((half2, mid), F32), pltpu.VMEM((half2, mid), jnp.int32),
            pltpu.VMEM((classes, head_cols), F32),
            pltpu.VMEM((n_rep, half1, mid), BF), pltpu.VMEM((n_rep, wide, head_cols), BF),
            pltpu.VMEM((rows, 9 * mid), BF), pltpu.VMEM((1, wide), F32),
            pltpu.VMEM((3, 2, 2, mid), F32), pltpu.VMEM((3, chips, 2, mid), F32),
            DMA((6,)), DMA((4, 2, 2)), DMA((4, 3, 2)), DMA((4, 1, 2)), DMA((3, 4)),
        ],
        compiler_params=pltpu.CompilerParams(
            collective_id=1, has_side_effects=True, vmem_limit_bytes=60 * 2**20
        ),
        name="forward",
    )(x, conv1, conv2, head, live1, live2, bias, norm, labels)


HIGH = lax.Precision.HIGHEST
NORM_EPS = 1e-05
COEF_A = 3.4445
COEF_B = -4.775
COEF_C = 2.0315


def patches_of(act):
    count = act.shape[0]
    chans = act.shape[3]
    padded = jnp.pad(act, ((0, 0), (1, 1), (1, 1), (0, 0)))
    pieces = [padded[:, dy : dy + SIDE, dx : dx + SIDE, :] for dy in range(3) for dx in range(3)]
    return jnp.concatenate(pieces, axis=3).reshape(count * SIDE * SIDE, 9 * chans)


def fold_patches(grad_rows, count, chans):
    pieces = grad_rows.reshape(count, SIDE, SIDE, 9, chans)
    padded = jnp.zeros((count, SIDE + 2, SIDE + 2, chans), jnp.float32)
    for dy in range(3):
        for dx in range(3):
            padded = padded.at[:, dy : dy + SIDE, dx : dx + SIDE, :].add(
                pieces[:, :, :, 3 * dy + dx, :]
            )
    return padded[:, 1 : SIDE + 1, 1 : SIDE + 1, :].reshape(count * SIDE * SIDE, chans)


def fold_rows(grad_rows, count, chans):
    pieces = grad_rows.reshape(SIDE, SIDE, count, 9, chans)
    padded = jnp.zeros((SIDE + 2, SIDE + 2, count, chans), jnp.float32)
    for dy in range(3):
        for dx in range(3):
            padded = padded.at[dy : dy + SIDE, dx : dx + SIDE].add(pieces[:, :, :, 3 * dy + dx])
    return padded[1 : SIDE + 1, 1 : SIDE + 1].reshape(count * SIDE * SIDE, chans)


def across_rows(left, right):
    return lax.dot_general(
        left, right, (((0,), (0,)), ((), ())), preferred_element_type=jnp.float32
    )


def against_cols(left, right):
    return lax.dot_general(
        left, right, (((1,), (1,)), ((), ())), preferred_element_type=jnp.float32
    )


def batchnorm_backward(
    activation_gradient, normed_output, standardized, inverse_deviation, norm_gain, element_count
):
    sig = jax.nn.sigmoid(normed_output)
    normed_gradient = activation_gradient * sig * (1.0 + normed_output * (1.0 - sig))
    shift_gradient, gain_gradient = lax.psum(
        (jnp.sum(normed_gradient, axis=0), jnp.sum(normed_gradient * standardized, axis=0)),
        ("dp", "rep"),
    )
    hidden_gradient = (
        norm_gain
        * inverse_deviation
        * (
            normed_gradient
            - shift_gradient / element_count
            - standardized * gain_gradient / element_count
        )
    )
    return (hidden_gradient, gain_gradient, shift_gradient)


def gram_of(x):
    return lax.dot_general(x, x, (((0,), (0,)), ((), ())), precision=HIGH)


def orthogonal(x, gram):
    scale = jnp.sqrt(jnp.trace(gram)) + 1e-07
    gram = gram / (scale * scale)
    unit = jnp.eye(gram.shape[0], dtype=jnp.float32)
    product = None
    for turn in range(TURNS):
        square = jnp.dot(gram, gram, precision=HIGH)
        factor = COEF_A * unit + COEF_B * gram + COEF_C * square
        product = factor if product is None else jnp.dot(product, factor, precision=HIGH)
        if turn < TURNS - 1:
            gram = jnp.dot(jnp.dot(gram, factor, precision=HIGH), factor, precision=HIGH)
    return jnp.dot(x / scale, product, precision=HIGH)


def adam_update(weight, first, second, grad, rate):
    first = 0.9 * first + 0.1 * grad
    second = 0.999 * second + 0.001 * grad * grad
    mhat = first / (1.0 - 0.9**STEP)
    vhat = second / (1.0 - 0.999**STEP)
    return (weight - rate * (mhat / (jnp.sqrt(vhat) + 1e-08) + 0.01 * weight), first, second)


def local(
    images,
    labels,
    conv1,
    conv2,
    classifier,
    class_bias,
    batchnorm_parameters,
    conv1_mom,
    conv2_mom,
    class_m,
    class_v,
    bias_m,
    bias_v,
    norm_m,
    norm_v,
    conv1_live,
    conv2_live,
    conv1_next,
    conv2_next,
):
    count = images.shape[0]
    c_in = images.shape[3]
    c_mid = conv1.shape[1]
    classes = class_bias.shape[0]
    all_images = count * lax.axis_size("dp") * lax.axis_size("rep")
    element_count = all_images * SIDE * SIDE
    n_dp, n_rep = lax.axis_size("dp"), lax.axis_size("rep")
    x = images.transpose(1, 2, 0, 3).reshape(SIDE * SIDE * count, c_in)
    (hidden_first, hidden_second, pad, w2b, stat, grad_z, pooled, loss_part, gbias_part, dpool) = run_a(
        n_dp, n_rep, x, conv1, conv2, classifier.T, conv1_live, conv2_live, class_bias.reshape(1, -1),
        batchnorm_parameters.reshape(4, c_mid), labels.reshape(-1, 1))
    w2b = w2b.reshape(-1, c_mid)
    loss_sum, g_bias = lax.psum((loss_part[0, 0], gbias_part[0, :classes]), ("dp", "rep"))
    standardized_first = (hidden_first - stat[0]) * stat[1]
    inverse_deviation_first = stat[1]
    normed_first = batchnorm_parameters[0, 0] * standardized_first + batchnorm_parameters[0, 1]
    standardized_second = (hidden_second - stat[2]) * stat[3]
    inverse_deviation_second = stat[3]
    normed_second = batchnorm_parameters[1, 0] * standardized_second + batchnorm_parameters[1, 1]
    inputs = x
    g_class = across_rows(pooled, grad_z[:, :classes])
    pieces = [pad[dy:dy+7, dx*count:dx*count+7*count, :].reshape(-1, c_mid) for dy in range(3) for dx in range(3)]
    patches = jnp.concatenate(pieces, axis=1)
    gradient_activation_second = jnp.broadcast_to(dpool[None], (49, count, c_mid)).reshape(-1, c_mid)
    grad_h2, gain_two, shift_two = batchnorm_backward(
        gradient_activation_second,
        normed_second,
        standardized_second,
        inverse_deviation_second,
        batchnorm_parameters[1, 0],
        element_count,
    )
    grad_h2 = grad_h2.astype(jnp.bfloat16)
    g_conv2 = across_rows(patches, grad_h2)
    gradient_activation_first = fold_rows(against_cols(grad_h2, w2b), count, c_mid)
    grad_h1, gain_one, shift_one = batchnorm_backward(
        gradient_activation_first,
        normed_first,
        standardized_first,
        inverse_deviation_first,
        batchnorm_parameters[0, 0],
        element_count,
    )
    g_conv1 = across_rows(inputs, grad_h1.astype(jnp.bfloat16))
    rows_one, rows_two, rows_head = (
        lax.psum_scatter(g_conv1, "rep", scatter_dimension=0, tiled=True),
        lax.psum_scatter(g_conv2, "rep", scatter_dimension=0, tiled=True),
        lax.psum_scatter(g_class, "rep", scatter_dimension=0, tiled=True),
    )
    rows_one, rows_two, rows_head = lax.psum((rows_one, rows_two, rows_head), "dp")
    mom_one = 0.5 * conv1_mom + rows_one
    mom_two = 0.5 * conv2_mom + rows_two

    gram_one, gram_two = lax.psum((gram_of(mom_one), gram_of(mom_two)), "rep")
    ortho_one, ortho_two = orthogonal(mom_one, gram_one), orthogonal(mom_two, gram_two)
    conv1_new = (conv1 - 1.0 * ortho_one) * conv1_next.astype(jnp.float32)
    conv2_new = (conv2 - 1.0 * ortho_two) * conv2_next.astype(jnp.float32)
    head_new, head_m, head_v = adam_update(classifier, class_m, class_v, rows_head, 0.03)
    bias_new, first_b, second_b = adam_update(class_bias, bias_m, bias_v, g_bias, 0.2)
    g_norm = jnp.stack([jnp.stack([gain_one, shift_one]), jnp.stack([gain_two, shift_two])])
    norm_new, first_n, second_n = adam_update(batchnorm_parameters, norm_m, norm_v, g_norm, 0.2)
    return (
        loss_sum,
        conv1_new,
        conv2_new,
        head_new,
        bias_new,
        norm_new,
        mom_one,
        mom_two,
        head_m,
        head_v,
        first_b,
        second_b,
        first_n,
        second_n[0],
        second_n[1],
    )


def solution(mesh):
    placed = (
        P(("dp", "rep"), None, None, None),
        P(("dp", "rep")),
        P("rep", None),
        P("rep", None),
        P("rep", None),
        P(),
        P(),
        P("rep", None),
        P("rep", None),
        P("rep", None),
        P("rep", None),
        P(),
        P(),
        P(),
        P(),
        P("rep", None),
        P("rep", None),
        P("rep", None),
        P("rep", None),
    )
    return jax.shard_map(
        local,
        mesh=mesh,
        in_specs=placed,
        out_specs=(
            P(),
            P("rep", None),
            P("rep", None),
            P("rep", None),
            P(),
            P(),
            P("rep", None),
            P("rep", None),
            P("rep", None),
            P("rep", None),
            P(),
            P(),
            P(),
            P(),
            P(),
        ),
        check_vma=False,
    )
```

```python
import functools

import jax
import jax.numpy as jnp
from jax import lax
from jax.experimental import pallas as pl
from jax.experimental.pallas import tpu as pltpu
from jax.sharding import PartitionSpec as P

SIDE = 7
TURNS = 5
STEP = 5
NORM_EPS = 1e-05
COEF_A = 3.4445
COEF_B = -4.775
COEF_C = 2.0315
MESH = pl.DeviceIdType.MESH
BF = jnp.bfloat16
F32 = jnp.float32
DMA = pltpu.SemaphoreType.DMA


def nn(a, b):
    return jnp.dot(a, b, preferred_element_type=F32)


def nt(a, b):
    return lax.dot_general(a, b, (((1,), (1,)), ((), ())), preferred_element_type=F32)


def tn(a, b):
    return lax.dot_general(a, b, (((0,), (0,)), ((), ())), preferred_element_type=F32)


def sigmoid(v):
    return 1.0 / (1.0 + jnp.exp(-v))


class Place:
    def __init__(self, n_dp, n_rep):
        self.n_dp, self.n_rep = n_dp, n_rep
        self.chips = n_dp // 2 * n_rep
        self.dp, self.rep = lax.axis_index("dp"), lax.axis_index("rep")
        self.core = lax.rem(self.dp, 2)
        self.chip = self.dp // 2 * n_rep + self.rep

    def flip(self, bit):
        half = 1 << bit
        set_now = lax.rem(self.dp // half, 2)
        return {"dp": self.dp + half - 2 * half * set_now, "rep": self.rep}

    def flip_rep(self, bit):
        half = 1 << bit
        set_now = lax.rem(self.rep // half, 2)
        return {"dp": self.dp, "rep": self.rep + half - 2 * half * set_now}

    def other_chip(self, step):
        to = lax.rem(self.chip + step, self.chips)
        return {"dp": to // self.n_rep * 2 + self.core, "rep": lax.rem(to, self.n_rep)}

    def other_rep(self, step):
        return {"dp": self.dp, "rep": lax.rem(self.rep + step, self.n_rep)}


def send(src, dst, send_sem, recv_sem, to):
    copy = pltpu.make_async_remote_copy(src, dst, send_sem, recv_sem, to, MESH)
    copy.start()


def wait_bytes(ref, sem):
    pltpu.make_async_copy(ref, ref, sem).wait()


def enter(place):
    barrier = pltpu.get_barrier_semaphore()

    def greet(step, carry):
        pl.semaphore_signal(barrier, 1, device_id=place.other_chip(step), device_id_type=MESH)
        return carry

    lax.fori_loop(1, place.chips, greet, 0)
    pl.semaphore_signal(barrier, 1, device_id=place.flip(0), device_id_type=MESH)
    pl.semaphore_wait(barrier, place.chips)


def sum_over_all(place, value, pair_buf, chip_buf, sems, meanwhile=None):
    pair_buf[place.core] = value
    mine = pair_buf.at[place.core]
    send(mine, mine, sems.at[0], sems.at[1], place.flip(0))
    wait_bytes(mine, sems.at[1])
    chip_buf[place.chip] = pair_buf[0] + pair_buf[1]
    block = chip_buf.at[place.chip]

    def one(step, carry):
        send(block, block, sems.at[2], sems.at[3], place.other_chip(step))
        return carry

    lax.fori_loop(1, place.chips, one, 0)
    if meanwhile is not None:
        meanwhile()
    wait_bytes(chip_buf.at[pl.ds(0, place.chips - 1)], sems.at[3])
    total = jnp.sum(chip_buf[...], axis=0)
    wait_bytes(mine, sems.at[0])
    wait_bytes(chip_buf.at[pl.ds(0, place.chips - 1)], sems.at[2])
    return total


class Total:
    def __init__(self, place, clock, pair_buf, chip_buf, sems, out):
        self.place, self.clock, self.pair, self.chip, self.sems, self.out = place, clock, pair_buf, chip_buf, sems, out
        self.step, self.ready = 0, None

    def start(self, value):
        self.pair[self.place.core] = value
        mine = self.pair.at[self.place.core]
        send(mine, mine, self.sems.at[0], self.sems.at[1], self.place.flip(0))
        self.ready = self.clock.carry("core", 2)

    def others(self):
        return self.chip.at[pl.ds(0, self.place.chips - 1)]

    def advance(self):
        place = self.place
        if self.step == 0:
            wait_bytes(self.pair.at[0], self.sems.at[1])
            self.chip[place.chip] = self.pair[0] + self.pair[1]
            block = self.chip.at[place.chip]

            def one(step, carry):
                send(block, block, self.sems.at[2], self.sems.at[3], place.other_chip(step))
                return carry

            lax.fori_loop(1, place.chips, one, 0)
            self.clock.work(0.8)
            self.ready = self.clock.now + 3.5
            self.step = 1
            return True
        wait_bytes(self.others(), self.sems.at[3])
        self.out[...] = jnp.sum(self.chip[...], axis=0)
        self.step = 2
        return False

    def drain(self):
        wait_bytes(self.pair.at[0], self.sems.at[0])
        wait_bytes(self.others(), self.sems.at[2])


class Clock:
    def __init__(self):
        self.now = 0.0
        self.free = {}

    def work(self, span):
        self.now += span

    def carry(self, link, kilobytes):
        rate, hop = {"core": (500.0, 1.0), "far": (24.0, 2.6)}.get(link, (47.0, 2.0))
        begin = max(self.now, self.free.get(link, 0.0))
        self.free[link] = begin + kilobytes / rate
        return self.free[link] + hop


class Gather:
    def __init__(self, place, buf, pieces, sems):
        self.place, self.buf, self.pieces, self.sems = place, buf, pieces, sems
        self.quarter = buf.shape[1] // 4
        self.rows = self.quarter // pieces
        self.y = lax.rem(place.dp // 2, 2)

    def at(self, block, y, piece):
        first = self.place.core * (2 * self.quarter) + y * self.quarter + piece * self.rows
        return self.buf.at[block, pl.ds(pl.multiple_of(first, 16), self.rows)]

    def blocks(self):
        return [lax.rem(self.place.rep + step, self.place.n_rep) for step in range(1, self.place.n_rep)]

    def size(self):
        return self.buf.at[pl.ds(0, self.place.n_rep - 1), pl.ds(0, self.rows)]

    def start(self, piece):
        mine = self.at(self.place.rep, self.y, piece)
        for step in range(1, self.place.n_rep):
            send(mine, mine, self.sems.at[0, piece, 0], self.sems.at[0, piece, 1], self.place.other_rep(step))

    def hop_y(self, piece):
        wait_bytes(self.size(), self.sems.at[0, piece, 1])
        for block in self.blocks():
            here = self.at(block, self.y, piece)
            send(here, here, self.sems.at[1, piece, 0], self.sems.at[1, piece, 1], self.place.flip(1))
            send(here, here, self.sems.at[2, piece, 0], self.sems.at[2, piece, 1], self.place.flip(0))

    def hop_core(self, piece):
        wait_bytes(self.size(), self.sems.at[1, piece, 1])
        for block in self.blocks():
            here = self.at(block, 1 - self.y, piece)
            send(here, here, self.sems.at[3, piece, 0], self.sems.at[3, piece, 1], self.place.flip(0))

    def finish(self, piece):
        wait_bytes(self.size(), self.sems.at[2, piece, 1])
        wait_bytes(self.size(), self.sems.at[3, piece, 1])

    def drain(self):
        for piece in range(self.pieces):
            for hop in range(4):
                wait_bytes(self.size(), self.sems.at[hop, piece, 0])


def norm_of(total, count):
    mean = total[0:1] / count
    return mean, lax.rsqrt(total[1:2] / count - mean * mean + NORM_EPS)


def over_pixels(step, init, images):
    def body(pixel, carry):
        return step(pixel, pl.multiple_of(pixel * images, 16), carry)

    return lax.fori_loop(0, SIDE * SIDE, body, init, unroll=7)


def fold(acc):
    return jnp.sum(acc, axis=0, keepdims=True)


def sums_of(h_ref, images):
    chans = h_ref.shape[1]

    def step(pixel, row, carry):
        v = h_ref[pl.ds(row, images), :]
        return carry[0] + v, carry[1] + v * v

    zero = jnp.zeros((images, chans), F32)
    one, two = over_pixels(step, (zero, zero), images)
    return jnp.concatenate([fold(one), fold(two)], axis=0)


def put_padded(pad_ref, pixel, value, images):
    y, x = pixel // SIDE, lax.rem(pixel, SIDE)
    pad_ref[1 + y, pl.ds(pl.multiple_of((1 + x) * images, 16), images), :] = value


def clear_border(pad_ref, images):
    line = SIDE * images
    pad_ref[0] = jnp.zeros(pad_ref.shape[1:], pad_ref.dtype)
    pad_ref[SIDE + 1] = jnp.zeros(pad_ref.shape[1:], pad_ref.dtype)
    edge = jnp.zeros((SIDE, images, pad_ref.shape[2]), pad_ref.dtype)
    pad_ref[1 : SIDE + 1, 0:images, :] = edge
    pad_ref[1 : SIDE + 1, images + line : 2 * images + line, :] = edge


def build_patches(pad_ref, to_ref):
    images, chans = pad_ref.shape[1] // (SIDE + 2), pad_ref.shape[2]
    line = SIDE * images
    for k in range(9):
        dy, dx = divmod(k, 3)
        piece = pad_ref[dy : dy + SIDE, dx * images : dx * images + line, :]
        to_ref[0 : SIDE * line, k * chans : (k + 1) * chans] = piece.reshape(SIDE * line, chans)


def kernel_a(n_dp, n_rep, *refs):
    (x_hbm, w1_hbm, w2_hbm, head_hbm, live1_hbm, live2_hbm, bias_ref, norm_ref, label_ref,
     h1_ref, h2_ref, pad_ref, w2b, stat_ref, factor_ref, head_sums_ref, dpool_ref, x_mean_ref,
     x_ref, f1, i1, f2, i2, fh, w1b, head_b, patches, bias_pad, x_sum, pair_buf, chip_buf, x_pair, x_chip,
     load_sem, w1_sem, w2_sem, head_sem, sum_sem, x_sem) = refs
    place = Place(n_dp, n_rep)
    core, rep = place.core, place.rep
    half1, half2, mid = w1b.shape[1], w2b.shape[1], w1b.shape[2]
    classes, head_cols = fh.shape
    wide = head_b.shape[1]
    rows = x_ref.shape[0]
    images = rows // (SIDE * SIDE)
    all_images = images * n_dp * n_rep
    count = all_images * SIDE * SIDE

    pairs = [(w1_hbm, f1), (live1_hbm, i1), (w2_hbm, f2), (live2_hbm, i2), (x_hbm, x_ref), (head_hbm, fh)]
    loads = [pltpu.make_async_copy(a, b, load_sem.at[k]) for k, (a, b) in enumerate(pairs)]
    for load in loads:
        load.start()
    g1, g2, gh = Gather(place, w1b, 2, w1_sem), Gather(place, w2b, 3, w2_sem), Gather(place, head_b, 1, head_sem)

    def mask(value, live, to, first, size):
        at = pl.ds(pl.multiple_of(first, 16), size)
        to[rep, at, :] = (value[at, :] * live[at, :].astype(F32)).astype(BF)

    def spread(gather, value, live, to):
        quarter = gather.quarter
        mine = core * 2 + gather.y
        for piece in range(gather.pieces):
            mask(value, live, to, mine * quarter + piece * gather.rows, gather.rows)
            gather.start(piece)
        for other in range(1, 4):
            mask(value, live, to, lax.rem(mine + other, 4) * quarter, quarter)

    loads[0].wait()
    loads[1].wait()
    enter(place)
    spread(g1, f1, i1, w1b)
    loads[2].wait()
    loads[3].wait()
    spread(g2, f2, i2, w2b)
    loads[5].wait()
    head_b[rep, 0:classes, :] = fh[...].astype(BF)
    head_b[rep, classes:, :] = jnp.zeros((wide - classes, head_cols), BF)
    gh.start(0)
    clear_border(pad_ref, images)
    bias_pad[:, 0:classes] = bias_ref[...]
    bias_pad[:, classes:] = jnp.zeros((1, wide - classes), F32)
    loads[4].wait()

    def cols(block, half):
        return pl.ds(pl.multiple_of(block * half, 128), half)

    h1_ref[...] = nn(x_ref[:, cols(rep, half1)], w1b[rep])
    x_total = Total(place, Clock(), x_pair, x_chip, x_sem, x_sum)
    x_sums = nn(jnp.ones((8, rows), BF), x_ref[...])
    parts = x_ref.shape[1] // mid
    x_total.start(jnp.concatenate([x_sums[0:1, k * mid : (k + 1) * mid] for k in range(parts)], axis=0))
    for piece in range(2):
        g1.hop_y(piece)
    for piece in range(2):
        g1.hop_core(piece)
    g2.hop_y(0)
    for piece in range(2):
        g1.finish(piece)
    for block in g1.blocks():
        h1_ref[...] += nn(x_ref[:, cols(block, half1)], w1b[block])

    sums = sums_of(h1_ref, images)
    total = sum_over_all(place, jnp.concatenate([sums, sums[0:1]], axis=0), pair_buf.at[0], chip_buf.at[0], sum_sem.at[0], lambda: g2.hop_y(1))
    mean1, inv1 = norm_of(total, count)
    scale1 = norm_ref[0, 0:1] * inv1
    move1 = norm_ref[0, 1:2] - mean1 * scale1
    g2.hop_core(0)
    g2.hop_core(1)

    def act1(pixel, row, carry):
        v = h1_ref[pl.ds(row, images), :] * scale1 + move1
        act = v * sigmoid(v)
        put_padded(pad_ref, pixel, act.astype(BF), images)
        return carry + act

    act_sums = over_pixels(act1, jnp.zeros((images, mid), F32), images)
    x_total.advance()
    g2.hop_y(2)
    build_patches(pad_ref, patches)
    if half2 % 128:
        g2.hop_core(2)
        gh.hop_y(0)
        gh.hop_core(0)
        for piece in range(3):
            g2.finish(piece)
        for block in range(n_rep):
            part = nn(patches[:, block * half2 : (block + 1) * half2], w2b[block])
            h2_ref[...] = part if block == 0 else h2_ref[...] + part
    else:
        h2_ref[...] = nn(patches[:, cols(rep, half2)], w2b[rep])
        g2.hop_core(2)
        gh.hop_y(0)
        gh.hop_core(0)
        for piece in range(3):
            g2.finish(piece)
        for block in g2.blocks():
            h2_ref[...] += nn(patches[:, cols(block, half2)], w2b[block])

    sums = jnp.concatenate([sums_of(h2_ref, images), fold(act_sums)], axis=0)
    total = sum_over_all(place, sums, pair_buf.at[1], chip_buf.at[1], sum_sem.at[1])
    act_mean = total[2:3] / count
    mean2, inv2 = norm_of(total, count)
    scale2 = norm_ref[1, 0:1] * inv2
    move2 = norm_ref[1, 1:2] - mean2 * scale2

    def pool(pixel, row, carry):
        v = h2_ref[pl.ds(row, images), :] * scale2 + move2
        return carry + v * sigmoid(v)

    pooled = (over_pixels(pool, jnp.zeros((images, mid), F32), images) / (SIDE * SIDE)).astype(BF)
    factor_ref[:, wide:] = pooled
    gh.finish(0)
    logits = bias_pad[...]
    for block in range(n_rep):
        logits = logits + nt(factor_ref[:, wide + block * head_cols : wide + (block + 1) * head_cols], head_b[block])
    column = lax.broadcasted_iota(jnp.int32, (images, wide), 1)
    shown = jnp.where(column < classes, logits, -jnp.inf)
    top = jnp.max(shown, axis=1, keepdims=True)
    lse = top + jnp.log(jnp.sum(jnp.exp(shown - top), axis=1, keepdims=True))
    image = lax.broadcasted_iota(jnp.int32, (images, wide), 0)
    label = jnp.zeros((images, wide), jnp.int32)
    for k in range(images):
        label = jnp.where(image == k, label_ref[k], label)
    hit = (column == label).astype(F32)
    target = jnp.sum(logits * hit, axis=1, keepdims=True)
    loss = jnp.sum(lse - target, axis=0, keepdims=True)
    grad = (jnp.exp(shown - lse) - hit) / all_images
    bias_sums = jnp.sum(grad, axis=0, keepdims=True)
    for k in range(wide // mid):
        head_sums_ref[k : k + 1, :] = bias_sums[:, k * mid : (k + 1) * mid]
    head_sums_ref[wide // mid :, :] = jnp.broadcast_to(loss, (1, mid))
    dz = grad.astype(BF)
    factor_ref[:, 0:wide] = dz
    for block in range(n_rep):
        dpool_ref[:, block * head_cols : (block + 1) * head_cols] = nn(dz, head_b[block]) / (SIDE * SIDE)
    dpool = dpool_ref[...]

    def back2(pixel, row, carry):
        h = h2_ref[pl.ds(row, images), :]
        v = h * scale2 + move2
        sig = sigmoid(v)
        dy = dpool * sig * (1.0 + v * (1.0 - sig))
        return carry[0] + dy, carry[1] + dy * ((h - mean2) * inv2)

    zero = jnp.zeros((images, mid), F32)
    one, two = over_pixels(back2, (zero, zero), images)
    sums = jnp.concatenate([fold(one), fold(two), fold(one)], axis=0)
    total = sum_over_all(place, sums, pair_buf.at[2], chip_buf.at[2], sum_sem.at[2])
    stat_ref[...] = jnp.concatenate([mean1, inv1, mean2, inv2, total[0:2], act_mean, act_mean], axis=0)
    x_total.advance()
    for k in range(parts):
        x_mean_ref[:, k * mid : (k + 1) * mid] = x_sum[k : k + 1, :] / count
    for gather in (g1, g2, gh, x_total):
        gather.drain()


def run_a(n_dp, n_rep, x, conv1, conv2, head, live1, live2, bias, norm, labels):
    rows, mid = x.shape[0], conv1.shape[1]
    images = rows // (SIDE * SIDE)
    half1, half2 = conv1.shape[0], conv2.shape[0]
    classes, head_cols = head.shape
    wide = (classes + 127) // 128 * 128
    chips, parts = n_dp // 2 * n_rep, x.shape[1] // mid
    shape = jax.ShapeDtypeStruct
    vmem, hbm = pl.BlockSpec(memory_space=pltpu.VMEM), pl.BlockSpec(memory_space=pl.ANY)
    return pl.pallas_call(
        functools.partial(kernel_a, n_dp, n_rep),
        out_shape=(
            shape((rows, mid), F32), shape((rows, mid), F32),
            shape((SIDE + 2, (SIDE + 2) * images, mid), BF), shape((n_rep, half2, mid), BF),
            shape((8, mid), F32), shape((images, wide + mid), BF), shape((wide // mid + 1, mid), F32),
            shape((images, mid), F32), shape((1, x.shape[1]), F32),
        ),
        in_specs=[hbm] * 6 + [vmem] * 2 + [pl.BlockSpec(memory_space=pltpu.SMEM)],
        out_specs=[vmem] * 9,
        scratch_shapes=[
            pltpu.VMEM(x.shape, BF),
            pltpu.VMEM((half1, mid), F32), pltpu.VMEM((half1, mid), jnp.int32),
            pltpu.VMEM((half2, mid), F32), pltpu.VMEM((half2, mid), jnp.int32),
            pltpu.VMEM((classes, head_cols), F32),
            pltpu.VMEM((n_rep, half1, mid), BF), pltpu.VMEM((n_rep, wide, head_cols), BF),
            pltpu.VMEM((rows, 9 * mid), BF), pltpu.VMEM((1, wide), F32),
            pltpu.VMEM((parts, mid), F32),
            pltpu.VMEM((3, 2, 3, mid), F32), pltpu.VMEM((3, chips, 3, mid), F32),
            pltpu.VMEM((2, parts, mid), F32), pltpu.VMEM((chips, parts, mid), F32),
            DMA((6,)), DMA((4, 2, 2)), DMA((4, 3, 2)), DMA((4, 1, 2)), DMA((3, 4)), DMA((4,)),
        ],
        compiler_params=pltpu.CompilerParams(
            collective_id=1, has_side_effects=True, vmem_limit_bytes=60 * 2**20
        ),
        name="forward",
    )(x, conv1, conv2, head, live1, live2, bias, norm, labels)


class Factors:
    def __init__(self, place, clock, buf, sems):
        self.place, self.clock, self.buf, self.sems = place, clock, buf, sems
        reps = [("rep", b) for b in range(place.n_rep.bit_length() - 1)]
        dps = [("dp", b) for b in reversed(range(1, place.n_dp.bit_length() - 1))]
        self.order = reps + dps + [("dp", 0)]
        self.index = 0
        for k, (axis, bit) in enumerate(self.order):
            self.index = self.index + (1 << k) * lax.rem((place.rep if axis == "rep" else place.dp) // (1 << bit), 2)
        self.step, self.ready = 0, None

    def start(self, value_ref):
        load = pltpu.make_async_copy(value_ref, self.buf.at[self.index], self.sems.at[len(self.order), 0])
        load.start()
        load.wait()
        self.ship()

    def ship(self):
        held = 1 << self.step
        mine = self.buf.at[pl.ds(self.index // held * held, held)]
        axis, bit = self.order[self.step]
        to = self.place.flip_rep(bit) if axis == "rep" else self.place.flip(bit)
        send(mine, mine, self.sems.at[self.step, 0], self.sems.at[self.step, 1], to)
        link = "x" if axis == "rep" else {0: "core", 1: "y", 2: "z"}.get(bit, "far")
        self.ready = self.clock.carry(link, held * self.buf.shape[1] * self.buf.shape[2] * 2 / 1024)

    def advance(self):
        wait_bytes(self.buf.at[pl.ds(0, 1 << self.step)], self.sems.at[self.step, 1])
        self.step += 1
        if self.step == len(self.order):
            return False
        self.ship()
        return True

    def drain(self):
        for k in range(len(self.order)):
            wait_bytes(self.buf.at[pl.ds(0, 1 << k)], self.sems.at[k, 0])


class Piece:
    def __init__(self, plan, place, clock, full, refs):
        self.plan, self.place, self.clock, self.full = plan, place, clock, full
        self.acc = refs[plan["acc"]]
        self.outgoing = [refs[k] for k in plan["outgoing"]]
        self.incoming = [refs[k] for k in plan["incoming"]]
        self.sems = refs[plan["sems"]]
        self.r0, self.nr, self.q0, self.nq = 0, place.n_rep, 0, plan["size"] // 2
        self.step, self.ready, self.undo = 0, None, []
        self.base = plan["part"] * plan["size"] + place.core * self.nq

    def bit(self, level):
        axis, bit = level["axis"], level["bit"]
        return lax.rem((self.place.rep if axis == "rep" else self.place.dp) // (1 << bit), 2)

    def partner(self, level):
        return self.place.flip_rep(level["bit"]) if level["axis"] == "rep" else self.place.flip(level["bit"])

    def kept(self, r0, nr, q0, nq):
        return (pl.ds(r0, nr), pl.ds(pl.multiple_of(q0, 16), nq), slice(None))

    def ship(self, src, dst, slot, to, link, kilobytes):
        send(src, dst, self.sems.at[slot, 0], self.sems.at[slot, 1], to)
        self.ready = self.clock.carry(link, kilobytes)

    def start(self):
        nbytes = self.place.n_rep * self.nq
        self.ship(self.outgoing[0], self.incoming[0], 0, self.place.flip(0), "core", nbytes)

    def advance(self):
        levels = self.plan["levels"]
        if self.step <= len(levels):
            wait_bytes(self.incoming[self.step], self.sems.at[self.step, 1])
            at = self.kept(self.r0, self.nr, self.q0, self.nq)
            self.acc[at] = self.acc[at] + self.incoming[self.step][...].astype(F32)
            self.clock.work(0.2)
        if self.step < len(levels):
            level = levels[self.step]
            self.begin(level)
            self.step += 1
            return True
        if self.step == len(levels):
            rows = self.rows(self.q0, self.nq)
            self.full[rows, :] = self.acc[self.kept(self.r0, self.nr, self.q0, self.nq)][0].astype(BF)
            self.step += 1
        else:
            bit = self.undo.pop()
            if bit is None:
                wait_bytes(self.full.at[pl.ds(0, self.nq)], self.sems.at[self.step, 1])
                return False
            wait_bytes(self.full.at[pl.ds(0, self.nq)], self.sems.at[self.step, 1])
            self.q0 = self.q0 - bit * self.nq
            self.nq *= 2
            self.step += 1
        back = [k for k in reversed(levels) if k["axis"] == "dp" and k["halve"]]
        done = self.step - len(levels) - 1
        here = self.full.at[self.rows(self.q0, self.nq)]
        if done < len(back):
            level = back[done]
            self.undo.append(self.bit(level))
            self.ship(here, here, self.step, self.partner(level), level["link"], self.nq)
        else:
            self.undo.append(None)
            self.ship(here, here, self.step, self.place.flip(0), "core", self.nq)
        return True

    def rows(self, q0, nq):
        return pl.ds(pl.multiple_of(self.base + q0, 16), nq)

    def begin(self, level):
        bit = self.bit(level)
        out = self.outgoing[self.step + 1]
        if level["halve"]:
            r1, q1 = self.r0, self.q0
            if level["axis"] == "rep":
                self.nr //= 2
                self.r0, r1 = self.r0 + bit * self.nr, self.r0 + (1 - bit) * self.nr
            else:
                self.nq //= 2
                self.q0, q1 = self.q0 + bit * self.nq, self.q0 + (1 - bit) * self.nq
            out[...] = self.acc[self.kept(r1, self.nr, q1, self.nq)].astype(BF)
        else:
            at = self.kept(self.r0, self.nr, self.q0, self.nq)
            out[...] = self.acc[at].astype(BF)
            self.acc[at] = out[...].astype(F32)
        self.ship(out, self.incoming[self.step + 1], self.step + 1, self.partner(level), level["link"], self.nr * self.nq)

    def drain(self):
        levels = self.plan["levels"]
        for k in range(len(levels) + 1):
            wait_bytes(self.outgoing[k], self.sems.at[k, 0])
        size = self.nq
        back = [k for k in reversed(levels) if k["axis"] == "dp" and k["halve"]]
        first = size >> len(back)
        for k in range(len(back)):
            wait_bytes(self.full.at[pl.ds(0, first << k)], self.sems.at[len(levels) + 1 + k, 0])
        wait_bytes(self.full.at[pl.ds(0, size)], self.sems.at[len(levels) + 1 + len(back), 0])


def plan_pieces(n_dp, n_rep, halves, mid, scratch):
    plans = []
    for conv, (half, parts, firsts) in enumerate(halves):
        fits = half % (parts * 16 * n_dp) == 0 and half // parts // 2 % 128 == 0
        if not fits:
            parts = 1
        for part in range(parts):
            size = half // parts
            reps = [("rep", b) for b in reversed(range(n_rep.bit_length() - 1))]
            dps = [("dp", b) for b in range(1, n_dp.bit_length() - 1)]
            order = reps + dps if firsts[part] == "rep" else dps[:1] + reps + dps[1:]
            nr, nq, levels, shapes = n_rep, size // 2, [], []
            shapes.append((nr, nq, mid))
            for axis, bit in order:
                halve = axis == "rep" or nq // 2 % 16 == 0
                if halve and axis == "rep":
                    nr //= 2
                elif halve:
                    nq //= 2
                link = "x" if axis == "rep" else {1: "y", 2: "z"}.get(bit, "far")
                levels.append({"axis": axis, "bit": bit, "halve": halve, "link": link})
                shapes.append((nr, nq, mid))
            plan = {"conv": conv, "part": part, "size": size, "half": half, "levels": levels, "fits": fits}

            def add(spec):
                scratch.append(spec)
                return len(scratch) - 1

            plan["acc"] = add(pltpu.VMEM((n_rep, size // 2, mid), F32))
            plan["outgoing"] = [add(pltpu.VMEM(s, BF)) for s in shapes]
            plan["incoming"] = [add(pltpu.VMEM(s, BF)) for s in shapes]
            plan["sems"] = add(DMA((2 * len(levels) + 2, 2)))
            plans.append(plan)
    return plans


def halves_of(v):
    high = v.astype(BF)
    return high, (v - high.astype(F32)).astype(BF)


def mm(a, b):
    return nn(a[0], b[0]) + (nn(a[0], b[1]) + nn(a[1], b[0]))


def square(a):
    cross = nn(a[0], a[1])
    return nn(a[0], a[0]) + (cross + cross.T)


def unit(n):
    return lax.broadcasted_iota(jnp.int32, (n, n), 0) == lax.broadcasted_iota(jnp.int32, (n, n), 1)


def newton_turn(turn, g_ref, q_ref):
    n = g_ref.shape[0]
    gram = halves_of(g_ref[...])
    factor = COEF_A * unit(n).astype(F32) + COEF_B * g_ref[...] + COEF_C * square(gram)
    factors = halves_of(factor)
    if turn == 0:
        q_ref[...] = factor
    else:
        q_ref[...] = mm(halves_of(q_ref[...]), factors)
    if turn < TURNS - 1:
        g_ref[...] = mm(halves_of(mm(gram, factors)), factors)


class Gram:
    def __init__(self, place, clock, g_ref, cross_ref, packed, sems):
        self.place, self.clock, self.g, self.cross, self.packed, self.sems = place, clock, g_ref, cross_ref, packed, sems
        self.fresh = True
        self.step, self.ready = 0, None
        self.b, self.levels = g_ref.shape[0] // 4, place.n_rep.bit_length() - 1

    def add(self, value):
        high, low = halves_of(value)
        if self.fresh:
            self.g[...] = tn(high, high)
            self.cross[...] = tn(high, low)
        else:
            self.g[...] += tn(high, high)
            self.cross[...] += tn(high, low)
        self.fresh = False

    def start(self):
        b = self.b
        g = self.g[...] + self.cross[...] + self.cross[...].T
        to = self.packed
        to[0, 0, :, 0 : 4 * b] = g[0:b, :]
        to[0, 0, :, 4 * b :] = g[3 * b :, 3 * b :]
        to[0, 1, :, 0 : 3 * b] = g[b : 2 * b, b:]
        to[0, 1, :, 3 * b :] = g[2 * b : 3 * b, 2 * b :]
        self.clock.work(1.5)
        self.ship()

    def ship(self):
        mine, theirs = self.packed.at[0, self.place.core], self.packed.at[self.step + 1, self.place.core]
        send(mine, theirs, self.sems.at[self.step, 0], self.sems.at[self.step, 1], self.place.flip_rep(self.step))
        self.ready = self.clock.carry("x", 5 * self.b * self.b * 4 / 1024)

    def advance(self):
        place, to, levels = self.place, self.packed, self.levels
        if self.step < levels:
            wait_bytes(to.at[0, 0], self.sems.at[self.step, 1])
            wait_bytes(to.at[0, 0], self.sems.at[self.step, 0])
            last = self.step + 1 == levels
            to[levels + 1 if last else 0, place.core] = to[0, place.core] + to[self.step + 1, place.core]
            self.step += 1
            if not last:
                self.ship()
                return True
            mine = to.at[levels + 1, place.core]
            send(mine, mine, self.sems.at[levels, 0], self.sems.at[levels, 1], place.flip(0))
            self.ready = self.clock.carry("core", 330)
            return True
        wait_bytes(to.at[0, 0], self.sems.at[levels, 1])
        b, n = self.b, levels + 1
        g = self.g
        g[0:b, :] = to[n, 0, :, 0 : 4 * b]
        g[3 * b :, 3 * b :] = to[n, 0, :, 4 * b :]
        g[b : 2 * b, b:] = to[n, 1, :, 0 : 3 * b]
        g[2 * b : 3 * b, 2 * b :] = to[n, 1, :, 3 * b :]
        for i in range(1, 4):
            for j in range(i):
                g[i * b : (i + 1) * b, j * b : (j + 1) * b] = g[j * b : (j + 1) * b, i * b : (i + 1) * b].T
        trace = jnp.sum(jnp.sum(jnp.where(unit(4 * b), g[...], 0.0), axis=0, keepdims=True), axis=1, keepdims=True)
        self.scale = jnp.sqrt(trace) + 1e-07
        g[...] = g[...] / (self.scale * self.scale)
        self.clock.work(1.0)
        return False

    def drain(self):
        wait_bytes(self.packed.at[0, 0], self.sems.at[self.levels, 0])


def kernel_b(n_dp, n_rep, plans, *refs):
    (x_hbm, mom1_hbm, mom2_hbm, h1_ref, h2_ref, pad_ref, w2b, stat_ref, dpool_ref, norm_ref, x_mean_ref, factor_ref,
     head_sums_ref,
     g1_ref, g2_ref, q1_ref, q2_ref, sums_ref, m1_ref, m2_ref, s1_ref, s2_ref, factors_ref, head_ref,
     x_ref, mom_ref, da1, dpad, dh, patches, gram1, gram2, cross, packed, pair_buf, chip_buf, s_total,
     s_pair, s_chip, head_pair, head_chip,
     load_sem, mom_sem, sum_sem, gram_sem, s_sem, head_sem, factor_sem) = refs[:48]
    refs = refs[48:]
    place, clock = Place(n_dp, n_rep), Clock()
    core = place.core
    mid = h1_ref.shape[1]
    rows = h1_ref.shape[0]
    line = rows // SIDE
    images = line // SIDE
    count = images * n_dp * n_rep * SIDE * SIDE

    half1, half2 = g1_ref.shape[0], g2_ref.shape[0]
    extra = slice(rows, rows + 16)
    first_row = lax.broadcasted_iota(jnp.int32, (16, mid), 0) < 1
    two_rows = lax.broadcasted_iota(jnp.int32, (16, mid), 0) < 2

    x_load = pltpu.make_async_copy(x_hbm, x_ref.at[pl.ds(0, rows)], load_sem)
    x_load.start()
    mom_hbm = [mom2_hbm, mom1_hbm]
    mom_loads = []
    for k, plan in enumerate(plans):
        src = mom_hbm[plan["conv"]].at[pl.ds(plan["part"] * plan["size"], plan["size"])]
        mom_loads.append(pltpu.make_async_copy(src, mom_ref.at[k % 2, pl.ds(0, plan["size"])], mom_sem.at[k]))
    for load in mom_loads[:2]:
        load.start()
    enter(place)

    mean1, inv1, mean2, inv2 = (stat_ref[k : k + 1] for k in range(4))
    shift2, gain2 = stat_ref[4:5] / count, stat_ref[5:6] / count
    scale1, scale2 = norm_ref[0, 0:1] * inv1, norm_ref[1, 0:1] * inv2
    move1, move2 = norm_ref[0, 1:2] - mean1 * scale1, norm_ref[1, 1:2] - mean2 * scale2
    dpool = dpool_ref[...]

    factors = Factors(place, clock, factors_ref, factor_sem)
    factors.start(factor_ref)
    head_total = Total(place, clock, head_pair, head_chip, head_sem, head_ref)
    head_total.start(head_sums_ref[...])
    s_totals = [Total(place, clock, s_pair.at[k], s_chip.at[k], s_sem.at[k], s_total.at[k]) for k in range(2)]

    clear_border(dpad, images)

    def back2(pixel, row, carry):
        h = h2_ref[pl.ds(row, images), :]
        v = h * scale2 + move2
        sig = sigmoid(v)
        dy = dpool * sig * (1.0 + v * (1.0 - sig))
        put = (scale2 * (dy - shift2 - (h - mean2) * inv2 * gain2)).astype(BF)
        put_padded(dpad, pixel, put, images)
        dh[pl.ds(row, images), :] = put
        return carry + put.astype(F32)

    zero = jnp.zeros((images, mid), F32)

    def offset(acc, total):
        share = fold(acc).astype(BF)
        dh[extra, :] = jnp.where(first_row, -share.astype(F32), 0.0).astype(BF)
        total.start(share.astype(F32))

    offset(over_pixels(back2, zero, images), s_totals[0])
    build_patches(pad_ref, patches)
    act_mean = stat_ref[6:7]
    for k in range(9):
        dy, dx = divmod(k, 3)
        inside = (1.0 if dy == 1 else 6 / 7) * (1.0 if dx == 1 else 6 / 7)
        patches[extra, k * mid : (k + 1) * mid] = jnp.where(two_rows, act_mean * inside, 0.0).astype(BF)
    for k in range(0, x_ref.shape[1], mid):
        x_ref[extra, k : k + mid] = jnp.where(two_rows, x_mean_ref[:, k : k + mid], 0.0).astype(BF)
    for source, to, half in ((patches, m2_ref, half2), (x_ref, m1_ref, half1)):
        for block in range(n_rep):

            @pl.when(place.rep == block)
            def own(source=source, to=to, half=half, block=block):
                to[...] = source[extra, block * half : (block + 1) * half]

    fulls = [g2_ref, g1_ref]
    pieces = [Piece(plan, place, clock, fulls[plan["conv"]], refs) for plan in plans]
    grams = [Gram(place, clock, g, cross, packed.at[k], gram_sem.at[k]) for k, g in enumerate((gram2, gram1))]
    active, waiting = [factors, head_total, s_totals[0]], []
    turns = []

    def gradient(piece, source):
        plan = piece.plan
        part = plan["size"] // 2
        if plan["fits"]:
            for who, store in ((1 - core, piece.outgoing[0]), (core, piece.acc)):
                for block in range(n_rep):
                    first = block * plan["half"] + plan["part"] * plan["size"] + who * part
                    lanes = source[:, pl.ds(pl.multiple_of(first, 128), part)]
                    store[block] = tn(lanes, dh[...]).astype(store.dtype)
                clock.work(part * n_rep * 0.0017)
                if store is not piece.acc:
                    piece.start()
        else:
            for block in range(n_rep):
                for who in range(2):
                    first = block * plan["half"] + plan["part"] * plan["size"] + who * part
                    value = tn(source[:, first : first + part], dh[...])

                    @pl.when(core == who)
                    def keep(block=block, value=value):
                        piece.acc[block] = value

                    @pl.when(core != who)
                    def give(block=block, value=value):
                        piece.outgoing[0][block] = value.astype(BF)

            piece.start()
        active.append(piece)

    def finished(piece):
        index = pieces.index(piece)
        size, part = piece.plan["size"], piece.plan["part"]
        mom_loads[index].wait()
        conv = piece.plan["conv"]
        if part == 0:
            total, to = s_totals[conv], (s2_ref, s1_ref)[conv]
            while total in active:
                do(total)
            high, low = halves_of(s_total[conv])
            first = jnp.where(first_row, high.astype(F32), 0.0)
            to[...] = jnp.where(two_rows, jnp.where(first_row, first, low.astype(F32)), 0.0).astype(BF)
        rows_at = slice(part * size, part * size + size)
        back = tn((m2_ref, m1_ref)[conv][:, rows_at], (s2_ref, s1_ref)[conv][...])
        grams[conv].add(0.5 * mom_ref[index % 2, 0:size, :] + (fulls[conv][rows_at, :].astype(F32) + back))
        clock.work(size * 0.002)
        if index + 2 < len(pieces):
            mom_loads[index + 2].start()
        later = [p for p in pieces[index + 1 :] if p.plan["conv"] == conv]
        if not later:
            grams[conv].start()
            active.append(grams[conv])

    def do(item):
        if item.advance():
            return
        active.remove(item)
        if isinstance(item, (Factors, Total)):
            return
        if isinstance(item, Piece):
            waiting.append(item)
            while len(added) < len(pieces) and pieces[len(added)] in waiting:
                added.append(pieces[len(added)])
                finished(added[-1])
        else:
            turns.extend((item, turn) for turn in range(TURNS))

    added = []

    def serve():
        while True:
            due = [k for k in active if k.ready <= clock.now]
            if not due:
                return
            do(min(due, key=lambda k: k.ready))

    def work_turn():
        item, turn = turns.pop(0)
        out = q2_ref if item is grams[0] else q1_ref
        newton_turn(turn, item.g, out)
        if turn == TURNS - 1:
            out[...] = out[...] / item.scale
        clock.work(3.0)

    for piece in pieces:
        if piece.plan["conv"] == 0:
            gradient(piece, patches)
            serve()

    for k in range(9):
        dy, dx = divmod(k, 3)
        piece = dpad[2 - dy : 2 - dy + SIDE, (2 - dx) * images : (2 - dx) * images + line, :]
        part = nt(piece.reshape(rows, mid), w2b[k * mid : (k + 1) * mid, :])
        da1[...] = part if k == 0 else da1[...] + part
        clock.work(0.65)
        if k % 3 == 2:
            serve()

    def back1(pixel, row, carry):
        h = h1_ref[pl.ds(row, images), :]
        v = h * scale1 + move1
        sig = sigmoid(v)
        dy = da1[pl.ds(row, images), :] * sig * (1.0 + v * (1.0 - sig))
        da1[pl.ds(row, images), :] = dy
        return carry[0] + dy, carry[1] + dy * ((h - mean1) * inv1)

    one, two = over_pixels(back1, (zero, zero), images)
    clock.work(2.0)
    serve()
    sums = jnp.concatenate([fold(one), fold(two)], axis=0)

    def meanwhile():
        clock.work(3.0)
        serve()
        clock.work(2.0)

    total = sum_over_all(place, sums, pair_buf, chip_buf, sum_sem, meanwhile)
    sums_ref[...] = total
    shift1, gain1 = total[0:1] / count, total[1:2] / count

    def finish1(pixel, row, carry):
        h = h1_ref[pl.ds(row, images), :]
        dy = da1[pl.ds(row, images), :]
        put = (scale1 * (dy - shift1 - (h - mean1) * inv1 * gain1)).astype(BF)
        dh[pl.ds(row, images), :] = put
        return carry + put.astype(F32)

    offset(over_pixels(finish1, zero, images), s_totals[1])
    active.append(s_totals[1])
    x_load.wait()
    for piece in pieces:
        if piece.plan["conv"] == 1:
            gradient(piece, x_ref)
            serve()

    while active or turns:
        due = min(active, key=lambda k: k.ready) if active else None
        if due is not None and (not turns or due.ready <= clock.now + 1.0):
            clock.now = max(clock.now, due.ready)
            do(due)
        else:
            work_turn()
    for piece in pieces:
        piece.drain()
    for item in [*grams, factors, head_total, *s_totals]:
        item.drain()


def run_b(n_dp, n_rep, x, mom1, mom2, h1, h2, pad, w2b, stat, dpool, norm, x_mean, factor, head_sums):
    rows, mid = h1.shape
    half1, half2 = mom1.shape[0], mom2.shape[0]
    chips = n_dp // 2 * n_rep
    shape = jax.ShapeDtypeStruct
    vmem, hbm = pl.BlockSpec(memory_space=pltpu.VMEM), pl.BlockSpec(memory_space=pl.ANY)
    scratch = []
    plans = plan_pieces(
        n_dp, n_rep, [(half2, 3, ("rep", "rep", "dp")), (half1, 2, ("dp", "dp"))], mid, scratch
    )
    biggest = max(plan["size"] for plan in plans)
    block = mid // 4
    return pl.pallas_call(
        functools.partial(kernel_b, n_dp, n_rep, plans),
        out_shape=(
            shape((half1, mid), BF), shape((half2, mid), BF),
            shape((mid, mid), F32), shape((mid, mid), F32), shape((2, mid), F32),
            shape((16, half1), BF), shape((16, half2), BF), shape((16, mid), BF), shape((16, mid), BF),
            shape((n_dp * n_rep,) + factor.shape, BF), shape(head_sums.shape, F32),
        ),
        in_specs=[hbm] * 3 + [vmem] * 10,
        out_specs=[vmem] * 9 + [hbm, vmem],
        scratch_shapes=[
            pltpu.VMEM((rows + 16, x.shape[1]), BF), pltpu.VMEM((2, biggest, mid), F32), pltpu.VMEM((rows, mid), F32),
            pltpu.VMEM(pad.shape, BF), pltpu.VMEM((rows + 16, mid), BF), pltpu.VMEM((rows + 16, 9 * mid), BF),
            pltpu.VMEM((mid, mid), F32), pltpu.VMEM((mid, mid), F32), pltpu.VMEM((mid, mid), F32),
            pltpu.VMEM((2, n_rep.bit_length() + 1, 2, block, 5 * block), F32),
            pltpu.VMEM((2, 2, mid), F32), pltpu.VMEM((chips, 2, mid), F32),
            pltpu.VMEM((2, 1, mid), F32), pltpu.VMEM((2, 2, 1, mid), F32), pltpu.VMEM((2, chips, 1, mid), F32),
            pltpu.VMEM((2,) + head_sums.shape, F32), pltpu.VMEM((chips,) + head_sums.shape, F32),
            DMA, DMA((len(plans),)), DMA((4,)), DMA((2, n_rep.bit_length(), 2)), DMA((2, 4)), DMA((4,)),
            DMA(((n_dp * n_rep).bit_length(), 2)),
        ] + scratch,
        compiler_params=pltpu.CompilerParams(
            collective_id=2, has_side_effects=True, vmem_limit_bytes=62 * 2**20
        ),
        name="backward",
    )(x, mom1, mom2, h1, h2, pad, w2b, stat, dpool, norm, x_mean, factor, head_sums)


def kernel_c(grad, mean, share, mom, weight, mask, q_ref, new_ref, mom_ref):
    q = halves_of(q_ref[...])
    value = 0.5 * mom[...] + (grad[...].astype(F32) + tn(mean[...], share[...]))
    mom_ref[...] = value
    new_ref[...] = (weight[...] - 1.0 * mm(halves_of(value), q)) * mask[...].astype(F32)


def run_c(grad, mean, share, mom, weight, mask, q):
    rows, mid = mom.shape
    size = next((k for k in (256, 128) if rows % k == 0), rows)
    shape = jax.ShapeDtypeStruct
    tile = pl.BlockSpec((size, mid), lambda i: (i, 0))
    return pl.pallas_call(
        kernel_c,
        grid=(rows // size,),
        out_shape=(shape((rows, mid), F32), shape((rows, mid), F32)),
        in_specs=[
            tile, pl.BlockSpec((16, size), lambda i: (0, i)), pl.BlockSpec((16, mid), lambda i: (0, 0)), tile, tile, tile,
            pl.BlockSpec((mid, mid), lambda i: (0, 0)),
        ],
        out_specs=[tile] * 2,
        compiler_params=pltpu.CompilerParams(vmem_limit_bytes=40 * 2**20),
        name="update",
    )(grad, mean, share, mom, weight, mask, q)


def adam_update(weight, first, second, grad, rate):
    first = 0.9 * first + 0.1 * grad
    second = 0.999 * second + 0.001 * grad * grad
    mhat = first / (1.0 - 0.9**STEP)
    vhat = second / (1.0 - 0.999**STEP)
    return (weight - rate * (mhat / (jnp.sqrt(vhat) + 1e-08) + 0.01 * weight), first, second)


def kernel_d(n_rep, factors, head_sums, sums, stat, weight, first, second, bias, bias_m, bias_v, norm, norm_m, norm_v,
             loss_out, weight_out, first_out, second_out, bias_out, bias_m_out, bias_v_out,
             norm_out, norm_m_out, norm_a_out, norm_b_out, share):
    classes, part = weight.shape
    mid = sums.shape[1]
    wide = factors.shape[2] - mid
    images = factors.shape[0] * factors.shape[1]
    every = factors[...].reshape(images, wide + mid)
    rep = lax.axis_index("rep")
    for block in range(n_rep):

        @pl.when(rep == block)
        def own(block=block):
            share[...] = every[:, wide + block * part : wide + (block + 1) * part]

    grad = tn(every[:, 0:wide], share[...])[0:classes]
    weight_out[...], first_out[...], second_out[...] = adam_update(weight[...], first[...], second[...], grad, 0.03)
    loss_out[...] = head_sums[wide // mid :, 0:1]
    for k in range(wide // mid):
        at = (slice(None), slice(k * mid, min((k + 1) * mid, classes)))
        grad = head_sums[k : k + 1, 0 : min(mid, classes - k * mid)]
        bias_out[at], bias_m_out[at], bias_v_out[at] = adam_update(bias[at], bias_m[at], bias_v[at], grad, 0.2)
    shifts = (sums[0:1], stat[4:5])
    gains = (sums[1:2], stat[5:6])
    for k, out in enumerate((norm_a_out, norm_b_out)):
        for j, grad in enumerate((gains[k], shifts[k])):
            at = (k, slice(j, j + 1))
            norm_out[at], norm_m_out[at], out[j : j + 1, :] = adam_update(norm[at], norm_m[at], norm_v[at], grad, 0.2)


def run_d(n_rep, *args):
    factors, sums, weight, bias, norm = args[0], args[2], args[4], args[7], args[10]
    shape = jax.ShapeDtypeStruct
    classes, part = weight.shape
    mid = sums.shape[1]
    vmem = pl.BlockSpec(memory_space=pltpu.VMEM)
    outs = [(1, 1)] + [weight.shape] * 3 + [bias.shape] * 3 + [norm.shape] * 2 + [norm.shape[1:]] * 2
    return pl.pallas_call(
        functools.partial(kernel_d, n_rep),
        out_shape=tuple(shape(s, F32) for s in outs),
        in_specs=[vmem] * len(args),
        out_specs=[vmem] * len(outs),
        scratch_shapes=[pltpu.VMEM((factors.shape[0] * factors.shape[1], part), BF)],
        compiler_params=pltpu.CompilerParams(vmem_limit_bytes=40 * 2**20),
        name="small_updates",
    )(*args)


def local(
    images,
    labels,
    conv1,
    conv2,
    classifier,
    class_bias,
    batchnorm_parameters,
    conv1_mom,
    conv2_mom,
    class_m,
    class_v,
    bias_m,
    bias_v,
    norm_m,
    norm_v,
    conv1_live,
    conv2_live,
    conv1_next,
    conv2_next,
):
    count, c_in = images.shape[0], images.shape[3]
    c_mid = conv1.shape[1]
    n_dp, n_rep = lax.axis_size("dp"), lax.axis_size("rep")
    x = images.transpose(1, 2, 0, 3).reshape(SIDE * SIDE * count, c_in)
    norm = batchnorm_parameters
    h1, h2, pad, w2b, stat, factor, head_sums, dpool, x_mean = run_a(
        n_dp, n_rep, x, conv1, conv2, classifier.T, conv1_live, conv2_live, class_bias.reshape(1, -1), norm, labels
    )
    g_one, g_two, q_one, q_two, sums, m_one, m_two, s_one, s_two, factors, head_sums = run_b(
        n_dp, n_rep, x, conv1_mom, conv2_mom, h1, h2, pad, w2b.reshape(-1, c_mid), stat, dpool, norm,
        x_mean, factor, head_sums,
    )
    conv1_new, mom_one = run_c(g_one, m_one, s_one, conv1_mom, conv1, conv1_next, q_one)
    conv2_new, mom_two = run_c(g_two, m_two, s_two, conv2_mom, conv2, conv2_next, q_two)
    loss, head_new, head_m, head_v, bias_new, first_b, second_b, norm_new, first_n, norm_a, norm_b = run_d(
        n_rep, factors, head_sums, sums, stat, classifier.T, class_m.T, class_v.T,
        class_bias.reshape(1, -1), bias_m.reshape(1, -1), bias_v.reshape(1, -1), norm, norm_m, norm_v,
    )
    return (
        loss[0, 0],
        conv1_new,
        conv2_new,
        head_new.T,
        bias_new[0],
        norm_new,
        mom_one,
        mom_two,
        head_m.T,
        head_v.T,
        first_b[0],
        second_b[0],
        first_n,
        norm_a,
        norm_b,
    )


def solution(mesh):
    placed = (
        P(("dp", "rep"), None, None, None),
        P(("dp", "rep")),
        P("rep", None),
        P("rep", None),
        P("rep", None),
        P(),
        P(),
        P("rep", None),
        P("rep", None),
        P("rep", None),
        P("rep", None),
        P(),
        P(),
        P(),
        P(),
        P("rep", None),
        P("rep", None),
        P("rep", None),
        P("rep", None),
    )
    return jax.shard_map(
        local,
        mesh=mesh,
        in_specs=placed,
        out_specs=(
            P(),
            P("rep", None),
            P("rep", None),
            P("rep", None),
            P(),
            P(),
            P("rep", None),
            P("rep", None),
            P("rep", None),
            P("rep", None),
            P(),
            P(),
            P(),
            P(),
            P(),
        ),
        check_vma=False,
    )
```

```python
import contextlib
import functools

import jax
import jax.numpy as jnp
from jax import lax
from jax.experimental import pallas as pl
from jax.experimental.pallas import tpu as pltpu
from jax.sharding import PartitionSpec as P

SIDE = 7
TURNS = 5
STEP = 5
NORM_EPS = 1e-05
COEF_A = 3.4445
COEF_B = -4.775
COEF_C = 2.0315
MESH = pl.DeviceIdType.MESH
BF = jnp.bfloat16
F32 = jnp.float32
DMA = pltpu.SemaphoreType.DMA


def scope(name):
    return contextlib.nullcontext()


def nn(a, b):
    return jnp.dot(a, b, preferred_element_type=F32)


def nt(a, b):
    return lax.dot_general(a, b, (((1,), (1,)), ((), ())), preferred_element_type=F32)


def tn(a, b):
    return lax.dot_general(a, b, (((0,), (0,)), ((), ())), preferred_element_type=F32)


def sigmoid(v):
    return 1.0 / (1.0 + jnp.exp(-v))


class Place:
    def __init__(self, n_dp, n_rep):
        self.n_dp, self.n_rep = n_dp, n_rep
        self.chips = n_dp // 2 * n_rep
        self.dp, self.rep = lax.axis_index("dp"), lax.axis_index("rep")
        self.core = lax.rem(self.dp, 2)
        self.chip = self.dp // 2 * n_rep + self.rep

    def flip(self, bit):
        half = 1 << bit
        set_now = lax.rem(self.dp // half, 2)
        return {"dp": self.dp + half - 2 * half * set_now, "rep": self.rep}

    def flip_rep(self, bit):
        half = 1 << bit
        set_now = lax.rem(self.rep // half, 2)
        return {"dp": self.dp, "rep": self.rep + half - 2 * half * set_now}

    def other_chip(self, step):
        to = lax.rem(self.chip + step, self.chips)
        return {"dp": to // self.n_rep * 2 + self.core, "rep": lax.rem(to, self.n_rep)}

    def other_rep(self, step):
        return {"dp": self.dp, "rep": lax.rem(self.rep + step, self.n_rep)}


def send(src, dst, send_sem, recv_sem, to):
    copy = pltpu.make_async_remote_copy(src, dst, send_sem, recv_sem, to, MESH)
    copy.start()


def wait_bytes(ref, sem):
    with scope("wait"):
        pltpu.make_async_copy(ref, ref, sem).wait()


def greet(place):
    barrier = pltpu.get_barrier_semaphore()

    def one(step, carry):
        pl.semaphore_signal(barrier, 1, device_id=place.other_chip(step), device_id_type=MESH)
        return carry

    lax.fori_loop(1, place.chips, one, 0)
    pl.semaphore_signal(barrier, 1, device_id=place.flip(0), device_id_type=MESH)


def met(place):
    pl.semaphore_wait(pltpu.get_barrier_semaphore(), place.chips)


def sum_over_all(place, value, pair_buf, chip_buf, sems, meanwhile=None):
    pair_buf[place.core] = value
    mine = pair_buf.at[place.core]
    send(mine, mine, sems.at[0], sems.at[1], place.flip(0))
    wait_bytes(mine, sems.at[1])
    chip_buf[place.chip] = pair_buf[0] + pair_buf[1]
    block = chip_buf.at[place.chip]

    def one(step, carry):
        send(block, block, sems.at[2], sems.at[3], place.other_chip(step))
        return carry

    lax.fori_loop(1, place.chips, one, 0)
    if meanwhile is not None:
        meanwhile()
    wait_bytes(chip_buf.at[pl.ds(0, place.chips - 1)], sems.at[3])
    total = jnp.sum(chip_buf[...], axis=0)
    wait_bytes(mine, sems.at[0])
    wait_bytes(chip_buf.at[pl.ds(0, place.chips - 1)], sems.at[2])
    return total


class Total:
    def __init__(self, place, clock, pair_buf, chip_buf, sems, out):
        self.place, self.clock, self.pair, self.chip, self.sems, self.out = place, clock, pair_buf, chip_buf, sems, out
        self.step, self.ready = 0, None

    def start(self, value):
        self.pair[self.place.core] = value
        mine = self.pair.at[self.place.core]
        send(mine, mine, self.sems.at[0], self.sems.at[1], self.place.flip(0))
        self.ready = self.clock.carry("core", 2)

    def others(self):
        return self.chip.at[pl.ds(0, self.place.chips - 1)]

    def advance(self):
        place = self.place
        if self.step == 0:
            wait_bytes(self.pair.at[0], self.sems.at[1])
            self.chip[place.chip] = self.pair[0] + self.pair[1]
            block = self.chip.at[place.chip]

            def one(step, carry):
                send(block, block, self.sems.at[2], self.sems.at[3], place.other_chip(step))
                return carry

            lax.fori_loop(1, place.chips, one, 0)
            self.clock.work(0.8)
            self.ready = self.clock.now + 3.5
            self.step = 1
            return True
        wait_bytes(self.others(), self.sems.at[3])
        self.out[...] = jnp.sum(self.chip[...], axis=0)
        self.step = 2
        return False

    def drain(self):
        wait_bytes(self.pair.at[0], self.sems.at[0])
        wait_bytes(self.others(), self.sems.at[2])


class Clock:
    RATES = {"core": (550.0, 1.0), "far": (23.0, 2.8)}

    def __init__(self):
        self.now = 0.0
        self.free, self.flying, self.queued = {}, {}, {}

    def work(self, span):
        self.now += span

    def carry(self, link, kilobytes, earliest=0.0):
        rate, hop = self.RATES.get(link, (46.0, 2.1))
        begin = max(self.now, earliest, self.free.get(link, 0.0))
        self.free[link] = begin + kilobytes / rate
        return self.free[link] + hop

    def launch(self, item):
        self.flying.setdefault(item.link, []).append(item)
        item.owner.ready = self.carry(item.link, item.kilobytes)
        for src, dst in item.pairs:
            send(src, dst, item.sems.at[0], item.sems.at[1], item.to)

    def ship(self, owner, link, pairs, size, sems, to, kilobytes):
        item = Transfer(owner, link, pairs, size, sems, to, kilobytes)
        owner.ready = float("inf")
        if link == "core" or not self.flying.get(link):
            self.launch(item)
        else:
            self.queued.setdefault(link, []).append(item)
        return item

    def receive(self, item):
        rate, hop = self.RATES.get(item.link, (46.0, 2.1))
        self.now = max(self.now, item.owner.ready - hop)
        wait_bytes(item.size, item.sems.at[0])
        self.flying[item.link].remove(item)
        queue = self.queued.get(item.link, [])
        if queue and item.link != "core":
            first = min(queue, key=lambda k: k.owner.rank)
            queue.remove(first)
            self.launch(first)
        self.now = max(self.now, item.owner.ready)
        wait_bytes(item.size, item.sems.at[1])


class Transfer:
    def __init__(self, owner, link, pairs, size, sems, to, kilobytes):
        self.owner, self.link, self.pairs, self.size, self.sems, self.to = owner, link, pairs, size, sems, to
        self.kilobytes = kilobytes


class Gather:
    def __init__(self, place, buf, pieces, sems):
        self.place, self.buf, self.pieces, self.sems = place, buf, pieces, sems
        self.quarter = buf.shape[1] // 4
        self.rows = self.quarter // pieces
        self.y = lax.rem(place.dp // 2, 2)

    def at(self, block, y, piece):
        first = self.place.core * (2 * self.quarter) + y * self.quarter + piece * self.rows
        return self.buf.at[block, pl.ds(pl.multiple_of(first, 16), self.rows)]

    def blocks(self):
        return [lax.rem(self.place.rep + step, self.place.n_rep) for step in range(1, self.place.n_rep)]

    def size(self):
        return self.buf.at[pl.ds(0, self.place.n_rep - 1), pl.ds(0, self.rows)]

    def start(self, piece):
        mine = self.at(self.place.rep, self.y, piece)
        for step in range(1, self.place.n_rep):
            send(mine, mine, self.sems.at[0, piece, 0], self.sems.at[0, piece, 1], self.place.other_rep(step))

    def hop_y(self, piece):
        wait_bytes(self.size(), self.sems.at[0, piece, 1])
        for block in self.blocks():
            here = self.at(block, self.y, piece)
            send(here, here, self.sems.at[1, piece, 0], self.sems.at[1, piece, 1], self.place.flip(1))
            send(here, here, self.sems.at[2, piece, 0], self.sems.at[2, piece, 1], self.place.flip(0))

    def hop_core(self, piece):
        wait_bytes(self.size(), self.sems.at[1, piece, 1])
        for block in self.blocks():
            here = self.at(block, 1 - self.y, piece)
            send(here, here, self.sems.at[3, piece, 0], self.sems.at[3, piece, 1], self.place.flip(0))

    def finish(self, piece):
        wait_bytes(self.size(), self.sems.at[2, piece, 1])
        wait_bytes(self.size(), self.sems.at[3, piece, 1])

    def drain(self):
        for piece in range(self.pieces):
            for hop in range(4):
                wait_bytes(self.size(), self.sems.at[hop, piece, 0])


def norm_of(total, count):
    mean = total[0:1] / count
    return mean, lax.rsqrt(total[1:2] / count - mean * mean + NORM_EPS)


def over_pixels(step, init, images):
    def body(pixel, carry):
        return step(pixel, pl.multiple_of(pixel * images, 16), carry)

    return lax.fori_loop(0, SIDE * SIDE, body, init, unroll=7)


def fold(acc):
    return jnp.sum(acc, axis=0, keepdims=True)


def sums_of(h_ref, images):
    chans = h_ref.shape[1]

    def step(pixel, row, carry):
        v = h_ref[pl.ds(row, images), :]
        return carry[0] + v, carry[1] + v * v

    zero = jnp.zeros((images, chans), F32)
    one, two = over_pixels(step, (zero, zero), images)
    return jnp.concatenate([fold(one), fold(two)], axis=0)


def put_padded(pad_ref, pixel, value, images):
    y, x = pixel // SIDE, lax.rem(pixel, SIDE)
    pad_ref[1 + y, pl.ds(pl.multiple_of((1 + x) * images, 16), images), :] = value


def clear_border(pad_ref, images):
    line = SIDE * images
    pad_ref[0] = jnp.zeros(pad_ref.shape[1:], pad_ref.dtype)
    pad_ref[SIDE + 1] = jnp.zeros(pad_ref.shape[1:], pad_ref.dtype)
    edge = jnp.zeros((SIDE, images, pad_ref.shape[2]), pad_ref.dtype)
    pad_ref[1 : SIDE + 1, 0:images, :] = edge
    pad_ref[1 : SIDE + 1, images + line : 2 * images + line, :] = edge


def build_patches(pad_ref, to_ref):
    images, chans = pad_ref.shape[1] // (SIDE + 2), pad_ref.shape[2]
    line = SIDE * images
    for k in range(9):
        dy, dx = divmod(k, 3)
        piece = pad_ref[dy : dy + SIDE, dx * images : dx * images + line, :]
        to_ref[0 : SIDE * line, k * chans : (k + 1) * chans] = piece.reshape(SIDE * line, chans)


class Factors:
    rank = 20

    def __init__(self, place, clock, buf, sems):
        self.place, self.clock, self.buf, self.sems = place, clock, buf, sems
        reps = [("rep", b) for b in range(place.n_rep.bit_length() - 1)]
        dps = [("dp", b) for b in reversed(range(1, place.n_dp.bit_length() - 1)) if b != 2]
        self.order = reps + dps + [("dp", 2), ("dp", 0)]
        self.index = 0
        for k, (axis, bit) in enumerate(self.order):
            self.index = self.index + (1 << k) * lax.rem((place.rep if axis == "rep" else place.dp) // (1 << bit), 2)
        self.step, self.chunk, self.ready = 0, 0, None

    @staticmethod
    def chunks(level, last):
        return 1 if last else max(1, (1 << level) // 2)

    def start(self, value_ref):
        load = pltpu.make_async_copy(value_ref, self.buf.at[self.index], self.sems.at[len(self.order), 0, 0])
        load.start()
        load.wait()
        self.ship()

    def ship(self):
        held = 1 << self.step
        size = held // self.chunks(self.step, self.step + 1 == len(self.order))
        mine = self.buf.at[pl.ds(self.index // held * held + self.chunk * size, size)]
        axis, bit = self.order[self.step]
        to = self.place.flip_rep(bit) if axis == "rep" else self.place.flip(bit)
        link = "x" if axis == "rep" else {0: "core", 1: "y", 2: "z"}.get(bit, "far")
        kilobytes = size * self.buf.shape[1] * self.buf.shape[2] * 2 / 1024
        sems = self.sems.at[self.step, self.chunk]
        self.item = self.clock.ship(self, link, [(mine, mine)], mine, sems, to, kilobytes)

    def advance(self):
        self.clock.receive(self.item)
        self.chunk += 1
        if self.chunk == self.chunks(self.step, self.step + 1 == len(self.order)):
            self.step, self.chunk = self.step + 1, 0
        if self.step == len(self.order):
            return False
        self.ship()
        return True


class Piece:
    def __init__(self, plan, place, clock, full, sums, weights, refs):
        self.plan, self.place, self.clock, self.full = plan, place, clock, full
        self.r0, self.nr, self.q0, self.nq = 0, place.n_rep, 0, plan["size"] // 2
        self.acc, wide, self.whole = sums, weights, self.nq
        self.first = plan["part"] * place.n_rep * self.nq
        low, middle = plan["part"] * self.nq, plan["half"] // 2
        self.outgoing = [wide.at[:, pl.ds(low, self.nq)]] + [refs[k] for k in plan["outgoing"]]
        self.incoming = [wide.at[:, pl.ds(middle + low, self.nq)]] + [refs[k] for k in plan["incoming"]]
        self.sems = refs[plan["sems"]]
        self.step, self.ready = 0, None
        self.rank = 10 * plan["conv"] + plan["part"]
        self.base = plan["part"] * plan["size"] + place.core * self.nq

    def bit(self, level):
        axis, bit = level["axis"], level["bit"]
        return lax.rem((self.place.rep if axis == "rep" else self.place.dp) // (1 << bit), 2)

    def partner(self, level):
        return self.place.flip_rep(level["bit"]) if level["axis"] == "rep" else self.place.flip(level["bit"])

    def part(self, block, q0, nq):
        return pl.ds(pl.multiple_of(self.first + block * self.whole + q0, 16), nq)

    def ship(self, pairs, size, slot, to, link, kilobytes):
        self.item = self.clock.ship(self, link, pairs, size, self.sems.at[slot], to, kilobytes)

    def start(self):
        size = self.place.n_rep * self.nq
        pairs = [(self.outgoing[0], self.incoming[0])]
        self.ship(pairs, self.outgoing[0], 0, self.place.flip(0), "core", size)

    def advance(self):
        with scope("piece%d%d_step%d" % (self.plan["conv"], self.plan["part"], self.step)):
            return self.move()

    def move(self):
        levels = self.plan["levels"]
        self.clock.receive(self.item)
        if self.step <= len(levels):
            for k in range(self.nr):
                at = self.part(self.r0 + k, self.q0, self.nq)
                self.acc[at, :] = self.acc[at, :] + self.incoming[self.step][k].astype(F32)
            self.clock.work(0.2)
        if self.step < len(levels):
            self.begin(levels[self.step])
            self.step += 1
            return True
        back = self.plan["back"]
        done = self.step - len(levels)
        self.step += 1
        if done == 0:
            self.full[self.rows(self.q0, self.nq), :] = self.acc[self.part(self.r0, self.q0, self.nq), :].astype(BF)
            self.held = [(self.q0, self.nq)]
        elif done <= len(back):
            level = back[done - 1]
            bit, apart = self.bit(level), level["rows"]
            if self.held[0][1] == apart:
                self.held = [(first - bit * apart, 2 * apart) for first, _ in self.held]
            else:
                self.held = [(at, n) for first, n in self.held for at in (first, first + (1 - 2 * bit) * apart)]
        else:
            return False
        if done < len(back):
            to, link = self.partner(back[done]), back[done]["link"]
        else:
            to, link, self.held = self.place.flip(0), "core", [(0, self.whole)]
        refs = [self.full.at[self.rows(first, n)] for first, n in self.held]
        size = sum(n for _, n in self.held)
        self.ship([(r, r) for r in refs], self.full.at[pl.ds(0, size)], self.step, to, link, size)
        return True

    def rows(self, q0, nq):
        return pl.ds(pl.multiple_of(self.base + q0, 16), nq)

    def begin(self, level):
        bit = self.bit(level)
        out = self.outgoing[self.step + 1]
        if level["halve"]:
            r1, q1 = self.r0, self.q0
            if level["axis"] == "rep":
                self.nr //= 2
                self.r0, r1 = self.r0 + bit * self.nr, self.r0 + (1 - bit) * self.nr
            else:
                self.nq //= 2
                self.q0, q1 = self.q0 + bit * self.nq, self.q0 + (1 - bit) * self.nq
            for k in range(self.nr):
                out[k] = self.acc[self.part(r1 + k, q1, self.nq), :].astype(BF)
        else:
            for k in range(self.nr):
                at = self.part(self.r0 + k, self.q0, self.nq)
                out[k] = self.acc[at, :].astype(BF)
                self.acc[at, :] = out[k].astype(F32)
        pairs = [(out, self.incoming[self.step + 1])]
        self.ship(pairs, out, self.step + 1, self.partner(level), level["link"], self.nr * self.nq)


def plan_pieces(n_dp, n_rep, halves, mid, scratch):
    plans = []
    for conv, (half, parts, firsts, backs) in enumerate(halves):
        fits = half % (parts * 16 * n_dp) == 0 and half // parts // 2 % 128 == 0
        if not fits:
            parts = 1
        for part in range(parts):
            size = half // parts
            reps = [("rep", b) for b in reversed(range(n_rep.bit_length() - 1))]
            dps = [("dp", b) for b in range(1, n_dp.bit_length() - 1)]
            order = reps + dps if firsts[part] == "rep" else dps[:1] + reps + dps[1:]
            nr, nq, levels, shapes = n_rep, size // 2, [], []
            for axis, bit in order:
                halve = axis == "rep" or nq // 2 % 16 == 0
                if halve and axis == "rep":
                    nr //= 2
                elif halve:
                    nq //= 2
                link = "x" if axis == "rep" else {1: "y", 2: "z"}.get(bit, "far")
                levels.append({"axis": axis, "bit": bit, "halve": halve, "link": link, "rows": nq})
                shapes.append((nr, nq, mid))
            plan = {"conv": conv, "part": part, "size": size, "half": half, "levels": levels, "fits": fits}
            back = [k for k in reversed(levels) if k["axis"] == "dp" and k["halve"]]
            plan["back"] = sorted(back, key=lambda k: k["bit"] != 1) if backs[part] == "early" else back

            def add(spec):
                scratch.append(spec)
                return len(scratch) - 1

            plan["outgoing"] = [add(pltpu.VMEM(s, BF)) for s in shapes]
            plan["incoming"] = [add(pltpu.VMEM(s, BF)) for s in shapes]
            plan["sems"] = add(DMA((2 * len(levels) + 2, 2)))
            plans.append(plan)
    return plans


def halves_of(v):
    high = v.astype(BF)
    return high, (v - high.astype(F32)).astype(BF)


def mm(a, b):
    return nn(a[0], b[0]) + (nn(a[0], b[1]) + nn(a[1], b[0]))


def square(a):
    cross = nn(a[0], a[1])
    return nn(a[0], a[0]) + (cross + cross.T)


def unit(n):
    return lax.broadcasted_iota(jnp.int32, (n, n), 0) == lax.broadcasted_iota(jnp.int32, (n, n), 1)


def newton_turn(turn, g_ref, q_ref):
    n = g_ref.shape[0]
    gram = halves_of(g_ref[...])
    factor = COEF_A * unit(n).astype(F32) + COEF_B * g_ref[...] + COEF_C * square(gram)
    factors = halves_of(factor)
    if turn == 0:
        q_ref[...] = factor
    else:
        q_ref[...] = mm(halves_of(q_ref[...]), factors)
    if turn < TURNS - 1:
        g_ref[...] = mm(halves_of(mm(gram, factors)), factors)


class Gram:
    def __init__(self, place, clock, g_ref, cross_ref, packed, total, sems):
        self.place, self.clock, self.g, self.cross, self.sems = place, clock, g_ref, cross_ref, sems
        self.packed, self.total = packed, total
        self.fresh, self.rank = True, -1
        self.step, self.ready = 0, None
        self.b, self.levels = g_ref.shape[0] // 4, place.n_rep.bit_length() - 1

    def add(self, value):
        high, low = halves_of(value)
        if self.fresh:
            self.g[...] = tn(high, high)
            self.cross[...] = tn(high, low)
        else:
            self.g[...] += tn(high, high)
            self.cross[...] += tn(high, low)
        self.fresh = False

    def start(self):
        b = self.b
        g = self.g[...] + self.cross[...] + self.cross[...].T
        to = self.packed
        one = jnp.concatenate([g[0:b, :], g[3 * b :, 3 * b :]], axis=1)
        two = jnp.concatenate([g[b : 2 * b, b:], g[2 * b : 3 * b, 2 * b :]], axis=1)
        to[0] = jnp.where(self.place.core == 0, one, two)
        self.clock.work(1.5)
        self.ship()

    def ship(self):
        mine, theirs = self.packed.at[0], self.packed.at[self.step + 1]
        self.item = self.clock.ship(
            self, "x", [(mine, theirs)], mine, self.sems.at[self.step], self.place.flip_rep(self.step), 5 * self.b * self.b * 4 / 1024
        )

    def advance(self):
        place, to, levels = self.place, self.packed, self.levels
        if self.step < levels:
            self.clock.receive(self.item)
            last = self.step + 1 == levels
            value = to[0] + to[self.step + 1]
            self.step += 1
            if not last:
                to[0] = value
                self.ship()
                return True
            self.total[place.core] = value
            mine = self.total.at[place.core]
            self.item = self.clock.ship(self, "core", [(mine, mine)], mine, self.sems.at[levels], place.flip(0), 330)
            return True
        self.clock.receive(self.item)
        b, to = self.b, self.total
        g = self.g
        g[0:b, :] = to[0, :, 0 : 4 * b]
        g[3 * b :, 3 * b :] = to[0, :, 4 * b :]
        g[b : 2 * b, b:] = to[1, :, 0 : 3 * b]
        g[2 * b : 3 * b, 2 * b :] = to[1, :, 3 * b :]
        for i in range(1, 4):
            for j in range(i):
                g[i * b : (i + 1) * b, j * b : (j + 1) * b] = g[j * b : (j + 1) * b, i * b : (i + 1) * b].T
        trace = jnp.sum(jnp.sum(jnp.where(unit(4 * b), g[...], 0.0), axis=0, keepdims=True), axis=1, keepdims=True)
        self.scale = jnp.sqrt(trace) + 1e-07
        g[...] = g[...] / (self.scale * self.scale)
        self.clock.work(1.0)
        return False


def kernel_step(n_dp, n_rep, plans, *refs):
    (x_hbm, w1_hbm, w2_hbm, head_hbm, live1_hbm, live2_hbm, mom1_hbm, mom2_hbm, bias_ref, norm_ref, label_ref,
     g1_ref, g2_ref, q1_ref, q2_ref, m1_ref, m2_ref, s1_ref, s2_ref, stat_ref, head_ref, factors_ref,
     x_ref, patches, h1_ref, h2_ref, da1, pad, dpad, dh, w1b, w2b, head_b, f1, f2, live, fh, bias_pad, factor,
     gram1, gram2, packed, gram_total, x_sum, s_total, dpool_ref,
     pair_buf, chip_buf, x_pair, x_chip, s_pair, s_chip, head_pair, head_chip,
     load_sem, w1_sem, w2_sem, head_sem, sum_sem, x_sem, mom_sem, gram_sem, s_sem, total_sem, factor_sem, q_sem) = refs[:66]
    refs = refs[66:]
    place, clock = Place(n_dp, n_rep), Clock()
    core, rep = place.core, place.rep
    half1, half2, mid = w1b.shape[1], w2b.shape[1], w1b.shape[2]
    classes, head_cols = fh.shape
    wide = head_b.shape[1]
    images = factor.shape[0]
    line = SIDE * images
    rows = SIDE * line
    all_images = images * n_dp * n_rep
    count = all_images * SIDE * SIDE
    parts = x_ref.shape[1] // mid
    zero = jnp.zeros((images, mid), F32)

    early = half2 - half1
    pairs = [
        (w1_hbm, f1.at[pl.ds(0, half1)]),
        (live1_hbm, live.at[pl.ds(early, half1)]),
        (w2_hbm, f2.at[pl.ds(0, half2)]),
        (live2_hbm.at[pl.ds(0, early)], live.at[pl.ds(0, early)]),
        (x_hbm, x_ref.at[pl.ds(0, rows)]),
        (head_hbm, fh),
        (live2_hbm.at[pl.ds(early, half1)], live.at[pl.ds(early, half1)]),
    ]
    loads = [pltpu.make_async_copy(a, b, load_sem.at[k]) for k, (a, b) in enumerate(pairs)]
    loads[0].start()
    loads[1].start()
    greet(place)
    g1, g2, gh = Gather(place, w1b, 4, w1_sem), Gather(place, w2b, 3, w2_sem), Gather(place, head_b, 1, head_sem)

    def mask(value, shift, to, first, size):
        at, at_live = pl.ds(pl.multiple_of(first, 16), size), pl.ds(pl.multiple_of(first + shift, 16), size)
        to[rep, at, :] = (value[at, :] * live[at_live, :].astype(F32)).astype(BF)

    def mask_quarters(gather, value, shift, to):
        mine = core * 2 + gather.y
        for other in range(1, 4):
            mask(value, shift, to, lax.rem(mine + other, 4) * gather.quarter, gather.quarter)

    def mask_piece(gather, value, shift, to, piece):
        mine = core * 2 + gather.y
        mask(value, shift, to, mine * gather.quarter + piece * gather.rows, gather.rows)

    loads[0].wait()
    loads[1].wait()
    for load in loads[2:6]:
        load.start()
    mask_piece(g1, f1, early, w1b, 0)
    met(place)
    g1.start(0)
    for piece in range(1, g1.pieces):
        mask_piece(g1, f1, early, w1b, piece)
        g1.start(piece)
    mask_quarters(g1, f1, early, w1b)
    loads[6].start()
    clear_border(pad, images)
    clear_border(dpad, images)
    bias_pad[:, 0:classes] = bias_ref[...]
    bias_pad[:, classes:] = jnp.zeros((1, wide - classes), F32)
    for k in (2, 3, 6):
        loads[k].wait()
    for piece in range(g2.pieces):
        mask_piece(g2, f2, 0, w2b, piece)
    mask_quarters(g2, f2, 0, w2b)
    loads[5].wait()
    head_b[rep, 0:classes, :] = fh[...].astype(BF)
    head_b[rep, classes:, :] = jnp.zeros((wide - classes, head_cols), BF)
    loads[4].wait()

    def cols(block, half):
        return pl.ds(pl.multiple_of(block * half, 128), half)

    h1_ref[...] = nn(x_ref[0:rows, cols(rep, half1)], w1b[rep])
    x_total = Total(place, Clock(), x_pair, x_chip, x_sem, x_sum)
    x_sums = nn(jnp.ones((8, rows), BF), x_ref[0:rows, :])
    x_total.start(jnp.concatenate([x_sums[0:1, k * mid : (k + 1) * mid] for k in range(parts)], axis=0))
    for piece in range(g1.pieces):
        g1.hop_y(piece)
        if piece == g1.pieces - 2:
            g2.start(0)
    for piece in range(g1.pieces):
        g1.hop_core(piece)
    g2.start(1)
    for piece in range(g1.pieces):
        g1.finish(piece)
    for block in g1.blocks():
        h1_ref[...] += nn(x_ref[0:rows, cols(block, half1)], w1b[block])
    g2.hop_y(0)
    g2.start(2)

    def during_first():
        gh.start(0)
        g2.hop_y(1)

    sums = sums_of(h1_ref, images)
    total = sum_over_all(
        place, jnp.concatenate([sums, sums[0:1]], axis=0), pair_buf.at[0], chip_buf.at[0], sum_sem.at[0], during_first
    )
    mean1, inv1 = norm_of(total, count)
    scale1 = norm_ref[0, 0:1] * inv1
    move1 = norm_ref[0, 1:2] - mean1 * scale1
    g2.hop_y(2)

    def act1(pixel, row, carry):
        v = h1_ref[pl.ds(row, images), :] * scale1 + move1
        act = v * sigmoid(v)
        put_padded(pad, pixel, act.astype(BF), images)
        return carry + act

    act_sums = over_pixels(act1, zero, images)
    x_total.advance()
    g2.hop_core(0)
    build_patches(pad, patches)
    g2.hop_core(1)

    def rest_of_weights():
        g2.hop_core(2)
        for piece in range(g2.pieces):
            g2.finish(piece)

    if half2 % 128:
        rest_of_weights()
        for block in range(n_rep):
            part = nn(patches[0:rows, block * half2 : (block + 1) * half2], w2b[block])
            h2_ref[...] = part if block == 0 else h2_ref[...] + part
    else:
        h2_ref[...] = nn(patches[0:rows, cols(rep, half2)], w2b[rep])
        rest_of_weights()
        for block in g2.blocks():
            h2_ref[...] += nn(patches[0:rows, cols(block, half2)], w2b[block])

    sums = jnp.concatenate([sums_of(h2_ref, images), fold(act_sums)], axis=0)
    gh.hop_y(0)
    total = sum_over_all(place, sums, pair_buf.at[1], chip_buf.at[1], sum_sem.at[1], lambda: gh.hop_core(0))
    act_mean = total[2:3] / count
    mean2, inv2 = norm_of(total, count)
    scale2 = norm_ref[1, 0:1] * inv2
    move2 = norm_ref[1, 1:2] - mean2 * scale2

    def pool(pixel, row, carry):
        v = h2_ref[pl.ds(row, images), :] * scale2 + move2
        return carry + v * sigmoid(v)

    factor[:, wide:] = (over_pixels(pool, zero, images) / (SIDE * SIDE)).astype(BF)
    gh.finish(0)
    logits = bias_pad[...]
    for block in range(n_rep):
        logits = logits + nt(factor[:, wide + block * head_cols : wide + (block + 1) * head_cols], head_b[block])
    column = lax.broadcasted_iota(jnp.int32, (images, wide), 1)
    shown = jnp.where(column < classes, logits, -jnp.inf)
    top = jnp.max(shown, axis=1, keepdims=True)
    lse = top + jnp.log(jnp.sum(jnp.exp(shown - top), axis=1, keepdims=True))
    image = lax.broadcasted_iota(jnp.int32, (images, wide), 0)
    label = jnp.zeros((images, wide), jnp.int32)
    for k in range(images):
        label = jnp.where(image == k, label_ref[k], label)
    hit = (column == label).astype(F32)
    target = jnp.sum(logits * hit, axis=1, keepdims=True)
    loss = jnp.sum(lse - target, axis=0, keepdims=True)
    grad = (jnp.exp(shown - lse) - hit) / all_images
    dz = grad.astype(BF)
    factor[:, 0:wide] = dz
    for block in range(n_rep):
        dpool_ref[:, block * head_cols : (block + 1) * head_cols] = nn(dz, head_b[block]) / (SIDE * SIDE)
    dpool = dpool_ref[...]

    def back2(row):
        h = h2_ref[pl.ds(row, images), :]
        v = h * scale2 + move2
        sig = sigmoid(v)
        return dpool * sig * (1.0 + v * (1.0 - sig)), (h - mean2) * inv2

    def back2_sums(pixel, row, carry):
        dy, unit_h = back2(row)
        return carry[0] + dy, carry[1] + dy * unit_h

    one, two = over_pixels(back2_sums, (zero, zero), images)
    sums = jnp.concatenate([fold(one), fold(two), fold(one)], axis=0)
    factors = Factors(place, clock, factors_ref, factor_sem)
    head_total = Total(place, clock, head_pair, head_chip, total_sem, head_ref)
    active = [factors, head_total]

    def during_third():
        factors.start(factor)
        bias_sums = jnp.sum(grad, axis=0, keepdims=True)
        pieces = [bias_sums[:, k * mid : (k + 1) * mid] for k in range(wide // mid)]
        head_total.start(jnp.concatenate([*pieces, jnp.broadcast_to(loss, (1, mid))], axis=0))
        x_total.advance()
        for k in range(parts):
            at = slice(k * mid, (k + 1) * mid)
            x_ref[extra, at] = jnp.where(two_rows, x_sum[k : k + 1, :] / count, 0.0).astype(BF)
        for k in range(9):
            dy, dx = divmod(k, 3)
            inside = (1.0 if dy == 1 else 6 / 7) * (1.0 if dx == 1 else 6 / 7)
            patches[extra, k * mid : (k + 1) * mid] = jnp.where(two_rows, act_mean * inside, 0.0).astype(BF)

    extra = slice(rows, rows + 16)
    first_row = lax.broadcasted_iota(jnp.int32, (16, mid), 0) < 1
    two_rows = lax.broadcasted_iota(jnp.int32, (16, mid), 0) < 2
    total = sum_over_all(place, sums, pair_buf.at[2], chip_buf.at[2], sum_sem.at[2], during_third)
    clock.work(3.5)
    shift2, gain2 = total[0:1] / count, total[1:2] / count
    for gather in (g1, g2, gh):
        gather.drain()

    s_totals = [Total(place, clock, s_pair.at[k], s_chip.at[k], s_sem.at[k], s_total.at[k]) for k in range(2)]

    def offset(acc, totals):
        share = fold(acc).astype(BF)
        dh[extra, :] = jnp.where(first_row, -share.astype(F32), 0.0).astype(BF)
        totals.start(share.astype(F32))
        active.append(totals)

    fulls, sums_refs, weight_refs = [g2_ref, g1_ref], [f2, f1], [w2b, w1b]
    pieces = [
        Piece(plan, place, clock, fulls[plan["conv"]], sums_refs[plan["conv"]], weight_refs[plan["conv"]], refs)
        for plan in plans
    ]
    slots = [h2_ref, h1_ref]
    mom_loads = []
    for k, plan in enumerate(plans):
        src = (mom2_hbm, mom1_hbm)[plan["conv"]].at[pl.ds(plan["part"] * plan["size"], plan["size"])]
        mom_loads.append(pltpu.make_async_copy(src, slots[k % 2].at[pl.ds(0, plan["size"])], mom_sem.at[k]))
    cross = da1.at[pl.ds(0, mid)]
    grams = [Gram(place, clock, g, cross, packed.at[k], gram_total.at[k], gram_sem.at[k]) for k, g in enumerate((gram2, gram1))]
    waiting, added, turns = [], [], []

    def gradient(piece, source):
        plan = piece.plan
        part = plan["size"] // 2
        for block in range(n_rep):
            for who in range(2):
                first = block * plan["half"] + plan["part"] * plan["size"]
                if plan["fits"]:
                    mine = core if who else 1 - core
                    value = tn(source[:, pl.ds(pl.multiple_of(first + mine * part, 128), part)], dh[...])
                    if who:
                        piece.acc[piece.part(block, 0, part), :] = value
                    else:
                        piece.outgoing[0][block] = value.astype(BF)
                else:
                    value = tn(source[:, first + who * part : first + who * part + part], dh[...])

                    @pl.when(core == who)
                    def keep(block=block, value=value):
                        piece.acc[piece.part(block, 0, part), :] = value

                    @pl.when(core != who)
                    def give(block=block, value=value):
                        piece.outgoing[0][block] = value.astype(BF)

                clock.work(part * 0.00135)
            if block == n_rep - 1:
                piece.start()
        active.append(piece)

    def finished(piece):
        index = pieces.index(piece)
        size, part, conv = piece.plan["size"], piece.plan["part"], piece.plan["conv"]
        mom_loads[index].wait()
        if part == 0:
            total, to = s_totals[conv], (s2_ref, s1_ref)[conv]
            while total in active:
                do(total)
            high, low = halves_of(s_total[conv])
            first = jnp.where(first_row, high.astype(F32), 0.0)
            to[...] = jnp.where(two_rows, jnp.where(first_row, first, low.astype(F32)), 0.0).astype(BF)
        rows_at = slice(part * size, part * size + size)
        back = tn((m2_ref, m1_ref)[conv][:, rows_at], (s2_ref, s1_ref)[conv][...])
        grams[conv].add(0.5 * slots[index % 2][0:size, :] + (fulls[conv][rows_at, :].astype(F32) + back))
        clock.work(size * 0.0015)
        if index + 2 < len(pieces):
            mom_loads[index + 2].start()
        if not [p for p in pieces[index + 1 :] if p.plan["conv"] == conv]:
            grams[conv].start()
            active.append(grams[conv])

    def do(item):
        if item.advance():
            return
        active.remove(item)
        if isinstance(item, (Factors, Total)):
            return
        if isinstance(item, Piece):
            waiting.append(item)
            while len(added) < len(pieces) and pieces[len(added)] in waiting:
                added.append(pieces[len(added)])
                finished(added[-1])
        else:
            turns.extend((item, turn) for turn in range(TURNS))

    def serve(margin=0.0):
        while True:
            due = [k for k in active if k.ready + margin <= clock.now]
            if not due:
                return
            do(min(due, key=lambda k: k.ready))

    def work_turn():
        item, turn = turns.pop(0)
        index = grams.index(item)
        out = (q2_ref, q1_ref)[index]

        @pl.when(core == index)
        def here():
            newton_turn(turn, item.g, out)
            if turn == TURNS - 1:
                out[...] = out[...] / item.scale
                send(out, out, q_sem.at[index, 0], q_sem.at[index, 1], place.flip(0))

        clock.work(2.8 if active else 0.0)

    def finish2(pixel, row, carry):
        dy, unit_h = back2(row)
        put = (scale2 * (dy - shift2 - unit_h * gain2)).astype(BF)
        put_padded(dpad, pixel, put, images)
        dh[pl.ds(row, images), :] = put
        return carry + put.astype(F32)

    offset(over_pixels(finish2, zero, images), s_totals[0])
    clock.work(1.3)
    mom_loads[0].start()
    for source, to, half in ((patches, m2_ref, half2), (x_ref, m1_ref, half1)):
        for block in range(n_rep):

            @pl.when(rep == block)
            def own(source=source, to=to, half=half, block=block):
                to[...] = source[extra, block * half : (block + 1) * half]

    for k in range(9):
        dy, dx = divmod(k, 3)
        lhs = dpad[2 - dy : 2 - dy + SIDE, (2 - dx) * images : (2 - dx) * images + line, :].reshape(rows, mid)
        first = k * mid
        weights = w2b[first // half2, first % half2 : first % half2 + mid, :] if half2 % mid == 0 else None
        if weights is None:
            ends = sorted({first, first + mid, *(b * half2 for b in range(n_rep) if first < b * half2 < first + mid)})
            weights = [w2b[a // half2, a % half2 : a % half2 + b - a, :] for a, b in zip(ends, ends[1:])]
            weights = weights[0] if len(weights) == 1 else jnp.concatenate(weights, axis=0)
        part = nt(lhs, weights)
        da1[...] = part if k == 0 else da1[...] + part
        clock.work(0.5)
        if k % 3 == 2:
            serve(2.0)

    def back1(pixel, row, carry):
        h = h1_ref[pl.ds(row, images), :]
        v = h * scale1 + move1
        sig = sigmoid(v)
        dy = da1[pl.ds(row, images), :] * sig * (1.0 + v * (1.0 - sig))
        da1[pl.ds(row, images), :] = dy
        return carry[0] + dy, carry[1] + dy * ((h - mean1) * inv1)

    one, two = over_pixels(back1, (zero, zero), images)
    clock.work(1.1)
    second = [p for p in pieces if p.plan["conv"] == 0]
    ahead = second[: max(1, len(second) - 1)]

    def during_fourth():
        clock.work(1.5)
        begun = clock.now
        for piece in ahead:
            gradient(piece, patches)
        clock.now = max(clock.now, begun + 4.0)
        serve(2.0)

    sums = jnp.concatenate([fold(one), fold(two), fold(one)], axis=0)
    total = sum_over_all(place, sums, pair_buf.at[3], chip_buf.at[3], sum_sem.at[3], during_fourth)
    stat_ref[...] = jnp.concatenate([total[0:2], shift2 * count, gain2 * count], axis=0)
    shift1, gain1 = total[0:1] / count, total[1:2] / count
    serve()
    for piece in second[len(ahead) :]:
        gradient(piece, patches)
        serve()

    def finish1(pixel, row, carry):
        h = h1_ref[pl.ds(row, images), :]
        dy = da1[pl.ds(row, images), :]
        put = (scale1 * (dy - shift1 - (h - mean1) * inv1 * gain1)).astype(BF)
        dh[pl.ds(row, images), :] = put
        return carry + put.astype(F32)

    offset(over_pixels(finish1, zero, images), s_totals[1])
    clock.work(0.8)
    mom_loads[1].start()
    serve()
    for piece in pieces:
        if piece.plan["conv"] == 1:
            gradient(piece, x_ref)
            serve()

    while active or turns:
        due = min(active, key=lambda k: k.ready) if active else None
        if due is not None and (not turns or due.ready <= clock.now + 2.0):
            if not isinstance(due, (Piece, Factors, Gram)):
                clock.now = max(clock.now, due.ready)
            do(due)
        else:
            work_turn()
    for index, out in enumerate((q2_ref, q1_ref)):

        @pl.when(core == index)
        def sent(index=index, out=out):
            wait_bytes(out, q_sem.at[index, 0])

        @pl.when(core != index)
        def came(index=index, out=out):
            wait_bytes(out, q_sem.at[index, 1])

    for item in [x_total, head_total, *s_totals]:
        item.drain()


def run_step(n_dp, n_rep, x, conv1, conv2, head, live1, live2, mom1, mom2, bias, norm, labels):
    rows, mid = x.shape[0], conv1.shape[1]
    images = rows // (SIDE * SIDE)
    half1, half2 = conv1.shape[0], conv2.shape[0]
    classes, head_cols = head.shape
    wide = (classes + mid - 1) // mid * mid
    devices, chips, parts = n_dp * n_rep, n_dp // 2 * n_rep, x.shape[1] // mid
    head_rows, block = wide // mid + 1, mid // 4
    shape = jax.ShapeDtypeStruct
    vmem, hbm = pl.BlockSpec(memory_space=pltpu.VMEM), pl.BlockSpec(memory_space=pl.ANY)
    more = []
    plans = plan_pieces(n_dp, n_rep, [(half2, 3, ("rep", "rep", "rep"), ("late",) * 3), (half1, 2, ("dp", "dp"), ("late",) * 2)], mid, more)
    pad = ((SIDE + 2), (SIDE + 2) * images, mid)
    levels = n_rep.bit_length()
    scratch = [
        pltpu.VMEM((rows + 16, x.shape[1]), BF), pltpu.VMEM((rows + 16, 9 * mid), BF),
        pltpu.VMEM((rows, mid), F32), pltpu.VMEM((rows, mid), F32), pltpu.VMEM((rows, mid), F32),
        pltpu.VMEM(pad, BF), pltpu.VMEM(pad, BF), pltpu.VMEM((rows + 16, mid), BF),
        pltpu.VMEM((n_rep, half1, mid), BF), pltpu.VMEM((n_rep, half2, mid), BF), pltpu.VMEM((n_rep, wide, head_cols), BF),
        pltpu.VMEM((n_rep * half1 // 2, mid), F32), pltpu.VMEM((n_rep * half2 // 2, mid), F32),
        pltpu.VMEM((half2, mid), jnp.int32), pltpu.VMEM((classes, head_cols), F32), pltpu.VMEM((1, wide), F32),
        pltpu.VMEM((images, wide + mid), BF),
        pltpu.VMEM((mid, mid), F32), pltpu.VMEM((mid, mid), F32),
        pltpu.VMEM((2, levels, block, 5 * block), F32), pltpu.VMEM((2, 2, block, 5 * block), F32),
        pltpu.VMEM((parts, mid), F32), pltpu.VMEM((2, 1, mid), F32), pltpu.VMEM((images, mid), F32),
        pltpu.VMEM((4, 2, 3, mid), F32), pltpu.VMEM((4, chips, 3, mid), F32),
        pltpu.VMEM((2, parts, mid), F32), pltpu.VMEM((chips, parts, mid), F32),
        pltpu.VMEM((2, 2, 1, mid), F32), pltpu.VMEM((2, chips, 1, mid), F32),
        pltpu.VMEM((2, head_rows, mid), F32), pltpu.VMEM((chips, head_rows, mid), F32),
        DMA((7,)), DMA((4, 4, 2)), DMA((4, 3, 2)), DMA((4, 1, 2)), DMA((4, 4)), DMA((4,)), DMA((len(plans),)),
        DMA((2, levels, 2)), DMA((2, 4)), DMA((4,)), DMA((devices.bit_length(), max(1, devices // 8), 2)), DMA((2, 2)),
    ]
    return pl.pallas_call(
        functools.partial(kernel_step, n_dp, n_rep, plans),
        out_shape=(
            shape((half1, mid), BF), shape((half2, mid), BF), shape((mid, mid), F32), shape((mid, mid), F32),
            shape((16, half1), BF), shape((16, half2), BF), shape((16, mid), BF), shape((16, mid), BF),
            shape((4, mid), F32), shape((head_rows, mid), F32), shape((devices, images, wide + mid), BF),
        ),
        in_specs=[hbm] * 8 + [vmem] * 2 + [pl.BlockSpec(memory_space=pltpu.SMEM)],
        out_specs=[vmem] * 10 + [hbm],
        scratch_shapes=scratch + more,
        compiler_params=pltpu.CompilerParams(
            collective_id=1, has_side_effects=True, vmem_limit_bytes=63 * 2**20
        ),
        name="gradients",
    )(x, conv1, conv2, head, live1, live2, mom1, mom2, bias, norm, labels)


def adam_update(weight, first, second, grad, rate):
    first = 0.9 * first + 0.1 * grad
    second = 0.999 * second + 0.001 * grad * grad
    mhat = first / (1.0 - 0.9**STEP)
    vhat = second / (1.0 - 0.999**STEP)
    return (weight - rate * (mhat / (jnp.sqrt(vhat) + 1e-08) + 0.01 * weight), first, second)


def kernel_update(n_rep, tiles2, tiles1, *refs):
    (grad2, mean2, share2, mom2, weight2, mask2, q2, grad1, mean1, share1, mom1, weight1, mask1, q1,
     sums, head_sums, bias, bias_m, bias_v, norm, norm_m, norm_v, factors_hbm, head_hbm, first_hbm, second_hbm,
     new2, mom2_out, new1, mom1_out, loss_out, bias_out, bias_m_out, bias_v_out, norm_out, norm_m_out, norm_a_out, norm_b_out,
     head_out, first_out, second_out,
     split, factors, state, share, in_sem, out_sem) = refs
    step = pl.program_id(0)
    part = state.shape[2]
    classes = state.shape[1]
    mid = sums.shape[1]
    images = factors.shape[0] * factors.shape[1]
    wide = factors.shape[2] - mid
    sources, results = (head_hbm, first_hbm, second_hbm), (head_out, first_out, second_out)
    loads = [pltpu.make_async_copy(factors_hbm, factors, in_sem.at[3])]
    loads += [pltpu.make_async_copy(src, state.at[k], in_sem.at[k]) for k, src in enumerate(sources)]
    stores = [pltpu.make_async_copy(state.at[k], dst, out_sem.at[k]) for k, dst in enumerate(results)]

    @pl.when(step == 0)
    def begin():
        for load in loads:
            load.start()
        for k, q in enumerate((q2, q1)):
            split[2 * k], split[2 * k + 1] = halves_of(q[...])

    def update(k, grad, mean, share_ref, mom, weight, mask, new, mom_out):
        value = 0.5 * mom[...] + (grad[...].astype(F32) + tn(mean[...], share_ref[...]))
        mom_out[...] = value
        ortho = mm(halves_of(value), (split[2 * k], split[2 * k + 1]))
        new[...] = (weight[...] - 1.0 * ortho) * mask[...].astype(F32)

    @pl.when(step < tiles2)
    def second():
        update(0, grad2, mean2, share2, mom2, weight2, mask2, new2, mom2_out)

    @pl.when(step >= tiles2)
    def first():
        update(1, grad1, mean1, share1, mom1, weight1, mask1, new1, mom1_out)

    @pl.when(step == min(3, tiles2 + tiles1 - 1))
    def head():
        for load in loads:
            load.wait()
        every = factors[...].reshape(images, wide + mid)
        rep = lax.axis_index("rep")
        for block in range(n_rep):

            @pl.when(rep == block)
            def own(block=block):
                share[...] = every[:, wide + block * part : wide + (block + 1) * part]

        grad = tn(every[:, 0:wide], share[...])[0:classes]
        state[0], state[1], state[2] = adam_update(state[0], state[1], state[2], grad, 0.03)
        for store in stores:
            store.start()
        loss_out[...] = head_sums[wide // mid :, 0:1]
        for k in range(wide // mid):
            at = (slice(None), slice(k * mid, min((k + 1) * mid, classes)))
            grad = head_sums[k : k + 1, 0 : min(mid, classes - k * mid)]
            bias_out[at], bias_m_out[at], bias_v_out[at] = adam_update(bias[at], bias_m[at], bias_v[at], grad, 0.2)
        for k, out in enumerate((norm_a_out, norm_b_out)):
            for j in range(2):
                at, grad = (k, slice(j, j + 1)), sums[2 * k + 1 - j : 2 * k + 2 - j]
                norm_out[at], norm_m_out[at], out[j : j + 1, :] = adam_update(norm[at], norm_m[at], norm_v[at], grad, 0.2)

    @pl.when(step == tiles2 + tiles1 - 1)
    def end():
        for store in stores:
            store.wait()


def run_update(n_rep, second, first, sums, head_sums, smalls, factors, heads):
    mid = sums.shape[1]
    shape = jax.ShapeDtypeStruct
    whole = pl.BlockSpec(memory_space=pltpu.VMEM)
    hbm = pl.BlockSpec(memory_space=pl.ANY)
    sizes = [next((k for k in (768, 512, 256, 128) if c[3].shape[0] % k == 0 and k < c[3].shape[0]), c[3].shape[0]) for c in (second, first)]
    tiles2, tiles1 = second[3].shape[0] // sizes[0], first[3].shape[0] // sizes[1]
    places = (lambda i: jnp.minimum(i, tiles2 - 1), lambda i: jnp.maximum(i - tiles2, 0))
    in_specs, out_specs = [], []
    for size, at in zip(sizes, places):
        tile = pl.BlockSpec((size, mid), lambda i, at=at: (at(i), 0))
        mean = pl.BlockSpec((16, size), lambda i, at=at: (0, at(i)))
        in_specs += [tile, mean, whole, tile, tile, tile, whole]
        out_specs += [tile, tile]
    bias, norm = smalls[0], smalls[3]
    classes, part = heads[0].shape
    outs = [second[3].shape] * 2 + [first[3].shape] * 2
    outs += [(1, 1)] + [bias.shape] * 3 + [norm.shape] * 2 + [norm.shape[1:]] * 2 + [heads[0].shape] * 3
    return pl.pallas_call(
        functools.partial(kernel_update, n_rep, tiles2, tiles1),
        grid=(tiles2 + tiles1,),
        out_shape=tuple(shape(s, F32) for s in outs),
        in_specs=in_specs + [whole] * 8 + [hbm] * 4,
        out_specs=out_specs + [whole] * 8 + [hbm] * 3,
        scratch_shapes=[
            pltpu.VMEM((4, mid, mid), BF), pltpu.VMEM(factors.shape, BF), pltpu.VMEM((3, classes, part), F32),
            pltpu.VMEM((factors.shape[0] * factors.shape[1], part), BF), DMA((4,)), DMA((3,)),
        ],
        compiler_params=pltpu.CompilerParams(vmem_limit_bytes=63 * 2**20),
        name="update",
    )(*second, *first, sums, head_sums, *smalls, factors, *heads)


def local(
    images,
    labels,
    conv1,
    conv2,
    classifier,
    class_bias,
    batchnorm_parameters,
    conv1_mom,
    conv2_mom,
    class_m,
    class_v,
    bias_m,
    bias_v,
    norm_m,
    norm_v,
    conv1_live,
    conv2_live,
    conv1_next,
    conv2_next,
):
    count, c_in = images.shape[0], images.shape[3]
    n_dp, n_rep = lax.axis_size("dp"), lax.axis_size("rep")
    x = images.transpose(1, 2, 0, 3).reshape(SIDE * SIDE * count, c_in)
    bias = class_bias.reshape(1, -1)
    g_one, g_two, q_one, q_two, m_one, m_two, s_one, s_two, sums, head_sums, factors = run_step(
        n_dp, n_rep, x, conv1, conv2, classifier.T, conv1_live, conv2_live, conv1_mom, conv2_mom,
        bias, batchnorm_parameters, labels,
    )
    (conv2_new, mom_two, conv1_new, mom_one, loss, bias_new, first_b, second_b, norm_new, first_n, norm_a, norm_b,
     head_new, head_m, head_v) = run_update(
        n_rep,
        (g_two, m_two, s_two, conv2_mom, conv2, conv2_next, q_two),
        (g_one, m_one, s_one, conv1_mom, conv1, conv1_next, q_one),
        sums,
        head_sums,
        (bias, bias_m.reshape(1, -1), bias_v.reshape(1, -1), batchnorm_parameters, norm_m, norm_v),
        factors,
        (classifier.T, class_m.T, class_v.T),
    )
    return (
        loss[0, 0],
        conv1_new,
        conv2_new,
        head_new.T,
        bias_new[0],
        norm_new,
        mom_one,
        mom_two,
        head_m.T,
        head_v.T,
        first_b[0],
        second_b[0],
        first_n,
        norm_a,
        norm_b,
    )


def solution(mesh):
    placed = (
        P(("dp", "rep"), None, None, None),
        P(("dp", "rep")),
        P("rep", None),
        P("rep", None),
        P("rep", None),
        P(),
        P(),
        P("rep", None),
        P("rep", None),
        P("rep", None),
        P("rep", None),
        P(),
        P(),
        P(),
        P(),
        P("rep", None),
        P("rep", None),
        P("rep", None),
        P("rep", None),
    )
    return jax.shard_map(
        local,
        mesh=mesh,
        in_specs=placed,
        out_specs=(
            P(),
            P("rep", None),
            P("rep", None),
            P("rep", None),
            P(),
            P(),
            P("rep", None),
            P("rep", None),
            P("rep", None),
            P("rep", None),
            P(),
            P(),
            P(),
            P(),
            P(),
        ),
        check_vma=False,
    )
```

```python
import contextlib
import functools

import jax
import jax.numpy as jnp
from jax import lax
from jax.experimental import pallas as pl
from jax.experimental.pallas import tpu as pltpu
from jax.sharding import PartitionSpec as P

SIDE = 7
TURNS = 5
STEP = 5
NORM_EPS = 1e-05
COEF_A = 3.4445
COEF_B = -4.775
COEF_C = 2.0315
MESH = pl.DeviceIdType.MESH
BF = jnp.bfloat16
F32 = jnp.float32
DMA = pltpu.SemaphoreType.DMA


def scope(name):
    return contextlib.nullcontext()


def nn(a, b):
    return jnp.dot(a, b, preferred_element_type=F32)


def nt(a, b):
    return lax.dot_general(a, b, (((1,), (1,)), ((), ())), preferred_element_type=F32)


def tn(a, b):
    return lax.dot_general(a, b, (((0,), (0,)), ((), ())), preferred_element_type=F32)


def sigmoid(v):
    return 1.0 / (1.0 + jnp.exp(-v))


class Place:
    def __init__(self, n_dp, n_rep):
        self.n_dp, self.n_rep = n_dp, n_rep
        self.chips = n_dp // 2 * n_rep
        self.dp, self.rep = lax.axis_index("dp"), lax.axis_index("rep")
        self.core = lax.rem(self.dp, 2)
        self.chip = self.dp // 2 * n_rep + self.rep

    def flip(self, bit):
        half = 1 << bit
        set_now = lax.rem(self.dp // half, 2)
        return {"dp": self.dp + half - 2 * half * set_now, "rep": self.rep}

    def flip_rep(self, bit):
        half = 1 << bit
        set_now = lax.rem(self.rep // half, 2)
        return {"dp": self.dp, "rep": self.rep + half - 2 * half * set_now}

    def other_chip(self, step):
        to = lax.rem(self.chip + step, self.chips)
        return {"dp": to // self.n_rep * 2 + self.core, "rep": lax.rem(to, self.n_rep)}

    def other_rep(self, step):
        return {"dp": self.dp, "rep": lax.rem(self.rep + step, self.n_rep)}


def send(src, dst, send_sem, recv_sem, to):
    copy = pltpu.make_async_remote_copy(src, dst, send_sem, recv_sem, to, MESH)
    copy.start()


def wait_bytes(ref, sem):
    with scope("wait"):
        pltpu.make_async_copy(ref, ref, sem).wait()


def greet(place):
    barrier = pltpu.get_barrier_semaphore()

    def one(step, carry):
        pl.semaphore_signal(barrier, 1, device_id=place.other_chip(step), device_id_type=MESH)
        return carry

    lax.fori_loop(1, place.chips, one, 0)
    pl.semaphore_signal(barrier, 1, device_id=place.flip(0), device_id_type=MESH)


def met(place):
    pl.semaphore_wait(pltpu.get_barrier_semaphore(), place.chips)


def sum_over_all(place, value, pair_buf, chip_buf, sems, meanwhile=None):
    pair_buf[place.core] = value
    mine = pair_buf.at[place.core]
    send(mine, mine, sems.at[0], sems.at[1], place.flip(0))
    wait_bytes(mine, sems.at[1])
    chip_buf[place.chip] = pair_buf[0] + pair_buf[1]
    block = chip_buf.at[place.chip]

    def one(step, carry):
        send(block, block, sems.at[2], sems.at[3], place.other_chip(step))
        return carry

    lax.fori_loop(1, place.chips, one, 0)
    if meanwhile is not None:
        meanwhile()
    wait_bytes(chip_buf.at[pl.ds(0, place.chips - 1)], sems.at[3])
    total = jnp.sum(chip_buf[...], axis=0)
    wait_bytes(mine, sems.at[0])
    wait_bytes(chip_buf.at[pl.ds(0, place.chips - 1)], sems.at[2])
    return total


class Total:
    def __init__(self, place, clock, pair_buf, chip_buf, sems, out):
        self.place, self.clock, self.pair, self.chip, self.sems, self.out = place, clock, pair_buf, chip_buf, sems, out
        self.step, self.ready = 0, None

    def start(self, value):
        self.pair[self.place.core] = value
        mine = self.pair.at[self.place.core]
        send(mine, mine, self.sems.at[0], self.sems.at[1], self.place.flip(0))
        self.ready = self.clock.carry("core", 2)

    def others(self):
        return self.chip.at[pl.ds(0, self.place.chips - 1)]

    def advance(self):
        place = self.place
        if self.step == 0:
            wait_bytes(self.pair.at[0], self.sems.at[1])
            self.chip[place.chip] = self.pair[0] + self.pair[1]
            block = self.chip.at[place.chip]

            def one(step, carry):
                send(block, block, self.sems.at[2], self.sems.at[3], place.other_chip(step))
                return carry

            lax.fori_loop(1, place.chips, one, 0)
            self.clock.work(0.8)
            self.ready = self.clock.now + 3.5
            self.step = 1
            return True
        wait_bytes(self.others(), self.sems.at[3])
        self.out[...] = jnp.sum(self.chip[...], axis=0)
        self.step = 2
        return False

    def drain(self):
        wait_bytes(self.pair.at[0], self.sems.at[0])
        wait_bytes(self.others(), self.sems.at[2])


class Clock:
    RATES = {"core": (550.0, 1.0), "far": (23.0, 2.8)}

    def __init__(self):
        self.now = 0.0
        self.free, self.flying, self.queued = {}, {}, {}

    def work(self, span):
        self.now += span

    def carry(self, link, kilobytes, earliest=0.0):
        rate, hop = self.RATES.get(link, (46.0, 2.1))
        begin = max(self.now, earliest, self.free.get(link, 0.0))
        self.free[link] = begin + kilobytes / rate
        return self.free[link] + hop

    def launch(self, item):
        line = self.flying.setdefault(item.link, [])
        if item.owner.rank < 20:
            line.append(item)
        item.owner.ready = self.carry(item.link, item.kilobytes)
        for src, dst, to in item.pairs:
            send(src, dst, item.sems.at[0], item.sems.at[1], to)

    def ship(self, owner, link, pairs, size, sems, kilobytes):
        item = Transfer(owner, link, pairs, size, sems, kilobytes)
        owner.ready = float("inf")
        if link == "core" or owner.rank >= 20 or len(self.flying.get(link, [])) < (3 if link != "x" else 1):
            self.launch(item)
        else:
            self.queued.setdefault(link, []).append(item)
        return item

    def receive(self, item):
        rate, hop = self.RATES.get(item.link, (46.0, 2.1))
        self.now = max(self.now, item.owner.ready - hop)
        wait_bytes(item.size, item.sems.at[0])
        if item in self.flying[item.link]:
            self.flying[item.link].remove(item)
        queue = self.queued.get(item.link, [])
        if queue and item.link != "core" and item.owner.rank < 20:
            first = min(queue, key=lambda k: k.owner.rank)
            queue.remove(first)
            self.launch(first)
        self.now = max(self.now, item.owner.ready)
        wait_bytes(item.size, item.sems.at[1])


class Transfer:
    def __init__(self, owner, link, pairs, size, sems, kilobytes):
        self.owner, self.link, self.pairs, self.size, self.sems = owner, link, pairs, size, sems
        self.kilobytes = kilobytes


class Gather:
    def __init__(self, place, buf, pieces, sems):
        self.place, self.buf, self.pieces, self.sems = place, buf, pieces, sems
        self.quarter = buf.shape[1] // 4
        self.rows = self.quarter // pieces
        self.y = lax.rem(place.dp // 2, 2)

    def at(self, block, y, piece):
        first = self.place.core * (2 * self.quarter) + y * self.quarter + piece * self.rows
        return self.buf.at[block, pl.ds(pl.multiple_of(first, 16), self.rows)]

    def blocks(self):
        return [lax.rem(self.place.rep + step, self.place.n_rep) for step in range(1, self.place.n_rep)]

    def size(self):
        return self.buf.at[pl.ds(0, self.place.n_rep - 1), pl.ds(0, self.rows)]

    def start(self, piece):
        mine = self.at(self.place.rep, self.y, piece)
        for step in range(1, self.place.n_rep):
            send(mine, mine, self.sems.at[0, piece, 0], self.sems.at[0, piece, 1], self.place.other_rep(step))

    def hop_y(self, piece):
        wait_bytes(self.size(), self.sems.at[0, piece, 1])
        for block in self.blocks():
            here = self.at(block, self.y, piece)
            send(here, here, self.sems.at[1, piece, 0], self.sems.at[1, piece, 1], self.place.flip(1))
            send(here, here, self.sems.at[2, piece, 0], self.sems.at[2, piece, 1], self.place.flip(0))

    def hop_core(self, piece):
        wait_bytes(self.size(), self.sems.at[1, piece, 1])
        for block in self.blocks():
            here = self.at(block, 1 - self.y, piece)
            send(here, here, self.sems.at[3, piece, 0], self.sems.at[3, piece, 1], self.place.flip(0))

    def finish(self, piece):
        wait_bytes(self.size(), self.sems.at[2, piece, 1])
        wait_bytes(self.size(), self.sems.at[3, piece, 1])

    def drain(self):
        for piece in range(self.pieces):
            for hop in range(4):
                wait_bytes(self.size(), self.sems.at[hop, piece, 0])


def norm_of(total, count):
    mean = total[0:1] / count
    return mean, lax.rsqrt(total[1:2] / count - mean * mean + NORM_EPS)


def over_pixels(step, init, images):
    def body(pixel, carry):
        return step(pixel, pl.multiple_of(pixel * images, 16), carry)

    return lax.fori_loop(0, SIDE * SIDE, body, init, unroll=7)


def fold(acc):
    return jnp.sum(acc, axis=0, keepdims=True)


def sums_of(h_ref, images):
    chans = h_ref.shape[1]

    def step(pixel, row, carry):
        v = h_ref[pl.ds(row, images), :]
        return carry[0] + v, carry[1] + v * v

    zero = jnp.zeros((images, chans), F32)
    one, two = over_pixels(step, (zero, zero), images)
    return jnp.concatenate([fold(one), fold(two)], axis=0)


def put_padded(pad_ref, pixel, value, images):
    y, x = pixel // SIDE, lax.rem(pixel, SIDE)
    pad_ref[1 + y, pl.ds(pl.multiple_of((1 + x) * images, 16), images), :] = value


def clear_border(pad_ref, images):
    line = SIDE * images
    pad_ref[0] = jnp.zeros(pad_ref.shape[1:], pad_ref.dtype)
    pad_ref[SIDE + 1] = jnp.zeros(pad_ref.shape[1:], pad_ref.dtype)
    edge = jnp.zeros((SIDE, images, pad_ref.shape[2]), pad_ref.dtype)
    pad_ref[1 : SIDE + 1, 0:images, :] = edge
    pad_ref[1 : SIDE + 1, images + line : 2 * images + line, :] = edge


def build_patches(pad_ref, to_ref):
    images, chans = pad_ref.shape[1] // (SIDE + 2), pad_ref.shape[2]
    line = SIDE * images
    for k in range(9):
        dy, dx = divmod(k, 3)
        piece = pad_ref[dy : dy + SIDE, dx * images : dx * images + line, :]
        to_ref[0 : SIDE * line, k * chans : (k + 1) * chans] = piece.reshape(SIDE * line, chans)


class Factors:
    rank = 20

    def __init__(self, place, clock, buf, sems):
        self.place, self.clock, self.buf, self.sems = place, clock, buf, sems
        reps = [("rep", b) for b in range(place.n_rep.bit_length() - 1)]
        dps = [("dp", b) for b in reversed(range(1, place.n_dp.bit_length() - 1)) if b != 2]
        self.order = reps + dps + [("dp", 2), ("dp", 0)]
        self.index = 0
        for k, (axis, bit) in enumerate(self.order):
            self.index = self.index + (1 << k) * lax.rem((place.rep if axis == "rep" else place.dp) // (1 << bit), 2)
        self.step, self.chunk, self.ready = 0, 0, None

    @staticmethod
    def chunks(level, last):
        return 1 if last else max(1, (1 << level) // 2)

    def start(self, value_ref):
        load = pltpu.make_async_copy(value_ref, self.buf.at[self.index], self.sems.at[len(self.order), 0, 0])
        load.start()
        load.wait()
        self.ship()

    def ship(self):
        held = 1 << self.step
        size = held // self.chunks(self.step, self.step + 1 == len(self.order))
        mine = self.buf.at[pl.ds(self.index // held * held + self.chunk * size, size)]
        axis, bit = self.order[self.step]
        to = self.place.flip_rep(bit) if axis == "rep" else self.place.flip(bit)
        link = "x" if axis == "rep" else {0: "core", 1: "y", 2: "z"}.get(bit, "far")
        kilobytes = size * self.buf.shape[1] * self.buf.shape[2] * 2 / 1024
        sems = self.sems.at[self.step, self.chunk]
        self.item = self.clock.ship(self, link, [(mine, mine, to)], mine, sems, kilobytes)

    def advance(self):
        self.clock.receive(self.item)
        self.chunk += 1
        if self.chunk == self.chunks(self.step, self.step + 1 == len(self.order)):
            self.step, self.chunk = self.step + 1, 0
        if self.step == len(self.order):
            return False
        self.ship()
        return True


class Piece:
    def __init__(self, plan, place, clock, full, sums, weights, refs):
        self.plan, self.place, self.clock, self.full = plan, place, clock, full
        self.r0, self.nr, self.q0, self.nq = 0, place.n_rep, 0, plan["size"] // 2
        self.acc, wide, self.whole = sums, weights, self.nq
        self.first = plan["part"] * place.n_rep * self.nq
        low, middle = plan["part"] * self.nq, plan["half"] // 2
        ends = [wide.at[:, pl.ds(low, self.nq)], wide.at[:, pl.ds(middle + low, self.nq)]]
        if plan["early"]:
            ends = [refs[k] for k in plan["early"]]
        self.outgoing = ends[:1] + [refs[k] for k in plan["outgoing"]]
        self.incoming = ends[1:] + [refs[k] for k in plan["incoming"]]
        self.sems = refs[plan["sems"]]
        self.step, self.ready = 0, None
        self.rank = 10 * plan["conv"] + plan["part"]
        self.base = plan["part"] * plan["size"] + place.core * self.nq

    def bit(self, level):
        axis, bit = level["axis"], level["bit"]
        if axis == "four":
            return lax.rem(self.place.dp // (1 << bit), 4)
        return lax.rem((self.place.rep if axis == "rep" else self.place.dp) // (1 << bit), 2)

    def partner(self, level):
        return self.place.flip_rep(level["bit"]) if level["axis"] == "rep" else self.place.flip(level["bit"])

    def others(self, level):
        mine = self.bit(level)
        for step in range(1, 4):
            there = lax.rem(mine + step, 4)
            yield step - 1, there, {"dp": self.place.dp + (there - mine) * (1 << level["bit"]), "rep": self.place.rep}

    def part(self, block, q0, nq):
        return pl.ds(pl.multiple_of(self.first + block * self.whole + q0, 16), nq)

    def ship(self, pairs, size, slot, link, kilobytes):
        self.item = self.clock.ship(self, link, pairs, size, self.sems.at[slot], kilobytes)

    def start(self):
        size = self.place.n_rep * self.nq
        pairs = [(self.outgoing[0], self.incoming[0], self.place.flip(0))]
        self.ship(pairs, self.outgoing[0], 0, "core", size)

    def advance(self):
        with scope("piece%d%d_step%d" % (self.plan["conv"], self.plan["part"], self.step)):
            return self.move()

    def move(self):
        levels = self.plan["levels"]
        self.clock.receive(self.item)
        if self.step <= len(levels):
            for k in range(self.nr):
                at = self.part(self.r0 + k, self.q0, self.nq)
                value = self.acc[at, :] + self.incoming[self.step][k].astype(F32)
                if self.step and levels[self.step - 1]["axis"] == "four":
                    value = value + self.incoming[self.step][1].astype(F32) + self.incoming[self.step][2].astype(F32)
                self.acc[at, :] = value
            self.clock.work(0.2)
        if self.step < len(levels):
            self.begin(levels[self.step])
            self.step += 1
            return True
        back = self.plan["back"]
        done = self.step - len(levels)
        self.step += 1
        if done == 0:
            self.full[self.rows(self.q0, self.nq), :] = self.acc[self.part(self.r0, self.q0, self.nq), :].astype(BF)
            self.held = [(self.q0, self.nq)]
        elif done <= len(back):
            level = back[done - 1]
            bit, apart = self.bit(level), level["rows"]
            if level["axis"] == "four":
                self.held = [(first - bit * apart, 4 * apart) for first, _ in self.held]
            elif self.held[0][1] == apart:
                self.held = [(first - bit * apart, 2 * apart) for first, _ in self.held]
            else:
                self.held = [(at, n) for first, n in self.held for at in (first, first + (1 - 2 * bit) * apart)]
        else:
            return False
        link, to, copies = "core", [self.place.flip(0)], 1
        if done == len(back):
            self.held = [(0, self.whole)]
        elif back[done]["axis"] == "four":
            link, to, copies = "z", [there for _, _, there in self.others(back[done])], 4
        else:
            link, to = back[done]["link"], [self.partner(back[done])]
        refs = [self.full.at[self.rows(first, n)] for first, n in self.held]
        size = sum(n for _, n in self.held)
        whole = self.full.at[pl.ds(0, len(to) * size)]
        self.ship([(r, r, there) for r in refs for there in to], whole, self.step, link, copies * size)
        return True

    def rows(self, q0, nq):
        return pl.ds(pl.multiple_of(self.base + q0, 16), nq)

    def begin(self, level):
        bit = self.bit(level)
        out = self.outgoing[self.step + 1]
        if level["axis"] == "four":
            self.nq //= 4
            there = self.incoming[self.step + 1]
            pairs = []
            for k, index, to in self.others(level):
                out[k] = self.acc[self.part(self.r0, self.q0 + index * self.nq, self.nq), :].astype(BF)
                pairs.append((out.at[k], there.at[k], to))
            self.q0 = self.q0 + bit * self.nq
            self.ship(pairs, out, self.step + 1, level["link"], 4 * self.nq)
            return
        if level["halve"]:
            r1, q1 = self.r0, self.q0
            if level["axis"] == "rep":
                self.nr //= 2
                self.r0, r1 = self.r0 + bit * self.nr, self.r0 + (1 - bit) * self.nr
            else:
                self.nq //= 2
                self.q0, q1 = self.q0 + bit * self.nq, self.q0 + (1 - bit) * self.nq
            for k in range(self.nr):
                out[k] = self.acc[self.part(r1 + k, q1, self.nq), :].astype(BF)
        else:
            for k in range(self.nr):
                at = self.part(self.r0 + k, self.q0, self.nq)
                out[k] = self.acc[at, :].astype(BF)
                self.acc[at, :] = out[k].astype(F32)
        pairs = [(out, self.incoming[self.step + 1], self.partner(level))]
        self.ship(pairs, out, self.step + 1, level["link"], self.nr * self.nq)


def plan_pieces(n_dp, n_rep, halves, mid, scratch):
    plans = []
    for conv, (half, parts, firsts, backs) in enumerate(halves):
        fits = half % (parts * 16 * n_dp) == 0 and half // parts // 2 % 128 == 0
        if not fits:
            parts = 1
        for part in range(parts):
            size = half // parts
            reps = [("rep", b) for b in reversed(range(n_rep.bit_length() - 1))]
            dps = [("dp", b) for b in range(1, n_dp.bit_length() - 1)]
            order = reps + dps if firsts[part] == "rep" else dps[:1] + reps + dps[1:]
            nr, nq, levels, shapes = n_rep, size // 2, [], []
            if order[-2:] == [("dp", 2), ("dp", 3)] and size // 2 % (2 * 4 * 16) == 0:
                order = order[:-2] + [("four", 2)]
            for axis, bit in order:
                if axis == "four":
                    nq //= 4
                    levels.append({"axis": axis, "bit": bit, "halve": True, "link": "z", "rows": nq})
                    shapes.append((3, nq, mid))
                    continue
                halve = axis == "rep" or nq // 2 % 16 == 0
                if halve and axis == "rep":
                    nr //= 2
                elif halve:
                    nq //= 2
                link = "x" if axis == "rep" else {1: "y", 2: "z"}.get(bit, "far")
                levels.append({"axis": axis, "bit": bit, "halve": halve, "link": link, "rows": nq})
                shapes.append((nr, nq, mid))
            plan = {"conv": conv, "part": part, "size": size, "half": half, "levels": levels, "fits": fits}
            back = [k for k in reversed(levels) if k["axis"] != "rep" and k["halve"]]
            plan["back"] = sorted(back, key=lambda k: k["bit"] != 1) if backs[part] == "early" else back

            def add(spec):
                scratch.append(spec)
                return len(scratch) - 1

            early = parts > 1 and conv == part == 0
            plan["early"] = [add(pltpu.VMEM((n_rep, size // 2, mid), BF)) for _ in range(2)] if early else []
            plan["outgoing"] = [add(pltpu.VMEM(s, BF)) for s in shapes]
            plan["incoming"] = [add(pltpu.VMEM(s, BF)) for s in shapes]
            plan["sems"] = add(DMA((2 * len(levels) + 2, 2)))
            plans.append(plan)
    return plans


def halves_of(v):
    high = v.astype(BF)
    return high, (v - high.astype(F32)).astype(BF)


def mm(a, b):
    return nn(a[0], b[0]) + (nn(a[0], b[1]) + nn(a[1], b[0]))


def square(a):
    cross = nn(a[0], a[1])
    return nn(a[0], a[0]) + (cross + cross.T)


def unit(n):
    return lax.broadcasted_iota(jnp.int32, (n, n), 0) == lax.broadcasted_iota(jnp.int32, (n, n), 1)


def newton_turn(turn, g_ref, q_ref):
    n = g_ref.shape[0]
    gram = halves_of(g_ref[...])
    factor = COEF_A * unit(n).astype(F32) + COEF_B * g_ref[...] + COEF_C * square(gram)
    factors = halves_of(factor)
    if turn == 0:
        q_ref[...] = factor
    else:
        q_ref[...] = mm(halves_of(q_ref[...]), factors)
    if turn < TURNS - 1:
        g_ref[...] = mm(halves_of(mm(gram, factors)), factors)


class Gram:
    def __init__(self, place, clock, g_ref, cross_ref, packed, total, sems):
        self.place, self.clock, self.g, self.cross, self.sems = place, clock, g_ref, cross_ref, sems
        self.packed, self.total = packed, total
        self.fresh, self.rank = True, -1
        self.step, self.ready = 0, None
        self.b, self.levels = g_ref.shape[0] // 4, place.n_rep.bit_length() - 1

    def add(self, value):
        high, low = halves_of(value)
        if self.fresh:
            self.g[...] = tn(high, high)
            self.cross[...] = tn(high, low)
        else:
            self.g[...] += tn(high, high)
            self.cross[...] += tn(high, low)
        self.fresh = False

    def start(self):
        b = self.b
        g = self.g[...] + self.cross[...] + self.cross[...].T
        to = self.packed
        one = jnp.concatenate([g[0:b, :], g[3 * b :, 3 * b :]], axis=1)
        two = jnp.concatenate([g[b : 2 * b, b:], g[2 * b : 3 * b, 2 * b :]], axis=1)
        to[0] = jnp.where(self.place.core == 0, one, two)
        self.clock.work(1.5)
        self.ship()

    def ship(self):
        mine, theirs = self.packed.at[0], self.packed.at[self.step + 1]
        self.item = self.clock.ship(
            self, "x", [(mine, theirs, self.place.flip_rep(self.step))], mine, self.sems.at[self.step], 5 * self.b * self.b * 4 / 1024
        )

    def advance(self):
        place, to, levels = self.place, self.packed, self.levels
        if self.step < levels:
            self.clock.receive(self.item)
            last = self.step + 1 == levels
            value = to[0] + to[self.step + 1]
            self.step += 1
            if not last:
                to[0] = value
                self.ship()
                return True
            self.total[place.core] = value
            mine = self.total.at[place.core]
            self.item = self.clock.ship(self, "core", [(mine, mine, place.flip(0))], mine, self.sems.at[levels], 330)
            return True
        self.clock.receive(self.item)
        b, to = self.b, self.total
        g = self.g
        g[0:b, :] = to[0, :, 0 : 4 * b]
        g[3 * b :, 3 * b :] = to[0, :, 4 * b :]
        g[b : 2 * b, b:] = to[1, :, 0 : 3 * b]
        g[2 * b : 3 * b, 2 * b :] = to[1, :, 3 * b :]
        for i in range(1, 4):
            for j in range(i):
                g[i * b : (i + 1) * b, j * b : (j + 1) * b] = g[j * b : (j + 1) * b, i * b : (i + 1) * b].T
        trace = jnp.sum(jnp.sum(jnp.where(unit(4 * b), g[...], 0.0), axis=0, keepdims=True), axis=1, keepdims=True)
        self.scale = jnp.sqrt(trace) + 1e-07
        g[...] = g[...] / (self.scale * self.scale)
        self.clock.work(1.0)
        return False


def kernel_step(n_dp, n_rep, plans, *refs):
    (x_hbm, w1_hbm, w2_hbm, head_hbm, live1_hbm, live2_hbm, mom1_hbm, mom2_hbm, next2_hbm, bias_ref, norm_ref, label_ref,
     f1, f2, live, q1_ref, q2_ref, stat_ref, head_ref, factors_ref,
     g1_ref, g2_ref, m1_ref, m2_ref, s1_ref, s2_ref,
     x_ref, patches, h1_ref, h2_ref, da1, pad, dpad, dh, w1b, w2b, head_b, fh, bias_pad, factor,
     gram1, gram2, packed, gram_total, x_sum, s_total, dpool_ref,
     pair_buf, chip_buf, x_pair, x_chip, s_pair, s_chip, head_pair, head_chip,
     load_sem, w1_sem, w2_sem, head_sem, sum_sem, x_sem, mom_sem, gram_sem, s_sem, total_sem, factor_sem, q_sem, next_sem) = refs[:68]
    refs = refs[68:]
    place, clock = Place(n_dp, n_rep), Clock()
    core, rep = place.core, place.rep
    half1, half2, mid = w1b.shape[1], w2b.shape[1], w1b.shape[2]
    classes, head_cols = fh.shape
    wide = head_b.shape[1]
    images = factor.shape[0]
    line = SIDE * images
    rows = SIDE * line
    all_images = images * n_dp * n_rep
    count = all_images * SIDE * SIDE
    parts = x_ref.shape[1] // mid
    zero = jnp.zeros((images, mid), F32)

    early = half2 - half1
    pairs = [
        (w1_hbm, f1.at[pl.ds(0, half1)]),
        (live1_hbm, live.at[pl.ds(early, half1)]),
        (w2_hbm, f2.at[pl.ds(0, half2)]),
        (live2_hbm.at[pl.ds(0, early)], live.at[pl.ds(0, early)]),
        (x_hbm, x_ref.at[pl.ds(0, rows)]),
        (head_hbm, fh),
        (live2_hbm.at[pl.ds(early, half1)], live.at[pl.ds(early, half1)]),
    ]
    loads = [pltpu.make_async_copy(a, b, load_sem.at[k]) for k, (a, b) in enumerate(pairs)]
    loads[0].start()
    loads[1].start()
    greet(place)
    g1, gh = Gather(place, w1b, 4, w1_sem), Gather(place, head_b, 1, head_sem)
    g2 = Gather(place, w2b, w2_sem.shape[1], w2_sem)

    def second(starts=(), over_y=(), over_core=()):
        for what, which in ((g2.hop_y, over_y), (g2.start, starts), (g2.hop_core, over_core)):
            for piece in which:
                if piece < g2.pieces:
                    what(piece)

    def mask(value, shift, to, first, size):
        at, at_live = pl.ds(pl.multiple_of(first, 16), size), pl.ds(pl.multiple_of(first + shift, 16), size)
        to[rep, at, :] = (value[at, :] * live[at_live, :].astype(F32)).astype(BF)

    def mask_quarters(gather, value, shift, to):
        mine = core * 2 + gather.y
        for other in range(1, 4):
            mask(value, shift, to, lax.rem(mine + other, 4) * gather.quarter, gather.quarter)

    def mask_piece(gather, value, shift, to, piece):
        mine = core * 2 + gather.y
        mask(value, shift, to, mine * gather.quarter + piece * gather.rows, gather.rows)

    loads[0].wait()
    loads[1].wait()
    for load in loads[2:6]:
        load.start()
    mask_piece(g1, f1, early, w1b, 0)
    met(place)
    g1.start(0)
    for piece in range(1, g1.pieces):
        mask_piece(g1, f1, early, w1b, piece)
        g1.start(piece)
    mask_quarters(g1, f1, early, w1b)
    loads[6].start()
    clear_border(pad, images)
    clear_border(dpad, images)
    bias_pad[:, 0:classes] = bias_ref[...]
    bias_pad[:, classes:] = jnp.zeros((1, wide - classes), F32)
    for k in (2, 3, 6):
        loads[k].wait()
    for piece in range(g2.pieces):
        mask_piece(g2, f2, 0, w2b, piece)
    mask_quarters(g2, f2, 0, w2b)
    next_load = pltpu.make_async_copy(next2_hbm, live.at[pl.ds(0, half2)], next_sem)
    next_load.start()
    loads[5].wait()
    head_b[rep, 0:classes, :] = fh[...].astype(BF)
    head_b[rep, classes:, :] = jnp.zeros((wide - classes, head_cols), BF)
    loads[4].wait()

    def cols(block, half):
        return pl.ds(pl.multiple_of(block * half, 128), half)

    h1_ref[...] = nn(x_ref[0:rows, cols(rep, half1)], w1b[rep])
    x_total = Total(place, Clock(), x_pair, x_chip, x_sem, x_sum)
    x_sums = nn(jnp.ones((8, rows), BF), x_ref[0:rows, :])
    x_total.start(jnp.concatenate([x_sums[0:1, k * mid : (k + 1) * mid] for k in range(parts)], axis=0))
    for piece in range(g1.pieces):
        g1.hop_y(piece)
        if piece == g1.pieces - 2:
            second(starts=[0])
    for piece in range(g1.pieces):
        g1.hop_core(piece)
        if piece % 2 == 0:
            second(starts=[1 + piece // 2])
    second(over_y=[0])
    for piece in range(g1.pieces):
        g1.finish(piece)
    second(starts=[3], over_y=[1])
    for block in g1.blocks():
        h1_ref[...] += nn(x_ref[0:rows, cols(block, half1)], w1b[block])
    second(starts=[4], over_y=[2])

    def during_first():
        second(starts=[5], over_y=[3], over_core=[0])
        gh.start(0)

    sums = sums_of(h1_ref, images)
    total = sum_over_all(
        place, jnp.concatenate([sums, sums[0:1]], axis=0), pair_buf.at[0], chip_buf.at[0], sum_sem.at[0], during_first
    )
    mean1, inv1 = norm_of(total, count)
    scale1 = norm_ref[0, 0:1] * inv1
    move1 = norm_ref[0, 1:2] - mean1 * scale1
    second(over_y=[4], over_core=[1, 2])

    def act1(pixel, row, carry):
        v = h1_ref[pl.ds(row, images), :] * scale1 + move1
        act = v * sigmoid(v)
        put_padded(pad, pixel, act.astype(BF), images)
        return carry + act

    act_sums = over_pixels(act1, zero, images)
    x_total.advance()
    second(over_y=[5], over_core=[3])
    build_patches(pad, patches)
    second(over_core=[4])

    def rest_of_weights():
        second(over_core=[5])
        for piece in range(g2.pieces):
            g2.finish(piece)

    if half2 % 128:
        rest_of_weights()
        for block in range(n_rep):
            part = nn(patches[0:rows, block * half2 : (block + 1) * half2], w2b[block])
            h2_ref[...] = part if block == 0 else h2_ref[...] + part
    else:
        h2_ref[...] = nn(patches[0:rows, cols(rep, half2)], w2b[rep])
        rest_of_weights()
        for block in g2.blocks():
            h2_ref[...] += nn(patches[0:rows, cols(block, half2)], w2b[block])

    sums = jnp.concatenate([sums_of(h2_ref, images), fold(act_sums)], axis=0)
    gh.hop_y(0)
    total = sum_over_all(place, sums, pair_buf.at[1], chip_buf.at[1], sum_sem.at[1], lambda: gh.hop_core(0))
    act_mean = total[2:3] / count
    mean2, inv2 = norm_of(total, count)
    scale2 = norm_ref[1, 0:1] * inv2
    move2 = norm_ref[1, 1:2] - mean2 * scale2

    def pool(pixel, row, carry):
        v = h2_ref[pl.ds(row, images), :] * scale2 + move2
        return carry + v * sigmoid(v)

    factor[:, wide:] = (over_pixels(pool, zero, images) / (SIDE * SIDE)).astype(BF)
    gh.finish(0)
    logits = bias_pad[...]
    for block in range(n_rep):
        logits = logits + nt(factor[:, wide + block * head_cols : wide + (block + 1) * head_cols], head_b[block])
    column = lax.broadcasted_iota(jnp.int32, (images, wide), 1)
    shown = jnp.where(column < classes, logits, -jnp.inf)
    top = jnp.max(shown, axis=1, keepdims=True)
    lse = top + jnp.log(jnp.sum(jnp.exp(shown - top), axis=1, keepdims=True))
    image = lax.broadcasted_iota(jnp.int32, (images, wide), 0)
    label = jnp.zeros((images, wide), jnp.int32)
    for k in range(images):
        label = jnp.where(image == k, label_ref[k], label)
    hit = (column == label).astype(F32)
    target = jnp.sum(logits * hit, axis=1, keepdims=True)
    loss = jnp.sum(lse - target, axis=0, keepdims=True)
    grad = (jnp.exp(shown - lse) - hit) / all_images
    dz = grad.astype(BF)
    factor[:, 0:wide] = dz
    for block in range(n_rep):
        dpool_ref[:, block * head_cols : (block + 1) * head_cols] = nn(dz, head_b[block]) / (SIDE * SIDE)
    dpool = dpool_ref[...]

    def back2(row):
        h = h2_ref[pl.ds(row, images), :]
        v = h * scale2 + move2
        sig = sigmoid(v)
        return dpool * sig * (1.0 + v * (1.0 - sig)), (h - mean2) * inv2

    def back2_sums(pixel, row, carry):
        dy, unit_h = back2(row)
        return carry[0] + dy, carry[1] + dy * unit_h

    one, two = over_pixels(back2_sums, (zero, zero), images)
    sums = jnp.concatenate([fold(one), fold(two), fold(one)], axis=0)
    factors = Factors(place, clock, factors_ref, factor_sem)
    head_total = Total(place, clock, head_pair, head_chip, total_sem, head_ref)
    active = [factors, head_total]

    def during_third():
        factors.start(factor)
        bias_sums = jnp.sum(grad, axis=0, keepdims=True)
        pieces = [bias_sums[:, k * mid : (k + 1) * mid] for k in range(wide // mid)]
        head_total.start(jnp.concatenate([*pieces, jnp.broadcast_to(loss, (1, mid))], axis=0))
        x_total.advance()
        for k in range(parts):
            at = slice(k * mid, (k + 1) * mid)
            x_ref[extra, at] = jnp.where(two_rows, x_sum[k : k + 1, :] / count, 0.0).astype(BF)
        for k in range(9):
            dy, dx = divmod(k, 3)
            inside = (1.0 if dy == 1 else 6 / 7) * (1.0 if dx == 1 else 6 / 7)
            patches[extra, k * mid : (k + 1) * mid] = jnp.where(two_rows, act_mean * inside, 0.0).astype(BF)

    extra = slice(rows, rows + 16)
    first_row = lax.broadcasted_iota(jnp.int32, (16, mid), 0) < 1
    two_rows = lax.broadcasted_iota(jnp.int32, (16, mid), 0) < 2
    total = sum_over_all(place, sums, pair_buf.at[2], chip_buf.at[2], sum_sem.at[2], during_third)
    clock.work(3.5)
    shift2, gain2 = total[0:1] / count, total[1:2] / count
    for gather in (g1, g2, gh):
        gather.drain()

    s_totals = [Total(place, clock, s_pair.at[k], s_chip.at[k], s_sem.at[k], s_total.at[k]) for k in range(2)]

    def offset(acc, totals):
        share = fold(acc).astype(BF)
        dh[extra, :] = jnp.where(first_row, -share.astype(F32), 0.0).astype(BF)
        totals.start(share.astype(F32))
        active.append(totals)

    fulls, sums_refs, weight_refs = [g2_ref, g1_ref], [f2, f1], [w2b, w1b]
    pieces = [
        Piece(plan, place, clock, fulls[plan["conv"]], sums_refs[plan["conv"]], weight_refs[plan["conv"]], refs)
        for plan in plans
    ]
    slots = [h2_ref, h1_ref]
    mom_loads = []
    for k, plan in enumerate(plans):
        src = (mom2_hbm, mom1_hbm)[plan["conv"]].at[pl.ds(plan["part"] * plan["size"], plan["size"])]
        mom_loads.append(pltpu.make_async_copy(src, slots[k % 2].at[pl.ds(0, plan["size"])], mom_sem.at[k]))
    cross = da1.at[pl.ds(0, mid)]
    grams = [Gram(place, clock, g, cross, packed.at[k], gram_total.at[k], gram_sem.at[k]) for k, g in enumerate((gram2, gram1))]
    waiting, added, turns = [], [], []

    def gradient(piece, source):
        plan = piece.plan
        part = plan["size"] // 2
        for block in range(n_rep):
            for who in range(2):
                first = block * plan["half"] + plan["part"] * plan["size"]
                if plan["fits"]:
                    mine = core if who else 1 - core
                    value = tn(source[:, pl.ds(pl.multiple_of(first + mine * part, 128), part)], dh[...])
                    if who:
                        piece.acc[piece.part(block, 0, part), :] = value
                    else:
                        piece.outgoing[0][block] = value.astype(BF)
                else:
                    value = tn(source[:, first + who * part : first + who * part + part], dh[...])

                    @pl.when(core == who)
                    def keep(block=block, value=value):
                        piece.acc[piece.part(block, 0, part), :] = value

                    @pl.when(core != who)
                    def give(block=block, value=value):
                        piece.outgoing[0][block] = value.astype(BF)

                clock.work(part * 0.00135)
            if block == n_rep - 1:
                piece.start()
        active.append(piece)

    def finished(piece):
        index = pieces.index(piece)
        size, part, conv = piece.plan["size"], piece.plan["part"], piece.plan["conv"]
        mom_loads[index].wait()
        if part == 0:
            total, to = s_totals[conv], (s2_ref, s1_ref)[conv]
            while total in active:
                do(total)
            high, low = halves_of(s_total[conv])
            first = jnp.where(first_row, high.astype(F32), 0.0)
            to[...] = jnp.where(two_rows, jnp.where(first_row, first, low.astype(F32)), 0.0).astype(BF)
        rows_at = slice(part * size, part * size + size)
        back = tn((m2_ref, m1_ref)[conv][:, rows_at], (s2_ref, s1_ref)[conv][...])
        value = 0.5 * slots[index % 2][0:size, :] + (fulls[conv][rows_at, :].astype(F32) + back)
        sums_refs[conv][rows_at, :] = value
        grams[conv].add(value)
        clock.work(size * 0.0015)
        if index + 2 < len(pieces):
            mom_loads[index + 2].start()
        if not [p for p in pieces[index + 1 :] if p.plan["conv"] == conv]:
            grams[conv].start()
            active.append(grams[conv])

    def do(item):
        if item.advance():
            return
        active.remove(item)
        if isinstance(item, (Factors, Total)):
            return
        if isinstance(item, Piece):
            waiting.append(item)
            while len(added) < len(pieces) and pieces[len(added)] in waiting:
                added.append(pieces[len(added)])
                finished(added[-1])
        else:
            turns.extend((item, turn) for turn in range(TURNS))

    def serve(margin=0.0, patient=True):
        while True:
            due = [k for k in active if k.ready + margin <= clock.now and not (patient and k is factors)]
            if not due:
                return
            do(min(due, key=lambda k: k.ready))

    def work_turn():
        item, turn = turns.pop(0)
        index = grams.index(item)
        out = (q2_ref, q1_ref)[index]

        @pl.when(core == index)
        def here():
            newton_turn(turn, item.g, out)
            if turn == TURNS - 1:
                out[...] = out[...] / item.scale
                send(out, out, q_sem.at[index, 0], q_sem.at[index, 1], place.flip(0))

        clock.work(2.8 if active else 0.0)

    def finish2(pixel, row, carry):
        dy, unit_h = back2(row)
        put = (scale2 * (dy - shift2 - unit_h * gain2)).astype(BF)
        put_padded(dpad, pixel, put, images)
        dh[pl.ds(row, images), :] = put
        return carry + put.astype(F32)

    offset(over_pixels(finish2, zero, images), s_totals[0])
    clock.work(1.3)
    mom_loads[0].start()
    for source, to, half in ((patches, m2_ref, half2), (x_ref, m1_ref, half1)):
        for block in range(n_rep):

            @pl.when(rep == block)
            def own(source=source, to=to, half=half, block=block):
                to[...] = source[extra, block * half : (block + 1) * half]

    begun = [p for p in pieces if p.plan["early"]]
    for piece in begun:
        gradient(piece, patches)
    for k in range(9):
        dy, dx = divmod(k, 3)
        lhs = dpad[2 - dy : 2 - dy + SIDE, (2 - dx) * images : (2 - dx) * images + line, :].reshape(rows, mid)
        first = k * mid
        weights = w2b[first // half2, first % half2 : first % half2 + mid, :] if half2 % mid == 0 else None
        if weights is None:
            ends = sorted({first, first + mid, *(b * half2 for b in range(n_rep) if first < b * half2 < first + mid)})
            weights = [w2b[a // half2, a % half2 : a % half2 + b - a, :] for a, b in zip(ends, ends[1:])]
            weights = weights[0] if len(weights) == 1 else jnp.concatenate(weights, axis=0)
        part = nt(lhs, weights)
        da1[...] = part if k == 0 else da1[...] + part
        clock.work(0.5)
        if k % 3 == 2:
            serve(2.0, False)

    def back1(pixel, row, carry):
        h = h1_ref[pl.ds(row, images), :]
        v = h * scale1 + move1
        sig = sigmoid(v)
        dy = da1[pl.ds(row, images), :] * sig * (1.0 + v * (1.0 - sig))
        da1[pl.ds(row, images), :] = dy
        return carry[0] + dy, carry[1] + dy * ((h - mean1) * inv1)

    one, two = over_pixels(back1, (zero, zero), images)
    clock.work(1.1)
    of_second = [p for p in pieces if p.plan["conv"] == 0 and p not in begun]
    ahead = of_second[:1]

    def during_fourth():
        clock.work(1.5)
        entered = clock.now
        for piece in ahead:
            gradient(piece, patches)
            serve(2.5)
        clock.now = max(clock.now, entered + 4.0)

    sums = jnp.concatenate([fold(one), fold(two), fold(one)], axis=0)
    total = sum_over_all(place, sums, pair_buf.at[3], chip_buf.at[3], sum_sem.at[3], during_fourth)
    stat_ref[...] = jnp.concatenate([total[0:2], shift2 * count, gain2 * count], axis=0)
    shift1, gain1 = total[0:1] / count, total[1:2] / count
    serve()
    for piece in of_second[1:]:
        gradient(piece, patches)
        serve()

    def finish1(pixel, row, carry):
        h = h1_ref[pl.ds(row, images), :]
        dy = da1[pl.ds(row, images), :]
        put = (scale1 * (dy - shift1 - (h - mean1) * inv1 * gain1)).astype(BF)
        dh[pl.ds(row, images), :] = put
        return carry + put.astype(F32)

    offset(over_pixels(finish1, zero, images), s_totals[1])
    clock.work(0.8)
    mom_loads[1].start()
    serve()
    for piece in pieces:
        if piece.plan["conv"] == 1:
            gradient(piece, x_ref)
            serve()

    while active or turns:
        due = min(active, key=lambda k: k.ready + (3.0 if k is factors else 0.0)) if active else None
        if due is not None and (not turns or due.ready <= clock.now + 2.0):
            if not isinstance(due, (Piece, Factors, Gram)):
                clock.now = max(clock.now, due.ready)
            do(due)
        else:
            work_turn()
    for index, out in enumerate((q2_ref, q1_ref)):

        @pl.when(core == index)
        def sent(index=index, out=out):
            wait_bytes(out, q_sem.at[index, 0])

        @pl.when(core != index)
        def came(index=index, out=out):
            wait_bytes(out, q_sem.at[index, 1])

    next_load.wait()
    for item in [x_total, head_total, *s_totals]:
        item.drain()


def room(n_rep, half1, half2, mid):
    carried = n_rep * (half1 + half2) // 2 * mid + half2 * mid + 2 * mid * mid
    return 63 * 2**20 - 4 * carried


def run_step(n_dp, n_rep, x, conv1, conv2, head, live1, live2, mom1, mom2, next2, bias, norm, labels):
    rows, mid = x.shape[0], conv1.shape[1]
    images = rows // (SIDE * SIDE)
    half1, half2 = conv1.shape[0], conv2.shape[0]
    classes, head_cols = head.shape
    wide = (classes + mid - 1) // mid * mid
    devices, chips, parts = n_dp * n_rep, n_dp // 2 * n_rep, x.shape[1] // mid
    head_rows, block = wide // mid + 1, mid // 4
    shape = jax.ShapeDtypeStruct
    vmem, hbm = pl.BlockSpec(memory_space=pltpu.VMEM), pl.BlockSpec(memory_space=pl.ANY)
    more = []
    plans = plan_pieces(n_dp, n_rep, [(half2, 3, ("rep", "rep", "rep"), ("late",) * 3), (half1, 2, ("rep", "rep"), ("late",) * 2)], mid, more)
    pad = ((SIDE + 2), (SIDE + 2) * images, mid)
    levels = n_rep.bit_length()
    weight_pieces = next(k for k in (6, 3, 1) if half2 // 4 % (16 * k) == 0)
    scratch = [
        pltpu.VMEM((half1, mid), BF), pltpu.VMEM((half2, mid), BF),
        pltpu.VMEM((16, half1), BF), pltpu.VMEM((16, half2), BF), pltpu.VMEM((16, mid), BF), pltpu.VMEM((16, mid), BF),
        pltpu.VMEM((rows + 16, x.shape[1]), BF), pltpu.VMEM((rows + 16, 9 * mid), BF),
        pltpu.VMEM((rows, mid), F32), pltpu.VMEM((rows, mid), F32), pltpu.VMEM((rows, mid), F32),
        pltpu.VMEM(pad, BF), pltpu.VMEM(pad, BF), pltpu.VMEM((rows + 16, mid), BF),
        pltpu.VMEM((n_rep, half1, mid), BF), pltpu.VMEM((n_rep, half2, mid), BF), pltpu.VMEM((n_rep, wide, head_cols), BF),
        pltpu.VMEM((classes, head_cols), F32), pltpu.VMEM((1, wide), F32),
        pltpu.VMEM((images, wide + mid), BF),
        pltpu.VMEM((mid, mid), F32), pltpu.VMEM((mid, mid), F32),
        pltpu.VMEM((2, levels, block, 5 * block), F32), pltpu.VMEM((2, 2, block, 5 * block), F32),
        pltpu.VMEM((parts, mid), F32), pltpu.VMEM((2, 1, mid), F32), pltpu.VMEM((images, mid), F32),
        pltpu.VMEM((4, 2, 3, mid), F32), pltpu.VMEM((4, chips, 3, mid), F32),
        pltpu.VMEM((2, parts, mid), F32), pltpu.VMEM((chips, parts, mid), F32),
        pltpu.VMEM((2, 2, 1, mid), F32), pltpu.VMEM((2, chips, 1, mid), F32),
        pltpu.VMEM((2, head_rows, mid), F32), pltpu.VMEM((chips, head_rows, mid), F32),
        DMA((7,)), DMA((4, 4, 2)), DMA((4, weight_pieces, 2)), DMA((4, 1, 2)), DMA((4, 4)), DMA((4,)), DMA((len(plans),)),
        DMA((2, levels, 2)), DMA((2, 4)), DMA((4,)), DMA((devices.bit_length(), max(1, devices // 8), 2)), DMA((2, 2)), DMA,
    ]
    return pl.pallas_call(
        functools.partial(kernel_step, n_dp, n_rep, plans),
        out_shape=(
            pltpu.VMEM((n_rep * half1 // 2, mid), F32), pltpu.VMEM((n_rep * half2 // 2, mid), F32),
            pltpu.VMEM((half2, mid), jnp.int32), pltpu.VMEM((mid, mid), F32), pltpu.VMEM((mid, mid), F32),
            shape((4, mid), F32), shape((head_rows, mid), F32), shape((devices, images, wide + mid), BF),
        ),
        in_specs=[hbm] * 9 + [vmem] * 2 + [pl.BlockSpec(memory_space=pltpu.SMEM)],
        out_specs=[vmem] * 7 + [hbm],
        scratch_shapes=scratch + more,
        compiler_params=pltpu.CompilerParams(
            collective_id=1, has_side_effects=True, vmem_limit_bytes=room(n_rep, half1, half2, mid)
        ),
        name="gradients",
    )(x, conv1, conv2, head, live1, live2, mom1, mom2, next2, bias, norm, labels)


def adam_update(weight, first, second, grad, rate):
    first = 0.9 * first + 0.1 * grad
    second = 0.999 * second + 0.001 * grad * grad
    mhat = first / (1.0 - 0.9**STEP)
    vhat = second / (1.0 - 0.999**STEP)
    return (weight - rate * (mhat / (jnp.sqrt(vhat) + 1e-08) + 0.01 * weight), first, second)


def kernel_update(n_rep, sizes, *refs):
    (x2, x1, mask2, q2, q1, weight2, weight1, mask1_hbm,
     sums, head_sums, bias, bias_m, bias_v, norm, norm_m, norm_v, factors_hbm, head_hbm, first_hbm, second_hbm,
     new2, mom2_out, new1, mom1_out, loss_out, bias_out, bias_m_out, bias_v_out, norm_out, norm_m_out, norm_a_out, norm_b_out,
     head_out, first_out, second_out,
     split, weight_buf, mask1, factors, state, share,
     tile_sem, store_sem, in_sem, out_sem) = refs
    classes, part = state.shape[1], state.shape[2]
    mid = sums.shape[1]
    images = factors.shape[0] * factors.shape[1]
    wide = factors.shape[2] - mid
    tiles, at = [], 0
    for k, (size, weight, new) in enumerate(zip(sizes, (weight2, weight1), (new2, new1))):
        for first in range(0, weight.shape[0], size):
            buf, sems = weight_buf.at[pl.ds(at, size)], tile_sem.at[len(tiles)]
            load = pltpu.make_async_copy(weight.at[pl.ds(first, size)], buf, sems.at[0])
            store = pltpu.make_async_copy(buf, new.at[pl.ds(first, size)], sems.at[1])
            tiles.append((k, first, size, at, load, store))
            at += size
    moms = [
        pltpu.make_async_copy(src.at[pl.ds(0, dst.shape[0])], dst, store_sem.at[k])
        for k, (src, dst) in enumerate(((x2, mom2_out), (x1, mom1_out)))
    ]
    mask_load = pltpu.make_async_copy(mask1_hbm, mask1, in_sem.at[4])
    heads = [pltpu.make_async_copy(factors_hbm, factors, in_sem.at[3])]
    heads += [pltpu.make_async_copy(s, state.at[k], in_sem.at[k]) for k, s in enumerate((head_hbm, first_hbm, second_hbm))]
    head_stores = [
        pltpu.make_async_copy(state.at[k], dst, out_sem.at[k]) for k, dst in enumerate((head_out, first_out, second_out))
    ]
    for k, tile in enumerate(tiles):
        tile[4].start()
        if k == 0:
            moms[0].start()
    mask_load.start()
    for load in heads:
        load.start()
    moms[1].start()
    for k, q in enumerate((q2, q1)):
        split[2 * k], split[2 * k + 1] = halves_of(q[...])

    def head():
        for load in heads:
            load.wait()
        every = factors[...].reshape(images, wide + mid)
        rep = lax.axis_index("rep")
        for block in range(n_rep):

            @pl.when(rep == block)
            def own(block=block):
                share[...] = every[:, wide + block * part : wide + (block + 1) * part]

        grad = tn(every[:, 0:wide], share[...])[0:classes]
        state[0], state[1], state[2] = adam_update(state[0], state[1], state[2], grad, 0.03)
        for store in head_stores:
            store.start()
        loss_out[...] = head_sums[wide // mid :, 0:1]
        for k in range(wide // mid):
            at = (slice(None), slice(k * mid, min((k + 1) * mid, classes)))
            grad = head_sums[k : k + 1, 0 : min(mid, classes - k * mid)]
            bias_out[at], bias_m_out[at], bias_v_out[at] = adam_update(bias[at], bias_m[at], bias_v[at], grad, 0.2)
        for k, out in enumerate((norm_a_out, norm_b_out)):
            for j in range(2):
                at, grad = (k, slice(j, j + 1)), sums[2 * k + 1 - j : 2 * k + 2 - j]
                norm_out[at], norm_m_out[at], out[j : j + 1, :] = adam_update(norm[at], norm_m[at], norm_v[at], grad, 0.2)

    waited = False
    for k, first, size, at, load, store in tiles:
        load.wait()
        if k and not waited:
            head()
            mask_load.wait()
            waited = True
        here, there = slice(at, at + size), slice(first, first + size)
        ortho = mm(halves_of((x2, x1)[k][there, :]), (split[2 * k], split[2 * k + 1]))
        weight_buf[here, :] = (weight_buf[here, :] - 1.0 * ortho) * (mask2, mask1)[k][there, :].astype(F32)
        store.start()
    for tile in tiles:
        tile[5].wait()
    for store in moms + head_stores:
        store.wait()


def run_update(n_rep, carried, weights, mask1, sums, head_sums, smalls, factors, heads):
    mid = sums.shape[1]
    shape = jax.ShapeDtypeStruct
    vmem = pl.BlockSpec(memory_space=pltpu.VMEM)
    hbm = pl.BlockSpec(memory_space=pl.ANY)
    halves = [w.shape[0] for w in weights]
    sizes = [next((k for k in (384, 256, 128) if half % k == 0), half) for half in halves]
    tiles, rows = sum(half // size for half, size in zip(halves, sizes)), sum(halves)
    bias, norm = smalls[0], smalls[3]
    classes, part = heads[0].shape
    outs = [weights[0].shape] * 2 + [weights[1].shape] * 2
    outs += [(1, 1)] + [bias.shape] * 3 + [norm.shape] * 2 + [norm.shape[1:]] * 2 + [heads[0].shape] * 3
    carried = [pltpu.with_memory_space_constraint(c, pltpu.VMEM) for c in carried]
    return pl.pallas_call(
        functools.partial(kernel_update, n_rep, sizes),
        out_shape=tuple(shape(s, F32) for s in outs),
        in_specs=[vmem] * 5 + [hbm] * 3 + [vmem] * 8 + [hbm] * 4,
        out_specs=[hbm] * 4 + [vmem] * 8 + [hbm] * 3,
        scratch_shapes=[
            pltpu.VMEM((4, mid, mid), BF), pltpu.VMEM((rows, mid), F32), pltpu.VMEM(mask1.shape, jnp.int32),
            pltpu.VMEM(factors.shape, BF), pltpu.VMEM((3, classes, part), F32),
            pltpu.VMEM((factors.shape[0] * factors.shape[1], part), BF),
            DMA((tiles, 2)), DMA((2,)), DMA((5,)), DMA((3,)),
        ],
        compiler_params=pltpu.CompilerParams(vmem_limit_bytes=room(n_rep, halves[1], halves[0], mid)),
        name="update",
    )(*carried, *weights, mask1, sums, head_sums, *smalls, factors, *heads)


def local(
    images,
    labels,
    conv1,
    conv2,
    classifier,
    class_bias,
    batchnorm_parameters,
    conv1_mom,
    conv2_mom,
    class_m,
    class_v,
    bias_m,
    bias_v,
    norm_m,
    norm_v,
    conv1_live,
    conv2_live,
    conv1_next,
    conv2_next,
):
    count, c_in = images.shape[0], images.shape[3]
    n_dp, n_rep = lax.axis_size("dp"), lax.axis_size("rep")
    x = images.transpose(1, 2, 0, 3).reshape(SIDE * SIDE * count, c_in)
    bias = class_bias.reshape(1, -1)
    mom1, mom2, next2, q_one, q_two, sums, head_sums, factors = run_step(
        n_dp, n_rep, x, conv1, conv2, classifier.T, conv1_live, conv2_live, conv1_mom, conv2_mom, conv2_next,
        bias, batchnorm_parameters, labels,
    )
    (conv2_new, mom_two, conv1_new, mom_one, loss, bias_new, first_b, second_b, norm_new, first_n, norm_a, norm_b,
     head_new, head_m, head_v) = run_update(
        n_rep,
        (mom2, mom1, next2, q_two, q_one),
        (conv2, conv1),
        conv1_next,
        sums,
        head_sums,
        (bias, bias_m.reshape(1, -1), bias_v.reshape(1, -1), batchnorm_parameters, norm_m, norm_v),
        factors,
        (classifier.T, class_m.T, class_v.T),
    )
    return (
        loss[0, 0],
        conv1_new,
        conv2_new,
        head_new.T,
        bias_new[0],
        norm_new,
        mom_one,
        mom_two,
        head_m.T,
        head_v.T,
        first_b[0],
        second_b[0],
        first_n,
        norm_a,
        norm_b,
    )


def solution(mesh):
    placed = (
        P(("dp", "rep"), None, None, None),
        P(("dp", "rep")),
        P("rep", None),
        P("rep", None),
        P("rep", None),
        P(),
        P(),
        P("rep", None),
        P("rep", None),
        P("rep", None),
        P("rep", None),
        P(),
        P(),
        P(),
        P(),
        P("rep", None),
        P("rep", None),
        P("rep", None),
        P("rep", None),
    )
    return jax.shard_map(
        local,
        mesh=mesh,
        in_specs=placed,
        out_specs=(
            P(),
            P("rep", None),
            P("rep", None),
            P("rep", None),
            P(),
            P(),
            P("rep", None),
            P("rep", None),
            P("rep", None),
            P("rep", None),
            P(),
            P(),
            P(),
            P(),
            P(),
        ),
        check_vma=False,
    )
```
